256 devices in a mesh: batch: 16 (over z, x_lo), member: 16 (over x_hi, y, core).
Axes of the slice: x: 4 (x_hi: 2, x_lo: 2; x = x_hi * 2 + x_lo), y: 4, z: 8, core: 2. Of those that a mesh axis runs over, the one named last changes fastest.
Arguments:
- contexts: bfloat16 [768, 8192], P('batch'), may hold values from -6 to 6
- trunk_weight: bfloat16 [8192, 8192], P('batch', 'member'), may hold values from -0.0625 to 0.0625
- trunk_bias: float32 [8192], P('member'), may hold values from -3 to 3
- head_weight: bfloat16 [16, 8192, 4096], P('member', None, 'batch'), may hold values from -0.0625 to 0.0625
- head_bias: float32 [16, 4096], P('member', 'batch'), may hold values from -3 to 3
- arm_embed: bfloat16 [2048, 4096], P(None, 'batch'), may hold values from -0.09375 to 0.09375
- slots: int32 [768, 8], replicated, may hold values from 0 to 2047, as said below
- feedback: float32 [768, 8], replicated, may hold values from 0 to 1
- boot_weight: int32 [16, 768], P('member'), may hold values from 0 to 3
Outputs:
- scores: bfloat16 [16, 768, 2048], P('member', 'batch')
- weight_grad: bfloat16 [16, 8192, 4096], P('member', None, 'batch')
- bias_grad: float32 [16, 4096], P('member', 'batch')
The draws below stay inside these ranges and needn't reach their ends.
Inputs may be any that keep to these rules, and one draw needn't show every extreme that they name: `slots`: each row names 8 different arms.
All inputs are finite; a program needn't handle non-finite values.
Results may differ from the reference program's by a relative error of at most 0.04.
The reference program's roundings to bfloat16 on the way (of `features`, `hidden` and `pre_grad`) count: a program that leaves them out, or rounds other values in their place, can miss the bound.
Values may be sent and summed in bfloat16 or wider, within the bound.
No kernel may reach another device: no remote copies, remote signals or barrier semaphores. Data moves between devices by JAX's collectives and lax.ppermute only.
A program may use at most 128 MiB of HBM per device.

```python
import jax
import jax.numpy as jnp
from jax import lax

DIN = 8192
D = 8192
H = 4096
ARMS = 2048
SLOTS = 8
CTX = 768
MEMBERS = 16


def draw_slots(key, part):
    row_ids = jnp.arange(CTX, dtype=jnp.int32)[:, None]
    col_ids = jnp.arange(ARMS, dtype=jnp.int32)[None, :]
    rank_keys = jax.random.randint(key, (CTX, ARMS), 0, 2 ** 19, dtype=jnp.int32) * ARMS + col_ids
    forced = (row_ids == 0) & ((col_ids == 0) | (col_ids == ARMS - 1))
    rank_keys = jnp.where(forced, 2 ** 30 + col_ids, rank_keys)
    return lax.top_k(rank_keys, SLOTS)[1].astype(jnp.int32)


def set_ends(result, rng, low, largest):
    extent = result.shape
    place = [jax.random.randint(jax.random.fold_in(rng, axis), (), 0, extent[axis]) for axis in range(len(extent))]
    result = result.at[tuple(place)].set(low)
    longest = extent.index(max(extent))
    place[longest] = (place[longest] + 1) % extent[longest]
    return result.at[tuple(place)].set(largest)


def level_of(own_key, extent, shards, least, high):
    def one(dim, parts):
        heights = jax.random.uniform(jax.random.fold_in(jax.random.fold_in(own_key, 6), dim), (parts,), jnp.float32, least / len(shards), high / len(shards))
        return jnp.repeat(jnp.exp(heights), extent[dim] // parts).reshape((-1,) + (1,) * (len(extent) - dim - 1))

    gain = one(*shards[0])
    for cut in shards[1:]:
        gain = gain * one(*cut)
    return gain


def normal_values(rng, dims, scale, reach, cuts=(), kind=jnp.bfloat16):
    entries = scale * jax.random.normal(rng, dims, jnp.float32)
    if cuts:
        entries = entries * level_of(rng, dims, cuts, -0.22, 0.18)
    return jnp.clip(entries, -reach, reach).astype(kind)


def setup_inputs(seed: int = 0) -> dict:
    splits = jax.random.split(jax.random.key(seed), 10)
    return {
        "contexts": normal_values(splits[0], (CTX, DIN), 1.0, 6.0, ((0, 16),)),
        "trunk_weight": normal_values(splits[1], (DIN, D), DIN ** -0.5, 0.0625, ((0, 16), (1, 16))),
        "trunk_bias": normal_values(splits[2], (D,), 0.5, 3.0, ((0, 16),), jnp.float32),
        "head_weight": normal_values(splits[3], (MEMBERS, D, H), D ** -0.5, 0.0625, ((0, 16), (2, 16))),
        "head_bias": normal_values(splits[4], (MEMBERS, H), 0.5, 3.0, ((0, 16), (1, 16)), jnp.float32),
        "arm_embed": normal_values(splits[5], (ARMS, H), H ** -0.5, 0.09375, ((1, 16),)),
        "slots": draw_slots(jax.random.fold_in(splits[9], 71), 0),
        "feedback": jnp.clip(jax.random.uniform(splits[7], (CTX, SLOTS), jnp.float32, 0.0, 1.0), 0.0, 1.0),
        "boot_weight": set_ends(jax.random.randint(splits[8], (MEMBERS, CTX), 0, 4), jax.random.fold_in(splits[8], 1), 0, 3).astype(jnp.int32),
    }


def reference(contexts, trunk_weight, trunk_bias, head_weight, head_bias, arm_embed, slots, feedback, boot_weight):
    features = jax.nn.relu(jnp.dot(contexts, trunk_weight, preferred_element_type=jnp.float32) + trunk_bias).astype(jnp.bfloat16)
    shown_embed = jnp.take(arm_embed, slots, axis=0).astype(jnp.float32)

    def member_step(inputs):
        weights, biases, boot_row = inputs
        pre_act = jnp.dot(features, weights, preferred_element_type=jnp.float32) + biases
        hidden = jax.nn.relu(pre_act).astype(jnp.bfloat16)
        full_scores = jnp.dot(hidden, arm_embed.T, preferred_element_type=jnp.float32)
        slot_scores = jnp.take_along_axis(full_scores, slots, axis=1)
        slot_grad = boot_row.astype(jnp.float32)[:, None] * (jax.nn.sigmoid(slot_scores) - feedback) / jnp.float32(SLOTS)
        hidden_grad = jnp.sum(slot_grad[:, :, None] * shown_embed, axis=1)
        pre_grad = jnp.where(pre_act > 0, hidden_grad, jnp.float32(0.0)).astype(jnp.bfloat16)
        weight_grad = jnp.dot(features.T, pre_grad, preferred_element_type=jnp.float32).astype(jnp.bfloat16)
        bias_grad = jnp.sum(pre_grad.astype(jnp.float32), axis=0)
        return full_scores.astype(jnp.bfloat16), weight_grad, bias_grad

    scores, weight_grad, bias_grad = lax.map(member_step, (head_weight, head_bias, boot_weight))
    return (scores, weight_grad, bias_grad)
```

```python
import jax
import jax.numpy as jnp
from jax import lax
from jax.experimental import pallas as pl
from jax.experimental.pallas import tpu as pltpu
from jax.sharding import Mesh
from jax.sharding import PartitionSpec as P

AXES = ("z", "xl", "xh", "y", "c")
NZ, NX, NY = 8, 4, 4
BF, F32 = jnp.bfloat16, jnp.float32
STEPS = (0, -1, 1, 2)
SLOT_Z = (0, -1, -2, -3, 4, 1, 2, 3)


def flat(z, x, y, c):
    z, x, y = z % NZ, x % NX, y % NY
    return (((z * 2 + x % 2) * 2 + x // 2) * NY + y) * 2 + c


def route(value, where):
    pairs = []
    for z in range(NZ):
        for x in range(NX):
            for y in range(NY):
                for c in range(2):
                    to = where(z, x, y, c)
                    if to is not None:
                        pairs.append((flat(z, x, y, c), flat(*to)))
    return lax.ppermute(value, AXES, pairs)


def other_core(value):
    return route(value, lambda z, x, y, c: (z, x, y, 1 - c))


def x_partner(value):
    return route(value, lambda z, x, y, c: (z, x ^ 1, y, c))


def out_z(value, i):
    if i == 4:
        return route(value, lambda z, x, y, c: (z - 4, x, y, c) if c else None)
    return route(value, lambda z, x, y, c: (z + (i if c == 0 else -i), x, y, c))


def back_z(value, i):
    if i == 4:
        return route(value, lambda z, x, y, c: (z + 4, x, y, c) if c else None)
    return route(value, lambda z, x, y, c: (z + (-i if c == 0 else i), x, y, c))


def first_ring(value, d):
    return route(value, lambda z, x, y, c: (z, x, y + d, c) if c == 0 else (z, x + d, y, c))


def last_ring(value, d):
    return route(value, lambda z, x, y, c: (z, x + d, y, c) if c == 0 else (z, x, y + d, c))


def gather_kernel(ids_ref, arm_ref, out_ref):
    rows = out_ref.shape[0]
    arms = arm_ref.shape[0]
    hot = ids_ref[...] == lax.broadcasted_iota(jnp.int32, (rows, arms), 1)
    out_ref[...] = jnp.dot(
        jnp.where(hot, F32(1.0), F32(0.0)).astype(BF), arm_ref[...], preferred_element_type=F32
    ).astype(BF)


def gather_rows(ids, arm):
    n, (arms, h) = ids.shape[0], arm.shape
    rows = 512
    return pl.pallas_call(
        gather_kernel,
        grid=(n // rows,),
        in_specs=[
            pl.BlockSpec((rows, 1), lambda i: (i, 0)),
            pl.BlockSpec((arms, h), lambda i: (0, 0)),
        ],
        out_specs=pl.BlockSpec((rows, h), lambda i: (i, 0)),
        out_shape=jax.ShapeDtypeStruct((n, h), BF),
        compiler_params=pltpu.CompilerParams(vmem_limit_bytes=40 * 2**20),
        cost_estimate=pl.CostEstimate(
            flops=2 * n * arms * h, bytes_accessed=n * h * 2 + arms * h * 2, transcendentals=0
        ),
        name="gather_rows",
    )(ids, arm)


def piece_copies(tbl, pieces, feats, sems):
    t = 0
    out = []
    for ref in pieces:
        for k in range(ref.shape[0]):
            cb, rg = tbl[2 * t], tbl[2 * t + 1]
            rows = ref.shape[1]
            out.append(
                pltpu.make_async_copy(
                    ref.at[k],
                    feats.at[cb, pl.ds(pl.multiple_of(rg * rows, 16), rows), :],
                    sems.at[cb, rg],
                )
            )
            t += 1
    return out


def wait_block(pieces, feats, sems, cb):
    rows = pieces[0].shape[1]
    for rg in range(4):
        pltpu.make_async_copy(
            pieces[0].at[0], feats.at[cb, pl.ds(rg * rows, rows), :], sems.at[cb, rg]
        ).wait()


def act_kernel(tbl, *refs):
    pieces, (w_ref, bias_ref, shown_ref, act_ref, hid_ref, pick_ref, feats, sems) = refs[:14], refs[14:]
    cb = pl.program_id(0)

    @pl.when(cb == 0)
    def _():
        for copy in piece_copies(tbl, pieces, feats, sems):
            copy.start()
        act_ref[...] = jnp.broadcast_to(bias_ref[...], act_ref.shape)

    wait_block(pieces, feats, sems, cb)
    act_ref[...] += jnp.dot(feats[cb], w_ref[0], preferred_element_type=F32)

    @pl.when(cb == pl.num_programs(0) - 1)
    def _():
        hid = jnp.maximum(act_ref[...], F32(0.0)).astype(BF)
        hid_ref[...] = hid
        wide = hid.astype(F32)
        for k in range(8):
            pick_ref[:, k : k + 1] = jnp.sum(
                wide * shown_ref[k].astype(F32), axis=1, keepdims=True
            )


def run_act(tbl, pieces, weight, bias, shown):
    blocks, depth, h = weight.shape
    rows = shown.shape[1]
    grid_spec = pltpu.PrefetchScalarGridSpec(
        num_scalar_prefetch=1,
        grid=(blocks,),
        in_specs=[pl.BlockSpec(memory_space=pl.ANY)] * 14
        + [
            pl.BlockSpec((1, depth, h), lambda i, t: (i, 0, 0)),
            pl.BlockSpec((1, h), lambda i, t: (0, 0)),
            pl.BlockSpec((8, rows, h), lambda i, t: (0, 0, 0)),
        ],
        out_specs=[
            pl.BlockSpec((rows, h), lambda i, t: (0, 0)),
            pl.BlockSpec((rows, h), lambda i, t: (0, 0)),
            pl.BlockSpec((rows, 8), lambda i, t: (0, 0)),
        ],
        scratch_shapes=[
            pltpu.VMEM((blocks, rows, depth), BF),
            pltpu.SemaphoreType.DMA((blocks, 4)),
        ],
    )
    return pl.pallas_call(
        act_kernel,
        grid_spec=grid_spec,
        out_shape=[
            jax.ShapeDtypeStruct((rows, h), F32),
            jax.ShapeDtypeStruct((rows, h), BF),
            jax.ShapeDtypeStruct((rows, 8), F32),
        ],
        compiler_params=pltpu.CompilerParams(vmem_limit_bytes=44 * 2**20),
        cost_estimate=pl.CostEstimate(
            flops=2 * rows * blocks * depth * h, bytes_accessed=20 * 2**20, transcendentals=0
        ),
        name="pre_act",
    )(tbl, *pieces, weight, bias, shown)


def grad_kernel(tbl, *refs):
    pieces = refs[:14]
    slot_ref, shown_ref, act_ref, out_ref, bias_ref, feats, pre_ref, sems = refs[14:]
    cb = pl.program_id(0)

    @pl.when(cb == 0)
    def _():
        for copy in piece_copies(tbl, pieces, feats, sems):
            copy.start()
        total = slot_ref[:, 0:1] * shown_ref[0].astype(F32)
        for k in range(1, 8):
            total += slot_ref[:, k : k + 1] * shown_ref[k].astype(F32)
        pre = jnp.where(act_ref[...] > 0, total, F32(0.0)).astype(BF)
        pre_ref[...] = pre
        bias_ref[...] = jnp.sum(pre.astype(F32), axis=0, keepdims=True)

    wait_block(pieces, feats, sems, cb)
    out_ref[0] = lax.dot_general(
        feats[cb], pre_ref[...], (((0,), (0,)), ((), ())), preferred_element_type=F32
    ).astype(BF)


def run_grad(tbl, pieces, slot_grad, shown, act, blocks, depth):
    rows, h = act.shape
    grid_spec = pltpu.PrefetchScalarGridSpec(
        num_scalar_prefetch=1,
        grid=(blocks,),
        in_specs=[pl.BlockSpec(memory_space=pl.ANY)] * 14
        + [
            pl.BlockSpec((rows, 8), lambda i, t: (0, 0)),
            pl.BlockSpec((8, rows, h), lambda i, t: (0, 0, 0)),
            pl.BlockSpec((rows, h), lambda i, t: (0, 0)),
        ],
        out_specs=[
            pl.BlockSpec((1, depth, h), lambda i, t: (i, 0, 0)),
            pl.BlockSpec((1, h), lambda i, t: (0, 0)),
        ],
        scratch_shapes=[
            pltpu.VMEM((blocks, rows, depth), BF),
            pltpu.VMEM((rows, h), BF),
            pltpu.SemaphoreType.DMA((blocks, 4)),
        ],
    )
    return pl.pallas_call(
        grad_kernel,
        grid_spec=grid_spec,
        out_shape=[
            jax.ShapeDtypeStruct((blocks, depth, h), BF),
            jax.ShapeDtypeStruct((1, h), F32),
        ],
        compiler_params=pltpu.CompilerParams(vmem_limit_bytes=44 * 2**20),
        cost_estimate=pl.CostEstimate(
            flops=2 * rows * blocks * depth * h, bytes_accessed=20 * 2**20, transcendentals=0
        ),
        name="weight_grad",
    )(tbl, *pieces, slot_grad, shown, act)


def piece_table(x, y, c):
    ring = lambda v, j, n: (v + STEPS[j] + n) % n
    order = [(p, 0) for p in range(4)]
    for q in (1, 2, 3):
        order += [(p, q) for p in range(4)]
    rows = []
    for half in range(2):
        core = c if half == 0 else 1 - c
        for p, q in order:
            xx = jnp.where(core == 0, ring(x, q, NX), ring(x, p, NX))
            yy = jnp.where(core == 0, ring(y, p, NY), ring(y, q, NY))
            rows.append((xx // 2) * NY + yy)
            rows.append(((xx ^ x) & 1) * 2 + core)
    return jnp.stack(rows).astype(jnp.int32)


def to_slots(value, z, xl):
    turned = lax.dynamic_slice_in_dim(jnp.concatenate([value, value], 0), z, NZ, 0)
    turned = jnp.stack([turned[d % NZ] for d in SLOT_Z])
    both = jnp.concatenate([turned, turned[:, :1]], 1)
    return jnp.swapaxes(lax.dynamic_slice_in_dim(both, xl, 2, 1), 0, 1)


def from_slots(value, z, xl):
    both = jnp.swapaxes(jnp.concatenate([value, value[:1]], 0), 0, 1)
    both = lax.dynamic_slice_in_dim(both, xl, 2, 1)
    turned = jnp.stack([both[SLOT_Z.index(d if d <= 4 else d - NZ)] for d in range(NZ)])
    return lax.dynamic_slice_in_dim(
        jnp.concatenate([turned, turned], 0), (NZ - z) % NZ, NZ, 0
    )


def per_device(
    contexts, trunk_weight, trunk_bias, head_weight, head_bias, arm_embed, slots, feedback, boot_weight
):
    group = contexts.shape[0]
    cols = trunk_weight.shape[1]
    n_ctx, n_slots = slots.shape
    arms, h = arm_embed.shape
    z, xl, xh, y, c = (lax.axis_index(a) for a in AXES)
    x = xh * 2 + xl
    low = c == 0
    pick = lambda a, b: jnp.where(low, a, b)

    k = trunk_weight.shape[0]
    cols_for = lambda zz: lax.dynamic_slice_in_dim(contexts, ((zz + NZ) % NZ) * 2 * k, 2 * k, 1)
    side = jnp.where(low, 1, -1)
    ctx_in = [out_z(cols_for(z + side * i), i) for i in (1, 2, 3)]
    ctx_far = out_z(cols_for(z + 4), 4)
    w_far = x_partner(trunk_weight)
    w_own = jnp.concatenate(
        [jnp.where(xl == 0, trunk_weight, w_far), jnp.where(xl == 0, w_far, trunk_weight)], 0
    )
    w_other = other_core(w_own)
    w_all = jnp.concatenate([pick(w_own, w_other), pick(w_other, w_own)], 1)

    arm_far = x_partner(arm_embed)
    ids = to_slots(slots.reshape(NZ, 2, group, n_slots), z, xl).reshape(n_ctx, n_slots)
    shown = gather_rows(ids.T.reshape(n_slots * n_ctx, 1), arm_embed).reshape(n_slots, n_ctx, h)

    ctx_all = jnp.concatenate([pick(cols_for(z), ctx_far)] + ctx_in, 0)
    part = jnp.dot(ctx_all, w_all, preferred_element_type=F32)
    part = part.reshape(4, group, 2 * cols)
    back = [back_z(part[i], i) for i in (1, 2, 3)]
    back_far = back_z(part[0], 4)
    bias = jnp.concatenate([pick(trunk_bias, 0.0), pick(0.0, trunk_bias)])
    mine = pick(part[0], back_far) + back[0] + back[1] + back[2] + bias
    feat = jnp.maximum(mine + other_core(mine), F32(0.0)).astype(BF)

    got = [out_z(feat, i) for i in (1, 2, 3)]
    far = out_z(feat, 4)
    block = jnp.concatenate([pick(feat, far)] + got, 0)
    block = jnp.stack([block] + [first_ring(block, d) for d in (1, -1, 2)])
    a, b = block[:2], block[2:]
    up_a, down_b = last_ring(a, 1), last_ring(b, -1)
    up_b, down_a = last_ring(b, 1), last_ring(a, -1)
    two_a, two_b = last_ring(up_a, 1), last_ring(down_b, -1)
    own = [block, up_a, up_b, down_a, down_b, two_a, two_b]
    pieces = own + [other_core(v) for v in own]
    tbl = piece_table(x, y, c)

    blocks = NX * NY // 2
    weight = head_weight[0].reshape(blocks, 2 * cols, h)
    act, hidden, picks = run_act(tbl, pieces, weight, head_bias, shown)

    total = from_slots(picks.reshape(2, NZ, group, n_slots), z, xl).reshape(-1, 128)
    total = total + x_partner(total)
    for d in (1, 2, 4):
        total = total + route(total, lambda z, x, y, c, d=d: (z ^ d, x, y, c))
    boot = boot_weight[0].astype(F32)
    slot_grad = (
        boot[:, None]
        * (jax.nn.sigmoid(total.reshape(n_ctx, n_slots)) - feedback)
        / F32(n_slots)
    )
    slot_grad = to_slots(slot_grad.reshape(NZ, 2, group, n_slots), z, xl).reshape(n_ctx, n_slots)
    weight_grad, bias_grad = run_grad(tbl, pieces, slot_grad, shown, act, blocks, 2 * cols)

    near = n_ctx // 2
    hid_far = x_partner(hidden[near:])
    dims = (((1,), (1,)), ((), ()))
    share = lax.dot_general(hidden[:near], arm_embed, dims, preferred_element_type=F32)
    share += lax.dot_general(hid_far, arm_far, dims, preferred_element_type=F32)
    share = share.reshape(NZ, group, arms)
    scores = share[0]
    for s in range(1, NZ):
        d = SLOT_Z[s]
        scores = scores + route(
            share[s].astype(BF), lambda z, x, y, c, d=d: (z + d, x, y, c)
        ).astype(F32)
    return (
        scores.astype(BF)[None],
        weight_grad.reshape(1, -1, h),
        bias_grad,
    )


def solution(mesh):
    inner = Mesh(mesh.devices.reshape(NZ, 2, 2, NY, 2), AXES)
    batch, member = ("z", "xl"), ("xh", "y", "c")
    placed = (
        P(batch, None),
        P(batch, member),
        P(member),
        P(member, None, batch),
        P(member, batch),
        P(None, batch),
        P(),
        P(),
        P(member, None),
    )
    return jax.shard_map(
        per_device,
        mesh=inner,
        in_specs=placed,
        out_specs=(P(member, batch, None), P(member, None, batch), P(member, batch)),
        check_vma=False,
    )
```

```python
import functools

import jax
import jax.numpy as jnp
from jax import lax
from jax.experimental import pallas as pl
from jax.experimental.pallas import tpu as pltpu
from jax.sharding import Mesh
from jax.sharding import PartitionSpec as P

AXES = ("z", "xl", "xh", "y", "c")
NZ, NX, NY = 8, 4, 4
BF, F32 = jnp.bfloat16, jnp.float32
RING = (0, 1, 3, 2)
SLOT_Z = (0, -1, -2, -3, 4, 1, 2, 3)


def flat(z, x, y, c):
    z, x, y = z % NZ, x % NX, y % NY
    return (((z * 2 + x % 2) * 2 + x // 2) * NY + y) * 2 + c


def route(value, where):
    pairs = []
    for z in range(NZ):
        for x in range(NX):
            for y in range(NY):
                for c in range(2):
                    to = where(z, x, y, c)
                    if to is not None:
                        pairs.append((flat(z, x, y, c), flat(*to)))
    return lax.ppermute(value, AXES, pairs)


def other_core(value):
    return route(value, lambda z, x, y, c: (z, x, y, 1 - c))


def x_partner(value):
    return route(value, lambda z, x, y, c: (z, x ^ 1, y, c))


def along_z(value, i, core=None):
    return route(
        value,
        lambda z, x, y, c: (z + (i if c == 0 else -i), x, y, c) if core in (None, c) else None,
    )


def first_ring(value, d):
    return route(value, lambda z, x, y, c: (z, x, y ^ d, c) if c == 0 else (z, x ^ d, y, c))


def last_ring(value, d):
    return route(value, lambda z, x, y, c: (z, x ^ d, y, c) if c == 0 else (z, x, y ^ d, c))


VMEM = pl.BlockSpec(memory_space=pltpu.VMEM)
ANYWHERE = pl.BlockSpec(memory_space=pl.ANY)


def params(mib):
    return pltpu.CompilerParams(vmem_limit_bytes=mib * 2**20)


def group_row(rel, slot, group):
    z, xl = lax.axis_index("z"), lax.axis_index("xl")
    zz = lax.rem(z + SLOT_Z[slot] + NZ, NZ)
    return pl.multiple_of((zz * 2 + (xl if rel == 0 else 1 - xl)) * group, 16)


def gather_kernel(slots_ref, arm_ref, out_ref, ids_ref):
    n_slots, n_ctx, _ = out_ref.shape
    arms = arm_ref.shape[0]
    group = n_ctx // 16
    for rel in range(2):
        for slot in range(NZ):
            ids_ref[pl.ds((rel * NZ + slot) * group, group), :] = slots_ref[
                pl.ds(group_row(rel, slot, group), group), :
            ]
    rows = n_ctx // 2
    for half in range(2):
        part = pl.ds(half * rows, rows)
        for k in range(n_slots):
            hot = ids_ref[part, k : k + 1] == lax.broadcasted_iota(jnp.int32, (rows, arms), 1)
            out_ref[k, part, :] = jnp.dot(
                jnp.where(hot, F32(1.0), F32(0.0)).astype(BF),
                arm_ref[...],
                preferred_element_type=F32,
            ).astype(BF)


def gather_rows(slots, arm):
    (n_ctx, n_slots), (arms, h) = slots.shape, arm.shape
    return pl.pallas_call(
        gather_kernel,
        in_specs=[VMEM, VMEM],
        out_specs=VMEM,
        out_shape=jax.ShapeDtypeStruct((n_slots, n_ctx, h), BF),
        scratch_shapes=[pltpu.VMEM((n_ctx, n_slots), jnp.int32)],
        compiler_params=params(24),
        cost_estimate=pl.CostEstimate(
            flops=2 * n_ctx * n_slots * arms * h, bytes_accessed=2**23, transcendentals=0
        ),
        name="gather_rows",
    )(slots, arm)


def place_kernel(near_ref, far_ref, arm_ref, *refs):
    out_ref, arm_out_ref = refs[-2:]
    k = near_ref.shape[0]
    xl = lax.axis_index("xl")
    out_ref[pl.ds(pl.multiple_of(xl * k, 16), k), :] = near_ref[...]
    out_ref[pl.ds(pl.multiple_of((1 - xl) * k, 16), k), :] = far_ref[...]
    arm_out_ref[...] = arm_ref[...]


def place(near, far, arm, after):
    k, n = near.shape
    return pl.pallas_call(
        place_kernel,
        in_specs=[VMEM] * 3 + [ANYWHERE] * len(after),
        out_specs=[VMEM] * 2,
        out_shape=[jax.ShapeDtypeStruct((2 * k, n), BF), jax.ShapeDtypeStruct(arm.shape, BF)],
        compiler_params=params(16),
        cost_estimate=pl.CostEstimate(flops=0, bytes_accessed=2**22, transcendentals=0),
        name="place_weight",
    )(near, far, arm, *after)


def feature_kernel(a_ref, b_ref, after_ref, out_ref):
    del after_ref
    out_ref[...] = jnp.maximum(a_ref[...] + b_ref[...], F32(0.0)).astype(BF)


def features_of(a, b, after):
    return pl.pallas_call(
        feature_kernel,
        in_specs=[VMEM, VMEM, ANYWHERE],
        out_specs=VMEM,
        out_shape=jax.ShapeDtypeStruct(a.shape, BF),
        compiler_params=params(8),
        cost_estimate=pl.CostEstimate(flops=a.size, bytes_accessed=a.size * 10, transcendentals=0),
        name="features",
    )(a, b, after)


def trunk_kernel(c0_ref, c4_ref, c1_ref, c2_ref, c3_ref, wa_ref, wb_ref, p0, p1, p2, p3, ctx_ref):
    core = lax.axis_index("c")
    group = c0_ref.shape[0]
    n = wa_ref.shape[1]

    @pl.when(core == 0)
    def _():
        ctx_ref[:group, :] = c0_ref[...]

    @pl.when(core == 1)
    def _():
        ctx_ref[:group, :] = c4_ref[...]

    for i, ref in enumerate((c1_ref, c2_ref, c3_ref)):
        ctx_ref[pl.ds((i + 1) * group, group), :] = ref[...]
    for own, w_ref in ((True, wa_ref), (False, wb_ref)):
        where = core if own else 1 - core
        part = jnp.dot(ctx_ref[...], w_ref[...], preferred_element_type=F32)
        for i, ref in enumerate((p0, p1, p2, p3)):
            ref[:, pl.ds(pl.multiple_of(where * n, 128), n)] = part[i * group : (i + 1) * group]


def trunk(ctx, w_own, w_other):
    group, n = ctx[0].shape[0], w_own.shape[1]
    return pl.pallas_call(
        trunk_kernel,
        in_specs=[VMEM] * 7,
        out_specs=[VMEM] * 4,
        out_shape=[jax.ShapeDtypeStruct((group, 2 * n), F32)] * 4,
        scratch_shapes=[pltpu.VMEM((4 * group, ctx[0].shape[1]), BF)],
        compiler_params=params(16),
        cost_estimate=pl.CostEstimate(
            flops=8 * group * ctx[0].shape[1] * 2 * n, bytes_accessed=2**22, transcendentals=0
        ),
        name="trunk_sums",
    )(*ctx, w_own, w_other)


def blocks_of(p, q, core):
    return (RING[q], RING[p]) if core == 0 else (RING[p], RING[q])


def act_kernel(qs, first, last, *refs):
    n = 4 * len(qs)
    pieces, refs = refs[:n], refs[n:]
    w_ref, start_ref = refs[:2]
    if last:
        shown_ref, act_ref, near_ref, far_ref, pick_ref, flat_ref = refs[2:]
    else:
        act_ref = refs[2]
    x_hi, y, core = lax.axis_index("xh"), lax.axis_index("y"), lax.axis_index("c")
    rows = pieces[0].shape[1]
    act_ref[...] = jnp.broadcast_to(start_ref[...], act_ref.shape)
    for half in range(2):
        of = core if half == 0 else 1 - core
        for i, q in enumerate(qs):
            for p in range(4):
                ref = pieces[half * 2 * len(qs) + 2 * i + p // 2]
                x0, y0 = blocks_of(p, q, 0)
                x1, y1 = blocks_of(p, q, 1)
                dx, dy = jnp.where(of == 0, x0, x1), jnp.where(of == 0, y0, y1)
                cb = lax.bitwise_xor(x_hi, lax.div(dx, 2)) * NY + lax.bitwise_xor(y, dy)
                rg = lax.rem(dx, 2) * 2 + of
                part = pl.ds(pl.multiple_of(rg * rows, 16), rows)
                act_ref[part, :] += jnp.dot(ref[p % 2], w_ref[cb], preferred_element_type=F32)
    if last:
        hid = jnp.maximum(act_ref[...], F32(0.0)).astype(BF)
        half_rows = near_ref.shape[0]
        near_ref[...] = hid[:half_rows]
        far_ref[...] = hid[half_rows:]
        wide = hid.astype(F32)
        lane = lax.broadcasted_iota(jnp.int32, (hid.shape[0], 128), 1)
        total = jnp.zeros((hid.shape[0], 128), F32)
        for k in range(8):
            one = jnp.sum(wide * shown_ref[k].astype(F32), axis=1, keepdims=True)
            total = jnp.where(lane == k, one, total)
        group = hid.shape[0] // 16
        for rel in range(2):
            for slot in range(NZ):
                at = (rel * NZ + slot) * group
                flat_ref[pl.ds(group_row(rel, slot, group), group), :] = total[at : at + group]
        pick_ref[...] = jnp.transpose(flat_ref[...])[:8]


def run_act(qs, pieces, weight, start, shown=None):
    blocks, depth, h = weight.shape
    rows = 4 * pieces[0].shape[1]
    first, last = start.shape[0] == 1, shown is not None
    shapes = [jax.ShapeDtypeStruct((rows, h), F32)]
    if last:
        shapes += [jax.ShapeDtypeStruct((rows // 2, h), BF)] * 2
        shapes += [jax.ShapeDtypeStruct((8, rows), F32)]
    args = list(pieces) + [weight, start] + ([shown] if last else [])
    return pl.pallas_call(
        functools.partial(act_kernel, qs, first, last),
        in_specs=[VMEM] * len(args),
        out_specs=[VMEM] * len(shapes),
        out_shape=shapes,
        scratch_shapes=[pltpu.VMEM((rows, 128), F32)] if last else [],
        compiler_params=params(24),
        cost_estimate=pl.CostEstimate(
            flops=2 * rows * blocks * depth * h * len(qs) // 4,
            bytes_accessed=len(qs) * 4 * 2**20,
            transcendentals=0,
        ),
        name="pre_act",
    )(*args)


def grad_kernel(n_slots, *refs):
    pieces = refs[:16]
    sum_ref, fed_ref, boot_ref, shown_ref, act_ref, out_ref, bias_ref = refs[16:23]
    flat_ref, slot_ref, pre_ref, stage, sems = refs[23:]
    x_hi, y, core = lax.axis_index("xh"), lax.axis_index("y"), lax.axis_index("c")
    rows, depth = pieces[0].shape[1:]
    n_ctx = act_ref.shape[0]
    group = n_ctx // 16
    grad = boot_ref[...] * (jax.nn.sigmoid(sum_ref[...]) - fed_ref[...]) / F32(n_slots)
    grad = jnp.concatenate([grad, jnp.zeros((128 - n_slots, n_ctx), F32)], 0)
    flat_ref[...] = jnp.transpose(grad)
    for rel in range(2):
        for slot in range(NZ):
            slot_ref[pl.ds((rel * NZ + slot) * group, group), :] = flat_ref[
                pl.ds(group_row(rel, slot, group), group), :
            ]
    total = slot_ref[:, 0:1] * shown_ref[0].astype(F32)
    for k in range(1, n_slots):
        total += slot_ref[:, k : k + 1] * shown_ref[k].astype(F32)
    pre = jnp.where(act_ref[...] > 0, total, F32(0.0)).astype(BF)
    pre_ref[...] = pre
    bias_ref[...] = jnp.sum(pre.astype(F32), axis=0, keepdims=True)

    def half_of(mine, core_of, dx, dy):
        p, q = (RING.index(dy), RING.index(dx)) if core_of == 0 else (RING.index(dx), RING.index(dy))
        return pieces[(0 if mine else 8) + 2 * q + p // 2], p % 2

    def run(own):
        copies = []
        for r in range(2):
            for dy in range(4):
                n = len(copies)
                slot = n % 2
                if n >= 2:
                    copies[n - 2].wait()
                parts = []
                for rg in range(4):
                    dx, core_of = 2 * r + rg // 2, rg % 2
                    parts.append(half_of(core_of == own, core_of, dx, dy))
                total = None
                for rg, (ref, k) in enumerate(parts):
                    one = lax.dot_general(
                        ref[k],
                        pre_ref[pl.ds(rg * rows, rows), :],
                        (((0,), (0,)), ((), ())),
                        preferred_element_type=F32,
                    )
                    total = one if total is None else total + one
                stage[slot] = total.astype(BF)
                cb = lax.bitwise_xor(x_hi, r) * NY + lax.bitwise_xor(y, dy)
                copy = pltpu.make_async_copy(stage.at[slot], out_ref.at[cb], sems.at[slot])
                copy.start()
                copies.append(copy)
        for copy in copies[-2:]:
            copy.wait()

    @pl.when(core == 0)
    def _():
        run(0)

    @pl.when(core == 1)
    def _():
        run(1)


def run_grad(pieces, sums, fed, boot, shown, act, blocks):
    rows, h = act.shape
    depth = pieces[0].shape[2]
    n_slots = shown.shape[0]
    return pl.pallas_call(
        functools.partial(grad_kernel, n_slots),
        in_specs=[VMEM] * 21,
        out_specs=[ANYWHERE, VMEM],
        out_shape=[
            jax.ShapeDtypeStruct((blocks, depth, h), BF),
            jax.ShapeDtypeStruct((1, h), F32),
        ],
        scratch_shapes=[
            pltpu.VMEM((rows, 128), F32),
            pltpu.VMEM((rows, 128), F32),
            pltpu.VMEM((rows, h), BF),
            pltpu.VMEM((2, depth, h), BF),
            pltpu.SemaphoreType.DMA((2,)),
        ],
        compiler_params=params(28),
        cost_estimate=pl.CostEstimate(
            flops=2 * rows * blocks * depth * h, bytes_accessed=20 * 2**20, transcendentals=0
        ),
        name="weight_grad",
    )(*pieces, sums, fed, boot, shown, act)


def share_kernel(near_ref, far_ref, arm_ref, armf_ref, *outs):
    dims = (((1,), (1,)), ((), ()))
    arms = arm_ref.shape[0]
    group = near_ref.shape[0] // NZ
    step = 512
    for j in range(0, arms, step):
        part = lax.dot_general(
            near_ref[...], arm_ref[pl.ds(j, step), :], dims, preferred_element_type=F32
        ) + lax.dot_general(
            far_ref[...], armf_ref[pl.ds(j, step), :], dims, preferred_element_type=F32
        )
        for s in range(NZ):
            piece = part[s * group : (s + 1) * group]
            if s == 4:
                half = arms // 2
                out = outs[4] if j < half else outs[8]
                out[:, pl.ds(j % half, step)] = piece.astype(BF)
            else:
                outs[s][:, pl.ds(j, step)] = piece.astype(outs[s].dtype)


def share_scores(near, far, arm, arm_far):
    group, arms = near.shape[0] // NZ, arm.shape[0]
    kinds = [F32 if s in (0, 2, 6) else BF for s in range(NZ)]
    shapes = [jax.ShapeDtypeStruct((group, arms // 2 if s == 4 else arms), kinds[s]) for s in range(NZ)]
    shapes.append(shapes[4])
    return pl.pallas_call(
        share_kernel,
        in_specs=[VMEM] * 4,
        out_specs=[VMEM] * 9,
        out_shape=shapes,
        compiler_params=params(24),
        cost_estimate=pl.CostEstimate(
            flops=4 * near.shape[0] * near.shape[1] * arms, bytes_accessed=2**22, transcendentals=0
        ),
        name="share_scores",
    )(near, far, arm, arm_far)


def z_shift(value, d):
    return route(value, lambda z, x, y, c: (z + d, x, y, c))


def per_device(
    contexts, trunk_weight, trunk_bias, head_weight, head_bias, arm_embed, slots, feedback, boot_weight
):
    cols = trunk_weight.shape[1]
    h = arm_embed.shape[1]
    z, c = lax.axis_index("z"), lax.axis_index("c")
    low = c == 0
    pick = lambda a, b: jnp.where(low, a, b)

    k = trunk_weight.shape[0]
    cols_for = lambda zz: lax.dynamic_slice_in_dim(contexts, ((zz + NZ) % NZ) * 2 * k, 2 * k, 1)
    side = jnp.where(low, 1, -1)
    ctx = [along_z(cols_for(z + side * i), i) for i in (1, 2, 3)]
    ctx_far = along_z(cols_for(z + 4), 4, core=1)
    ctx = [cols_for(z), ctx_far] + ctx
    w_far = x_partner(trunk_weight)
    shown = gather_rows(slots, arm_embed)
    w_own, arm_copy = place(trunk_weight, w_far, arm_embed, ctx + [shown])
    arm_far = x_partner(arm_copy)
    w_other = other_core(w_own)
    p0, p1, p2, p3 = trunk(ctx, w_own, w_other)

    third = along_z(p3, -1)
    fourth = along_z(p0, -4 + 2, core=1)
    next_one = along_z(p1, -1)
    second = along_z(p2 + third + fourth, -2)
    bias = jnp.concatenate([pick(trunk_bias, 0.0), pick(0.0, trunk_bias)])
    mine = pick(p0, 0.0) + next_one + second + bias
    feat = features_of(mine, other_core(mine), arm_far)

    got = [along_z(feat, i) for i in (1, 2, 3)]
    far = along_z(feat, 4, core=1)
    block = jnp.concatenate([pick(feat, far)] + got, 0)
    ring = [block] + [first_ring(block, d) for d in RING[1:]]
    a, b = jnp.stack(ring[:2]), jnp.stack(ring[2:])
    s_a, t_a = last_ring(a, 1), last_ring(a, 3)
    s_b, t_b = last_ring(b, 1), last_ring(b, 3)
    u_a, u_b = last_ring(s_a, 3), last_ring(t_b, 1)
    own = [a, b, s_a, s_b, t_a, t_b, u_a, u_b]
    other = [other_core(v) for v in own]
    both = lambda i, j: own[i:j] + other[i:j]

    blocks = NX * NY // 2
    weight = head_weight[0].reshape(blocks, 2 * cols, h)
    (act,) = run_act((0,), both(0, 2), weight, head_bias)
    (act,) = run_act((1, 2), both(2, 6), weight, act)
    act, near, far, total = run_act((3,), both(6, 8), weight, act, shown)

    share = share_scores(near, x_partner(far), arm_embed, arm_far)
    up3, down3 = z_shift(share[7], 1), z_shift(share[3], -1)
    up4, down4 = z_shift(share[4], 2), z_shift(share[8], -2)
    up1, down1 = z_shift(share[5], 1), z_shift(share[1], -1)
    none = jnp.zeros_like(up4)
    up2 = share[6] + up3.astype(F32) + jnp.concatenate([up4, none], 1).astype(F32)
    down2 = share[2] + down3.astype(F32) + jnp.concatenate([none, down4], 1).astype(F32)
    up2, down2 = z_shift(up2.astype(BF), 2), z_shift(down2.astype(BF), -2)
    scores = share[0]
    for part in (up1, down1, up2, down2):
        scores = scores + part.astype(F32)

    total = total + x_partner(total)
    for d in (1, 2, 4):
        total = total + route(total, lambda z, x, y, c, d=d: (z ^ d, x, y, c))
    weight_grad, bias_grad = run_grad(
        own + other, total, feedback.T, boot_weight.astype(F32), shown, act, blocks
    )
    return (
        scores.astype(BF)[None],
        weight_grad.reshape(1, -1, h),
        bias_grad,
    )


def solution(mesh):
    inner = Mesh(mesh.devices.reshape(NZ, 2, 2, NY, 2), AXES)
    batch, member = ("z", "xl"), ("xh", "y", "c")
    placed = (
        P(batch, None),
        P(batch, member),
        P(member),
        P(member, None, batch),
        P(member, batch),
        P(None, batch),
        P(),
        P(),
        P(member, None),
    )
    return jax.shard_map(
        per_device,
        mesh=inner,
        in_specs=placed,
        out_specs=(P(member, batch, None), P(member, None, batch), P(member, batch)),
        check_vma=False,
    )
```

```python
import functools

import jax
import jax.numpy as jnp
from jax import lax
from jax.experimental import pallas as pl
from jax.experimental.pallas import tpu as pltpu
from jax.sharding import Mesh
from jax.sharding import PartitionSpec as P

AXES = ("z", "xl", "xh", "y", "c")
NZ, NX, NY = 8, 4, 4
BF, F32 = jnp.bfloat16, jnp.float32
GRAD_COST, JOIN_COST, FINAL_COST = 2**30, 2**34, 2**34
RING = (0, 1, 3, 2)
SLOT_Z = (0, -1, -2, -3, 4, 1, 2, 3)


def flat(z, x, y, c):
    z, x, y = z % NZ, x % NX, y % NY
    return (((z * 2 + x % 2) * 2 + x // 2) * NY + y) * 2 + c


def route(value, where):
    pairs = []
    for z in range(NZ):
        for x in range(NX):
            for y in range(NY):
                for c in range(2):
                    to = where(z, x, y, c)
                    if to is not None:
                        pairs.append((flat(z, x, y, c), flat(*to)))
    return lax.ppermute(value, AXES, pairs)


def other_core(value):
    return route(value, lambda z, x, y, c: (z, x, y, 1 - c))


def x_partner(value):
    return route(value, lambda z, x, y, c: (z, x ^ 1, y, c))


def along_z(value, i, core=None):
    return route(
        value,
        lambda z, x, y, c: (z + (i if c == 0 else -i), x, y, c) if core in (None, c) else None,
    )


def first_ring(value, d):
    return route(value, lambda z, x, y, c: (z, x, y ^ d, c) if c == 0 else (z, x ^ d, y, c))


def last_ring(value, d):
    return route(value, lambda z, x, y, c: (z, x ^ d, y, c) if c == 0 else (z, x, y ^ d, c))


VMEM = pl.BlockSpec(memory_space=pltpu.VMEM)
ANYWHERE = pl.BlockSpec(memory_space=pl.ANY)


def params(mib):
    return pltpu.CompilerParams(vmem_limit_bytes=mib * 2**20)


def group_row(rel, slot, group):
    z, xl = lax.axis_index("z"), lax.axis_index("xl")
    zz = lax.rem(z + SLOT_Z[slot] + NZ, NZ)
    return pl.multiple_of((zz * 2 + (xl if rel == 0 else 1 - xl)) * group, 16)


def gather_kernel(slots_ref, arm_ref, out_ref, ids_ref):
    n_slots, n_ctx, _ = out_ref.shape
    arms = arm_ref.shape[0]
    group = n_ctx // 16
    for rel in range(2):
        for slot in range(NZ):
            ids_ref[pl.ds((rel * NZ + slot) * group, group), :] = slots_ref[
                pl.ds(group_row(rel, slot, group), group), :
            ]
    rows = n_ctx // 2
    for half in range(2):
        part = pl.ds(half * rows, rows)
        for k in range(n_slots):
            hot = ids_ref[part, k : k + 1] == lax.broadcasted_iota(jnp.int32, (rows, arms), 1)
            out_ref[k, part, :] = jnp.dot(
                jnp.where(hot, F32(1.0), F32(0.0)).astype(BF),
                arm_ref[...],
                preferred_element_type=F32,
            ).astype(BF)


def gather_rows(slots, arm):
    (n_ctx, n_slots), (arms, h) = slots.shape, arm.shape
    return pl.pallas_call(
        gather_kernel,
        in_specs=[VMEM, VMEM],
        out_specs=VMEM,
        out_shape=jax.ShapeDtypeStruct((n_slots, n_ctx, h), BF),
        scratch_shapes=[pltpu.VMEM((n_ctx, n_slots), jnp.int32)],
        compiler_params=params(24),
        cost_estimate=pl.CostEstimate(
            flops=2 * n_ctx * n_slots * arms * h, bytes_accessed=2**23, transcendentals=0
        ),
        name="gather_rows",
    )(slots, arm)


def place_kernel(near_ref, far_ref, arm_ref, *refs):
    out_ref, arm_out_ref = refs[-2:]
    k = near_ref.shape[0]
    xl = lax.axis_index("xl")
    out_ref[pl.ds(pl.multiple_of(xl * k, 16), k), :] = near_ref[...]
    out_ref[pl.ds(pl.multiple_of((1 - xl) * k, 16), k), :] = far_ref[...]
    arm_out_ref[...] = arm_ref[...]


def place(near, far, arm, after):
    k, n = near.shape
    return pl.pallas_call(
        place_kernel,
        in_specs=[VMEM] * 3 + [ANYWHERE] * len(after),
        out_specs=[VMEM] * 2,
        out_shape=[jax.ShapeDtypeStruct((2 * k, n), BF), jax.ShapeDtypeStruct(arm.shape, BF)],
        compiler_params=params(16),
        cost_estimate=pl.CostEstimate(flops=0, bytes_accessed=2**22, transcendentals=0),
        name="place_weight",
    )(near, far, arm, *after)


def stack_kernel(own_ref, far_ref, g1_ref, g2_ref, g3_ref, after_ref, out_ref):
    del after_ref
    core = lax.axis_index("c")
    group = own_ref.shape[0]

    @pl.when(core == 0)
    def _():
        out_ref[:group, :] = own_ref[...]

    @pl.when(core == 1)
    def _():
        out_ref[:group, :] = far_ref[...]

    for i, ref in enumerate((g1_ref, g2_ref, g3_ref)):
        out_ref[pl.ds((i + 1) * group, group), :] = ref[...]


def stack_rows(own, far, got, after):
    group, n = own.shape
    return pl.pallas_call(
        stack_kernel,
        in_specs=[VMEM] * 5 + [ANYWHERE],
        out_specs=VMEM,
        out_shape=jax.ShapeDtypeStruct((4 * group, n), BF),
        compiler_params=params(8),
        cost_estimate=pl.CostEstimate(flops=0, bytes_accessed=16 * group * n, transcendentals=0),
        name="stack_rows",
    )(own, far, *got, after)


def trunk_kernel(c0_ref, c4_ref, c1_ref, c2_ref, c3_ref, wa_ref, wb_ref, p0, p1, p2, p3, ctx_ref):
    core = lax.axis_index("c")
    group = c0_ref.shape[0]
    n = wa_ref.shape[1]

    @pl.when(core == 0)
    def _():
        ctx_ref[:group, :] = c0_ref[...]

    @pl.when(core == 1)
    def _():
        ctx_ref[:group, :] = c4_ref[...]

    for i, ref in enumerate((c1_ref, c2_ref, c3_ref)):
        ctx_ref[pl.ds((i + 1) * group, group), :] = ref[...]
    for own, w_ref in ((True, wa_ref), (False, wb_ref)):
        where = core if own else 1 - core
        part = jnp.dot(ctx_ref[...], w_ref[...], preferred_element_type=F32)
        for i, ref in enumerate((p0, p1, p2, p3)):
            ref[:, pl.ds(pl.multiple_of(where * n, 128), n)] = part[i * group : (i + 1) * group]


def trunk(ctx, w_own, w_other):
    group, n = ctx[0].shape[0], w_own.shape[1]
    return pl.pallas_call(
        trunk_kernel,
        in_specs=[VMEM] * 7,
        out_specs=[VMEM] * 4,
        out_shape=[jax.ShapeDtypeStruct((group, 2 * n), F32)] * 4,
        scratch_shapes=[pltpu.VMEM((4 * group, ctx[0].shape[1]), BF)],
        compiler_params=params(16),
        cost_estimate=pl.CostEstimate(
            flops=8 * group * ctx[0].shape[1] * 2 * n, bytes_accessed=2**22, transcendentals=0
        ),
        name="trunk_sums",
    )(*ctx, w_own, w_other)


def blocks_of(p, q, core):
    return (RING[q], RING[p]) if core == 0 else (RING[p], RING[q])


def act_kernel(qs, first, last, *refs):
    n = 4 * len(qs)
    pieces, refs = refs[:n], refs[n:]
    w_ref, start_ref = refs[:2]
    if last:
        shown_ref, act_ref, near_ref, far_ref, pick_ref, flat_ref = refs[2:]
    else:
        act_ref = refs[2]
    x_hi, y, core = lax.axis_index("xh"), lax.axis_index("y"), lax.axis_index("c")
    rows = pieces[0].shape[1]
    act_ref[...] = jnp.broadcast_to(start_ref[...], act_ref.shape)
    for half in range(2):
        of = core if half == 0 else 1 - core
        for i, q in enumerate(qs):
            for p in range(4):
                ref = pieces[half * 2 * len(qs) + 2 * i + p // 2]
                x0, y0 = blocks_of(p, q, 0)
                x1, y1 = blocks_of(p, q, 1)
                dx, dy = jnp.where(of == 0, x0, x1), jnp.where(of == 0, y0, y1)
                cb = lax.bitwise_xor(x_hi, lax.div(dx, 2)) * NY + lax.bitwise_xor(y, dy)
                rg = lax.rem(dx, 2) * 2 + of
                part = pl.ds(pl.multiple_of(rg * rows, 16), rows)
                act_ref[part, :] += jnp.dot(ref[p % 2], w_ref[cb], preferred_element_type=F32)
    if last:
        hid = jnp.maximum(act_ref[...], F32(0.0)).astype(BF)
        half_rows = near_ref.shape[0]
        near_ref[...] = hid[:half_rows]
        far_ref[...] = hid[half_rows:]
        wide = hid.astype(F32)
        lane = lax.broadcasted_iota(jnp.int32, (hid.shape[0], 128), 1)
        total = jnp.zeros((hid.shape[0], 128), F32)
        for k in range(8):
            one = jnp.sum(wide * shown_ref[k].astype(F32), axis=1, keepdims=True)
            total = jnp.where(lane == k, one, total)
        group = hid.shape[0] // 16
        for rel in range(2):
            for slot in range(NZ):
                at = (rel * NZ + slot) * group
                flat_ref[pl.ds(group_row(rel, slot, group), group), :] = total[at : at + group]
        pick_ref[...] = jnp.transpose(flat_ref[...])[:8]


def run_act(qs, pieces, weight, start, shown=None):
    blocks, depth, h = weight.shape
    rows = 4 * pieces[0].shape[1]
    first, last = start.shape[0] == 1, shown is not None
    shapes = [jax.ShapeDtypeStruct((rows, h), F32)]
    if last:
        shapes += [jax.ShapeDtypeStruct((rows // 2, h), BF)] * 2
        shapes += [jax.ShapeDtypeStruct((8, rows), F32)]
    args = list(pieces) + [weight, start] + ([shown] if last else [])
    return pl.pallas_call(
        functools.partial(act_kernel, qs, first, last),
        in_specs=[VMEM] * len(args),
        out_specs=[VMEM] * len(shapes),
        out_shape=shapes,
        scratch_shapes=[pltpu.VMEM((rows, 128), F32)] if last else [],
        compiler_params=params(24),
        cost_estimate=pl.CostEstimate(
            flops=2 * rows * blocks * depth * h * len(qs) // 4,
            bytes_accessed=len(qs) * 4 * 2**20,
            transcendentals=0,
        ),
        name="pre_act",
    )(*args)


def turn_kernel(*refs):
    pieces, out_ref = refs[:16], refs[16]
    core = lax.axis_index("c")
    rows, depth = pieces[0].shape[1:]

    def half_of(mine, core_of, dx, dy):
        p, q = (RING.index(dy), RING.index(dx)) if core_of == 0 else (RING.index(dx), RING.index(dy))
        return pieces[(0 if mine else 8) + 2 * q + p // 2], p % 2

    def run(own):
        for r in range(2):
            for dy in range(4):
                for low in range(2):
                    dx = 2 * r + low
                    (a, i), (b, j) = (half_of(of == own, of, dx, dy) for of in range(2))
                    both = jnp.concatenate([a[i], b[j]], 0)
                    out_ref[r * 4 + dy, :, pl.ds(low * 2 * rows, 2 * rows)] = jnp.transpose(both)

    @pl.when(core == 0)
    def _():
        run(0)

    @pl.when(core == 1)
    def _():
        run(1)


def turned(pieces):
    rows, depth = pieces[0].shape[1:]
    return pl.pallas_call(
        turn_kernel,
        in_specs=[VMEM] * 16,
        out_specs=VMEM,
        out_shape=jax.ShapeDtypeStruct((8, depth, 4 * rows), BF),
        compiler_params=params(8),
        cost_estimate=pl.CostEstimate(flops=0, bytes_accessed=24 * 2**20, transcendentals=0),
        name="turn_features",
    )(*pieces)


def grad_kernel(n_slots, feats_ref, sum_ref, fed_ref, boot_ref, shown_ref, act_ref, *refs):
    out_ref, bias_ref, flat_ref, slot_ref, pre_ref, stage, sems = refs
    x_hi, y = lax.axis_index("xh"), lax.axis_index("y")
    n_ctx = act_ref.shape[0]
    group = n_ctx // 16
    grad = boot_ref[...] * (jax.nn.sigmoid(sum_ref[...]) - fed_ref[...]) / F32(n_slots)
    grad = jnp.concatenate([grad, jnp.zeros((128 - n_slots, n_ctx), F32)], 0)
    flat_ref[...] = jnp.transpose(grad)
    for rel in range(2):
        for slot in range(NZ):
            slot_ref[pl.ds((rel * NZ + slot) * group, group), :] = flat_ref[
                pl.ds(group_row(rel, slot, group), group), :
            ]
    total = slot_ref[:, 0:1] * shown_ref[0].astype(F32)
    for k in range(1, n_slots):
        total += slot_ref[:, k : k + 1] * shown_ref[k].astype(F32)
    pre = jnp.where(act_ref[...] > 0, total, F32(0.0)).astype(BF)
    pre_ref[...] = pre
    bias_ref[...] = jnp.sum(pre.astype(F32), axis=0, keepdims=True)
    copies = []
    for n in range(feats_ref.shape[0]):
        slot = n % 2
        if n >= 2:
            copies[n - 2].wait()
        stage[slot] = jnp.dot(feats_ref[n], pre_ref[...], preferred_element_type=F32).astype(BF)
        cb = lax.bitwise_xor(x_hi, n // 4) * NY + lax.bitwise_xor(y, n % 4)
        copy = pltpu.make_async_copy(stage.at[slot], out_ref.at[cb], sems.at[slot])
        copy.start()
        copies.append(copy)
    for copy in copies[-2:]:
        copy.wait()


def run_grad(feats, sums, fed, boot, shown, act):
    rows, h = act.shape
    blocks, depth, _ = feats.shape
    n_slots = shown.shape[0]
    return pl.pallas_call(
        functools.partial(grad_kernel, n_slots),
        in_specs=[VMEM] * 6,
        out_specs=[ANYWHERE, VMEM],
        out_shape=[
            jax.ShapeDtypeStruct((blocks, depth, h), BF),
            jax.ShapeDtypeStruct((1, h), F32),
        ],
        scratch_shapes=[
            pltpu.VMEM((rows, 128), F32),
            pltpu.VMEM((rows, 128), F32),
            pltpu.VMEM((rows, h), BF),
            pltpu.VMEM((2, depth, h), BF),
            pltpu.SemaphoreType.DMA((2,)),
        ],
        compiler_params=params(20),
        cost_estimate=pl.CostEstimate(flops=GRAD_COST, bytes_accessed=2**20, transcendentals=0),
        name="weight_grad",
    )(feats, sums, fed, boot, shown, act)


def share_kernel(near_ref, far_ref, arm_ref, armf_ref, *refs):
    outs = refs[-9:]
    dims = (((1,), (1,)), ((), ()))
    arms = arm_ref.shape[0]
    group = near_ref.shape[0] // NZ
    step = 512
    for j in range(0, arms, step):
        part = lax.dot_general(
            near_ref[...], arm_ref[pl.ds(j, step), :], dims, preferred_element_type=F32
        ) + lax.dot_general(
            far_ref[...], armf_ref[pl.ds(j, step), :], dims, preferred_element_type=F32
        )
        for s in range(NZ):
            piece = part[s * group : (s + 1) * group]
            if s == 4:
                half = arms // 2
                out = outs[4] if j < half else outs[8]
                out[:, pl.ds(j % half, step)] = piece.astype(BF)
            else:
                outs[s][:, pl.ds(j, step)] = piece.astype(outs[s].dtype)


def share_scores(near, far, arm, arm_far, after):
    group, arms = near.shape[0] // NZ, arm.shape[0]
    kinds = [F32 if s in (0, 2, 6) else BF for s in range(NZ)]
    shapes = [jax.ShapeDtypeStruct((group, arms // 2 if s == 4 else arms), kinds[s]) for s in range(NZ)]
    shapes.append(shapes[4])
    return pl.pallas_call(
        share_kernel,
        in_specs=[VMEM] * 4 + [ANYWHERE] * len(after),
        out_specs=[VMEM] * 9,
        out_shape=shapes,
        compiler_params=params(24),
        cost_estimate=pl.CostEstimate(
            flops=4 * near.shape[0] * near.shape[1] * arms, bytes_accessed=2**22, transcendentals=0
        ),
        name="share_scores",
    )(near, far, arm, arm_far, *after)


def join_kernel(*refs):
    ins, outs = refs[:6], refs[7:]
    half = ins[2].shape[1]
    for i, out_ref in enumerate(outs):
        own_ref, near_ref, far_ref = ins[3 * i : 3 * i + 3]
        for at in range(0, 2 * half, half):
            part = pl.ds(at, half)
            total = own_ref[:, part] + near_ref[:, part].astype(F32)
            if at == i * half:
                total += far_ref[...].astype(F32)
            out_ref[:, part] = total.astype(BF)


def join(up, down, after):
    own = up[0]
    return pl.pallas_call(
        join_kernel,
        in_specs=[VMEM] * 6 + [ANYWHERE],
        out_specs=[VMEM] * 2,
        out_shape=[jax.ShapeDtypeStruct(own.shape, BF)] * 2,
        compiler_params=params(8),
        cost_estimate=pl.CostEstimate(flops=JOIN_COST, bytes_accessed=2**20, transcendentals=0),
        name="join_shares",
    )(*up, *down, after)


def final_kernel(own_ref, *refs):
    total = own_ref[...]
    for ref in refs[:-1]:
        total = total + ref[...].astype(F32)
    refs[-1][...] = total.astype(BF)


def final_sum(own, parts):
    return pl.pallas_call(
        final_kernel,
        in_specs=[VMEM] * (1 + len(parts)),
        out_specs=VMEM,
        out_shape=jax.ShapeDtypeStruct(own.shape, BF),
        compiler_params=params(8),
        cost_estimate=pl.CostEstimate(flops=FINAL_COST, bytes_accessed=2**20, transcendentals=0),
        name="sum_shares",
    )(own, *parts)


def z_shift(value, d):
    return route(value, lambda z, x, y, c: (z + d, x, y, c))


def per_device(
    contexts, trunk_weight, trunk_bias, head_weight, head_bias, arm_embed, slots, feedback, boot_weight
):
    cols = trunk_weight.shape[1]
    h = arm_embed.shape[1]
    z, c = lax.axis_index("z"), lax.axis_index("c")
    low = c == 0
    pick = lambda a, b: jnp.where(low, a, b)

    k = trunk_weight.shape[0]
    cols_for = lambda zz: lax.dynamic_slice_in_dim(contexts, ((zz + NZ) % NZ) * 2 * k, 2 * k, 1)
    side = jnp.where(low, 1, -1)
    ctx = [along_z(cols_for(z + side * i), i) for i in (1, 2, 3)]
    ctx_far = along_z(cols_for(z + 4), 4, core=1)
    ctx = [cols_for(z), ctx_far] + ctx
    w_far = x_partner(trunk_weight)
    shown = gather_rows(slots, arm_embed)
    w_own, arm_copy = place(trunk_weight, w_far, arm_embed, ctx + [shown])
    arm_far = x_partner(arm_copy)
    w_other = other_core(w_own)
    p0, p1, p2, p3 = trunk(ctx, w_own, w_other)

    third = along_z(p3, -1)
    fourth = along_z(p0, -4 + 2, core=1)
    next_one = along_z(p1, -1)
    second = along_z(p2 + third + fourth, -2)
    bias = jnp.concatenate([pick(trunk_bias, 0.0), pick(0.0, trunk_bias)])
    mine = pick(p0, 0.0) + next_one + second + bias
    feat = jnp.maximum(mine + other_core(mine), F32(0.0)).astype(BF)

    got = [along_z(feat, i) for i in (1, 2, 3)]
    far = along_z(feat, 4, core=1)
    block = stack_rows(feat, far, got, arm_far)
    ring = [block] + [first_ring(block, d) for d in RING[1:]]
    a, b = jnp.stack(ring[:2]), jnp.stack(ring[2:])
    s_a, t_a = last_ring(a, 1), last_ring(a, 3)
    s_b, t_b = last_ring(b, 1), last_ring(b, 3)
    u_a, u_b = last_ring(s_a, 3), last_ring(t_b, 1)
    own = [a, b, s_a, s_b, t_a, t_b, u_a, u_b]
    other = [other_core(v) for v in own]
    both = lambda i, j: own[i:j] + other[i:j]

    blocks = NX * NY // 2
    weight = head_weight[0].reshape(blocks, 2 * cols, h)
    (act,) = run_act((0,), both(0, 2), weight, head_bias)
    (act,) = run_act((1, 2), both(2, 6), weight, act)
    act, near, far, total = run_act((3,), both(6, 8), weight, act, shown)

    feats = turned(own + other)
    total = total + x_partner(total)
    share = share_scores(near, x_partner(far), arm_embed, arm_far, [feats, total])
    up3, down3 = z_shift(share[7], 1), z_shift(share[3], -1)
    up4, down4 = z_shift(share[4], 2), z_shift(share[8], -2)
    up1, down1 = z_shift(share[5], 1), z_shift(share[1], -1)
    z_sum = lambda v, d: v + route(v, lambda z, x, y, c: (z ^ d, x, y, c))
    total = z_sum(z_sum(total, 1), 2)
    up2, down2 = join((share[6], up3, up4), (share[2], down3, down4), total)
    up2, down2 = z_shift(up2, 2), z_shift(down2, -2)
    scores = final_sum(share[0], (up1, down1, up2, down2))

    total = z_sum(total, 4)
    weight_grad, bias_grad = run_grad(
        feats, total, feedback.T, boot_weight.astype(F32), shown, act
    )
    return (
        scores[None],
        weight_grad.reshape(1, -1, h),
        bias_grad,
    )


def solution(mesh):
    inner = Mesh(mesh.devices.reshape(NZ, 2, 2, NY, 2), AXES)
    batch, member = ("z", "xl"), ("xh", "y", "c")
    placed = (
        P(batch, None),
        P(batch, member),
        P(member),
        P(member, None, batch),
        P(member, batch),
        P(None, batch),
        P(),
        P(),
        P(member, None),
    )
    return jax.shard_map(
        per_device,
        mesh=inner,
        in_specs=placed,
        out_specs=(P(member, batch, None), P(member, None, batch), P(member, batch)),
        check_vma=False,
    )
```

```python
import functools

import jax
import jax.numpy as jnp
from jax import lax
from jax.experimental import pallas as pl
from jax.experimental.pallas import tpu as pltpu
from jax.sharding import Mesh
from jax.sharding import PartitionSpec as P

AXES = ("z", "xl", "xh", "y", "c")
NZ, NX, NY = 8, 4, 4
BF, F32 = jnp.bfloat16, jnp.float32
GRAD_COST, JOIN_COST, FINAL_COST = 2**30, 2**34, 2**34
RING = (0, 1, 3, 2)
SLOT_Z = (0, -1, -2, -3, 4, 1, 2, 3)


def flat(z, x, y, c):
    z, x, y = z % NZ, x % NX, y % NY
    return (((z * 2 + x % 2) * 2 + x // 2) * NY + y) * 2 + c


def route(value, where):
    pairs = []
    for z in range(NZ):
        for x in range(NX):
            for y in range(NY):
                for c in range(2):
                    to = where(z, x, y, c)
                    if to is not None:
                        pairs.append((flat(z, x, y, c), flat(*to)))
    return lax.ppermute(value, AXES, pairs)


def other_core(value):
    return route(value, lambda z, x, y, c: (z, x, y, 1 - c))


def x_partner(value):
    return route(value, lambda z, x, y, c: (z, x ^ 1, y, c))


def along_z(value, i, core=None):
    return route(
        value,
        lambda z, x, y, c: (z + (i if c == 0 else -i), x, y, c) if core in (None, c) else None,
    )


def first_ring(value, d):
    return route(value, lambda z, x, y, c: (z, x, y ^ d, c) if c == 0 else (z, x ^ d, y, c))


def last_ring(value, d):
    return route(value, lambda z, x, y, c: (z, x ^ d, y, c) if c == 0 else (z, x, y ^ d, c))


VMEM = pl.BlockSpec(memory_space=pltpu.VMEM)
ANYWHERE = pl.BlockSpec(memory_space=pl.ANY)


def params(mib):
    return pltpu.CompilerParams(vmem_limit_bytes=mib * 2**20)


def group_row(rel, slot, group):
    z, xl = lax.axis_index("z"), lax.axis_index("xl")
    zz = lax.rem(z + SLOT_Z[slot] + NZ, NZ)
    return pl.multiple_of((zz * 2 + (xl if rel == 0 else 1 - xl)) * group, 16)


def gather_kernel(slots_ref, arm_ref, out_ref, ids_ref):
    n_slots, n_ctx, _ = out_ref.shape
    arms = arm_ref.shape[0]
    group = n_ctx // 16
    for rel in range(2):
        for slot in range(NZ):
            ids_ref[pl.ds((rel * NZ + slot) * group, group), :] = slots_ref[
                pl.ds(group_row(rel, slot, group), group), :
            ]
    rows = n_ctx // 2
    for half in range(2):
        part = pl.ds(half * rows, rows)
        for k in range(n_slots):
            hot = ids_ref[part, k : k + 1] == lax.broadcasted_iota(jnp.int32, (rows, arms), 1)
            out_ref[k, part, :] = jnp.dot(
                jnp.where(hot, F32(1.0), F32(0.0)).astype(BF),
                arm_ref[...],
                preferred_element_type=F32,
            ).astype(BF)


def gather_rows(slots, arm):
    (n_ctx, n_slots), (arms, h) = slots.shape, arm.shape
    return pl.pallas_call(
        gather_kernel,
        in_specs=[VMEM, VMEM],
        out_specs=VMEM,
        out_shape=jax.ShapeDtypeStruct((n_slots, n_ctx, h), BF),
        scratch_shapes=[pltpu.VMEM((n_ctx, n_slots), jnp.int32)],
        compiler_params=params(24),
        cost_estimate=pl.CostEstimate(
            flops=2 * n_ctx * n_slots * arms * h, bytes_accessed=2**23, transcendentals=0
        ),
        name="gather_rows",
    )(slots, arm)


def place_kernel(near_ref, far_ref, arm_ref, *refs):
    out_ref, arm_out_ref = refs[-2:]
    k = near_ref.shape[0]
    xl = lax.axis_index("xl")
    out_ref[pl.ds(pl.multiple_of(xl * k, 16), k), :] = near_ref[...]
    out_ref[pl.ds(pl.multiple_of((1 - xl) * k, 16), k), :] = far_ref[...]
    arm_out_ref[...] = arm_ref[...]


def place(near, far, arm, after):
    k, n = near.shape
    return pl.pallas_call(
        place_kernel,
        in_specs=[VMEM] * 3 + [ANYWHERE] * len(after),
        out_specs=[VMEM] * 2,
        out_shape=[jax.ShapeDtypeStruct((2 * k, n), BF), jax.ShapeDtypeStruct(arm.shape, BF)],
        compiler_params=params(16),
        cost_estimate=pl.CostEstimate(flops=0, bytes_accessed=2**22, transcendentals=0),
        name="place_weight",
    )(near, far, arm, *after)


def stack_kernel(own_ref, far_ref, g1_ref, g2_ref, g3_ref, after_ref, out_ref):
    del after_ref
    core = lax.axis_index("c")
    group = own_ref.shape[0]

    @pl.when(core == 0)
    def _():
        out_ref[:group, :] = own_ref[...]

    @pl.when(core == 1)
    def _():
        out_ref[:group, :] = far_ref[...]

    for i, ref in enumerate((g1_ref, g2_ref, g3_ref)):
        out_ref[pl.ds((i + 1) * group, group), :] = ref[...]


def stack_rows(own, far, got, after):
    group, n = own.shape
    return pl.pallas_call(
        stack_kernel,
        in_specs=[VMEM] * 5 + [ANYWHERE],
        out_specs=VMEM,
        out_shape=jax.ShapeDtypeStruct((4 * group, n), BF),
        compiler_params=params(8),
        cost_estimate=pl.CostEstimate(flops=0, bytes_accessed=16 * group * n, transcendentals=0),
        name="stack_rows",
    )(own, far, *got, after)


def trunk_kernel(c0_ref, c4_ref, c1_ref, c2_ref, c3_ref, wa_ref, wb_ref, p0, p1, p2, p3, ctx_ref):
    core = lax.axis_index("c")
    group = c0_ref.shape[0]
    n = wa_ref.shape[1]

    @pl.when(core == 0)
    def _():
        ctx_ref[:group, :] = c0_ref[...]

    @pl.when(core == 1)
    def _():
        ctx_ref[:group, :] = c4_ref[...]

    for i, ref in enumerate((c1_ref, c2_ref, c3_ref)):
        ctx_ref[pl.ds((i + 1) * group, group), :] = ref[...]
    for own, w_ref in ((True, wa_ref), (False, wb_ref)):
        where = core if own else 1 - core
        part = jnp.dot(ctx_ref[...], w_ref[...], preferred_element_type=F32)
        for i, ref in enumerate((p0, p1, p2, p3)):
            ref[:, pl.ds(pl.multiple_of(where * n, 128), n)] = part[i * group : (i + 1) * group]


def trunk(ctx, w_own, w_other):
    group, n = ctx[0].shape[0], w_own.shape[1]
    return pl.pallas_call(
        trunk_kernel,
        in_specs=[VMEM] * 7,
        out_specs=[VMEM] * 4,
        out_shape=[jax.ShapeDtypeStruct((group, 2 * n), F32)] * 4,
        scratch_shapes=[pltpu.VMEM((4 * group, ctx[0].shape[1]), BF)],
        compiler_params=params(16),
        cost_estimate=pl.CostEstimate(
            flops=8 * group * ctx[0].shape[1] * 2 * n, bytes_accessed=2**22, transcendentals=0
        ),
        name="trunk_sums",
    )(*ctx, w_own, w_other)


def find(pieces, p, q):
    at = 4 * q + p
    for ref in pieces:
        if at < ref.shape[0]:
            return ref, at
        at -= ref.shape[0]


def blocks_of(p, q, core):
    return (RING[q], RING[p]) if core == 0 else (RING[p], RING[q])


def act_kernel(qs, first, last, *refs):
    n = 2 * len(qs)
    pieces, refs = refs[:n], refs[n:]
    w_ref, start_ref = refs[:2]
    if last:
        shown_ref, act_ref, near_ref, far_ref, pick_ref, flat_ref = refs[2:]
    else:
        act_ref = refs[2]
    x_hi, y, core = lax.axis_index("xh"), lax.axis_index("y"), lax.axis_index("c")
    rows = pieces[0].shape[1]
    act_ref[...] = jnp.broadcast_to(start_ref[...], act_ref.shape)
    for half in range(2):
        of = core if half == 0 else 1 - core
        for i, q in enumerate(qs):
            for p in range(4):
                ref, at = find(pieces[half * n // 2 : (half + 1) * n // 2], p, i)
                x0, y0 = blocks_of(p, q, 0)
                x1, y1 = blocks_of(p, q, 1)
                dx, dy = jnp.where(of == 0, x0, x1), jnp.where(of == 0, y0, y1)
                cb = lax.bitwise_xor(x_hi, lax.div(dx, 2)) * NY + lax.bitwise_xor(y, dy)
                rg = lax.rem(dx, 2) * 2 + of
                part = pl.ds(pl.multiple_of(rg * rows, 16), rows)
                act_ref[part, :] += jnp.dot(ref[at], w_ref[cb], preferred_element_type=F32)
    if last:
        hid = jnp.maximum(act_ref[...], F32(0.0)).astype(BF)
        half_rows = near_ref.shape[0]
        near_ref[...] = hid[:half_rows]
        far_ref[...] = hid[half_rows:]
        wide = hid.astype(F32)
        lane = lax.broadcasted_iota(jnp.int32, (hid.shape[0], 128), 1)
        total = jnp.zeros((hid.shape[0], 128), F32)
        for k in range(8):
            one = jnp.sum(wide * shown_ref[k].astype(F32), axis=1, keepdims=True)
            total = jnp.where(lane == k, one, total)
        group = hid.shape[0] // 16
        for rel in range(2):
            for slot in range(NZ):
                at = (rel * NZ + slot) * group
                flat_ref[pl.ds(group_row(rel, slot, group), group), :] = total[at : at + group]
        pick_ref[...] = jnp.transpose(flat_ref[...])[:8]


def run_act(qs, pieces, weight, start, shown=None):
    blocks, depth, h = weight.shape
    rows = 4 * pieces[0].shape[1]
    first, last = start.shape[0] == 1, shown is not None
    shapes = [jax.ShapeDtypeStruct((rows, h), F32)]
    if last:
        shapes += [jax.ShapeDtypeStruct((rows // 2, h), BF)] * 2
        shapes += [jax.ShapeDtypeStruct((8, rows), F32)]
    args = list(pieces) + [weight, start] + ([shown] if last else [])
    return pl.pallas_call(
        functools.partial(act_kernel, qs, first, last),
        in_specs=[VMEM] * len(args),
        out_specs=[VMEM] * len(shapes),
        out_shape=shapes,
        scratch_shapes=[pltpu.VMEM((rows, 128), F32)] if last else [],
        compiler_params=params(24),
        cost_estimate=pl.CostEstimate(
            flops=2 * rows * blocks * depth * h // 4 if last else 0,
            bytes_accessed=2**22 if last else 0,
            transcendentals=0,
        ),
        name="pre_act",
    )(*args)


def cut_kernel(s_ref, t_ref, s_out, t_out, s_half, t_half):
    half = s_half.shape[0]
    s_out[...] = s_ref[...]
    t_out[...] = t_ref[...]
    s_half[...] = s_ref[:half]
    t_half[...] = t_ref[half:]


def cut(s_in, t_in):
    half = (s_in.shape[0] // 2,) + s_in.shape[1:]
    return pl.pallas_call(
        cut_kernel,
        in_specs=[VMEM] * 2,
        out_specs=[VMEM] * 4,
        out_shape=[jax.ShapeDtypeStruct(v, BF) for v in (s_in.shape, t_in.shape, half, half)],
        compiler_params=params(8),
        cost_estimate=pl.CostEstimate(flops=0, bytes_accessed=2**20, transcendentals=0),
        name="cut_halves",
    )(s_in, t_in)


def turn_kernel(*refs):
    pieces, out_ref = refs[:8], refs[8]
    core = lax.axis_index("c")
    rows, depth = pieces[0].shape[1:]

    def half_of(mine, core_of, dx, dy):
        p, q = (RING.index(dy), RING.index(dx)) if core_of == 0 else (RING.index(dx), RING.index(dy))
        return find(pieces[:4] if mine else pieces[4:], p, q)

    def run(own):
        for r in range(2):
            for dy in range(4):
                for low in range(2):
                    dx = 2 * r + low
                    (a, i), (b, j) = (half_of(of == own, of, dx, dy) for of in range(2))
                    both = jnp.concatenate([a[i], b[j]], 0)
                    out_ref[r * 4 + dy, :, pl.ds(low * 2 * rows, 2 * rows)] = jnp.transpose(both)

    @pl.when(core == 0)
    def _():
        run(0)

    @pl.when(core == 1)
    def _():
        run(1)


def turned(pieces):
    rows, depth = pieces[0].shape[1:]
    return pl.pallas_call(
        turn_kernel,
        in_specs=[VMEM] * 8,
        out_specs=VMEM,
        out_shape=jax.ShapeDtypeStruct((8, depth, 4 * rows), BF),
        compiler_params=params(8),
        cost_estimate=pl.CostEstimate(flops=0, bytes_accessed=24 * 2**20, transcendentals=0),
        name="turn_features",
    )(*pieces)


def grad_kernel(n_slots, feats_ref, sum_ref, fed_ref, boot_ref, shown_ref, act_ref, *refs):
    out_ref, bias_ref, flat_ref, slot_ref, pre_ref, stage, sems = refs
    x_hi, y = lax.axis_index("xh"), lax.axis_index("y")
    n_ctx = act_ref.shape[0]
    group = n_ctx // 16
    grad = boot_ref[...] * (jax.nn.sigmoid(sum_ref[...]) - fed_ref[...]) / F32(n_slots)
    grad = jnp.concatenate([grad, jnp.zeros((128 - n_slots, n_ctx), F32)], 0)
    flat_ref[...] = jnp.transpose(grad)
    for rel in range(2):
        for slot in range(NZ):
            slot_ref[pl.ds((rel * NZ + slot) * group, group), :] = flat_ref[
                pl.ds(group_row(rel, slot, group), group), :
            ]
    total = slot_ref[:, 0:1] * shown_ref[0].astype(F32)
    for k in range(1, n_slots):
        total += slot_ref[:, k : k + 1] * shown_ref[k].astype(F32)
    pre = jnp.where(act_ref[...] > 0, total, F32(0.0)).astype(BF)
    pre_ref[...] = pre
    bias_ref[...] = jnp.sum(pre.astype(F32), axis=0, keepdims=True)
    copies = []
    for n in range(feats_ref.shape[0]):
        slot = n % 2
        if n >= 2:
            copies[n - 2].wait()
        stage[slot] = jnp.dot(feats_ref[n], pre_ref[...], preferred_element_type=F32).astype(BF)
        cb = lax.bitwise_xor(x_hi, n // 4) * NY + lax.bitwise_xor(y, n % 4)
        copy = pltpu.make_async_copy(stage.at[slot], out_ref.at[cb], sems.at[slot])
        copy.start()
        copies.append(copy)
    for copy in copies[-2:]:
        copy.wait()


def run_grad(feats, sums, fed, boot, shown, act):
    rows, h = act.shape
    blocks, depth, _ = feats.shape
    n_slots = shown.shape[0]
    return pl.pallas_call(
        functools.partial(grad_kernel, n_slots),
        in_specs=[VMEM] * 6,
        out_specs=[ANYWHERE, VMEM],
        out_shape=[
            jax.ShapeDtypeStruct((blocks, depth, h), BF),
            jax.ShapeDtypeStruct((1, h), F32),
        ],
        scratch_shapes=[
            pltpu.VMEM((rows, 128), F32),
            pltpu.VMEM((rows, 128), F32),
            pltpu.VMEM((rows, h), BF),
            pltpu.VMEM((2, depth, h), BF),
            pltpu.SemaphoreType.DMA((2,)),
        ],
        compiler_params=params(20),
        cost_estimate=pl.CostEstimate(flops=GRAD_COST, bytes_accessed=2**20, transcendentals=0),
        name="weight_grad",
    )(feats, sums, fed, boot, shown, act)


def share_kernel(near_ref, far_ref, arm_ref, armf_ref, *refs):
    outs = refs[-9:]
    dims = (((1,), (1,)), ((), ()))
    arms = arm_ref.shape[0]
    group = near_ref.shape[0] // NZ
    step = 512
    for j in range(0, arms, step):
        part = lax.dot_general(
            near_ref[...], arm_ref[pl.ds(j, step), :], dims, preferred_element_type=F32
        ) + lax.dot_general(
            far_ref[...], armf_ref[pl.ds(j, step), :], dims, preferred_element_type=F32
        )
        for s in range(NZ):
            piece = part[s * group : (s + 1) * group]
            if s == 4:
                half = arms // 2
                out = outs[4] if j < half else outs[8]
                out[:, pl.ds(j % half, step)] = piece.astype(BF)
            else:
                outs[s][:, pl.ds(j, step)] = piece.astype(outs[s].dtype)


def share_scores(near, far, arm, arm_far, after):
    group, arms = near.shape[0] // NZ, arm.shape[0]
    kinds = [F32 if s in (0, 2, 6) else BF for s in range(NZ)]
    shapes = [jax.ShapeDtypeStruct((group, arms // 2 if s == 4 else arms), kinds[s]) for s in range(NZ)]
    shapes.append(shapes[4])
    return pl.pallas_call(
        share_kernel,
        in_specs=[VMEM] * 4 + [ANYWHERE] * len(after),
        out_specs=[VMEM] * 9,
        out_shape=shapes,
        compiler_params=params(24),
        cost_estimate=pl.CostEstimate(
            flops=4 * near.shape[0] * near.shape[1] * arms, bytes_accessed=2**22, transcendentals=0
        ),
        name="share_scores",
    )(near, far, arm, arm_far, *after)


def join_kernel(*refs):
    ins, outs = refs[:6], refs[7:]
    half = ins[2].shape[1]
    for i, out_ref in enumerate(outs):
        own_ref, near_ref, far_ref = ins[3 * i : 3 * i + 3]
        for at in range(0, 2 * half, half):
            part = pl.ds(at, half)
            total = own_ref[:, part] + near_ref[:, part].astype(F32)
            if at == i * half:
                total += far_ref[...].astype(F32)
            out_ref[:, part] = total.astype(BF)


def join(up, down, after):
    own = up[0]
    return pl.pallas_call(
        join_kernel,
        in_specs=[VMEM] * 6 + [ANYWHERE],
        out_specs=[VMEM] * 2,
        out_shape=[jax.ShapeDtypeStruct(own.shape, BF)] * 2,
        compiler_params=params(8),
        cost_estimate=pl.CostEstimate(flops=JOIN_COST, bytes_accessed=2**20, transcendentals=0),
        name="join_shares",
    )(*up, *down, after)


def final_kernel(own_ref, *refs):
    total = own_ref[...]
    for ref in refs[:-1]:
        total = total + ref[...].astype(F32)
    refs[-1][...] = total.astype(BF)


def final_sum(own, parts):
    return pl.pallas_call(
        final_kernel,
        in_specs=[VMEM] * (1 + len(parts)),
        out_specs=VMEM,
        out_shape=jax.ShapeDtypeStruct(own.shape, BF),
        compiler_params=params(8),
        cost_estimate=pl.CostEstimate(flops=FINAL_COST, bytes_accessed=2**20, transcendentals=0),
        name="sum_shares",
    )(own, *parts)


def z_shift(value, d):
    return route(value, lambda z, x, y, c: (z + d, x, y, c))


def per_device(
    contexts, trunk_weight, trunk_bias, head_weight, head_bias, arm_embed, slots, feedback, boot_weight
):
    cols = trunk_weight.shape[1]
    h = arm_embed.shape[1]
    z, c = lax.axis_index("z"), lax.axis_index("c")
    low = c == 0
    pick = lambda a, b: jnp.where(low, a, b)

    k = trunk_weight.shape[0]
    cols_for = lambda zz: lax.dynamic_slice_in_dim(contexts, ((zz + NZ) % NZ) * 2 * k, 2 * k, 1)
    side = jnp.where(low, 1, -1)
    ctx = [along_z(cols_for(z + side * i), i) for i in (1, 2, 3)]
    ctx_far = along_z(cols_for(z + 4), 4, core=1)
    ctx = [cols_for(z), ctx_far] + ctx
    w_far = x_partner(trunk_weight)
    shown = gather_rows(slots, arm_embed)
    w_own, arm_copy = place(trunk_weight, w_far, arm_embed, ctx + [shown])
    arm_far = x_partner(arm_copy)
    w_other = other_core(w_own)
    p0, p1, p2, p3 = trunk(ctx, w_own, w_other)

    third = along_z(p3, -1)
    fourth = along_z(p0, -4 + 2, core=1)
    next_one = along_z(p1, -1)
    second = along_z(p2 + third + fourth, -2)
    bias = jnp.concatenate([pick(trunk_bias, 0.0), pick(0.0, trunk_bias)])
    mine = pick(p0, 0.0) + next_one + second + bias
    feat = jnp.maximum(mine + other_core(mine), F32(0.0)).astype(BF)

    got = [along_z(feat, i) for i in (1, 2, 3)]
    far = along_z(feat, 4, core=1)
    block = stack_rows(feat, far, got, arm_far)
    block = jnp.stack([block] + [first_ring(block, d) for d in RING[1:]])
    s_in, t_in = last_ring(block, 1), last_ring(block, 3)
    blocks = NX * NY // 2
    weight = head_weight[0].reshape(blocks, 2 * cols, h)
    block_other = other_core(block)
    (act,) = run_act((0,), [block, block_other], weight, head_bias)
    s_in, t_in, s_half, t_half = cut(s_in, t_in)
    u_in = jnp.concatenate([last_ring(s_half, 3), last_ring(t_half, 1)], 0)
    own = [block, s_in, t_in, u_in]
    other = [block_other] + [other_core(v) for v in own[1:]]
    both = lambda i, j: own[i:j] + other[i:j]

    (act,) = run_act((1, 2), both(1, 3), weight, act)
    act, near, far, total = run_act((3,), both(3, 4), weight, act, shown)

    feats = turned(own + other)
    total = total + x_partner(total)
    share = share_scores(near, x_partner(far), arm_embed, arm_far, [feats, total])
    up3, down3 = z_shift(share[7], 1), z_shift(share[3], -1)
    up4, down4 = z_shift(share[4], 2), z_shift(share[8], -2)
    up1, down1 = z_shift(share[5], 1), z_shift(share[1], -1)
    z_sum = lambda v, d: v + route(v, lambda z, x, y, c: (z ^ d, x, y, c))
    total = z_sum(z_sum(z_sum(total, 1), 2), 4)
    up2, down2 = join((share[6], up3, up4), (share[2], down3, down4), total)
    up2, down2 = z_shift(up2, 2), z_shift(down2, -2)
    scores = final_sum(share[0], (up1, down1, up2, down2))

    weight_grad, bias_grad = run_grad(
        feats, total, feedback.T, boot_weight.astype(F32), shown, act
    )
    return (
        scores[None],
        weight_grad.reshape(1, -1, h),
        bias_grad,
    )


def solution(mesh):
    inner = Mesh(mesh.devices.reshape(NZ, 2, 2, NY, 2), AXES)
    batch, member = ("z", "xl"), ("xh", "y", "c")
    placed = (
        P(batch, None),
        P(batch, member),
        P(member),
        P(member, None, batch),
        P(member, batch),
        P(None, batch),
        P(),
        P(),
        P(member, None),
    )
    return jax.shard_map(
        per_device,
        mesh=inner,
        in_specs=placed,
        out_specs=(P(member, batch, None), P(member, None, batch), P(member, batch)),
        check_vma=False,
    )
```

```python
import functools

import jax
import jax.numpy as jnp
from jax import lax
from jax.experimental import pallas as pl
from jax.experimental.pallas import tpu as pltpu
from jax.sharding import Mesh
from jax.sharding import PartitionSpec as P

AXES = ("z", "xl", "xh", "y", "c")
NZ, NX, NY = 8, 4, 4
BF, F32 = jnp.bfloat16, jnp.float32
GRAD_COST, JOIN_COST, FINAL_COST = 2**30, 2**34, 2**34
RING = (0, 1, 3, 2)
SLOT_Z = (0, -1, -2, -3, 4, 1, 2, 3)


def flat(z, x, y, c):
    z, x, y = z % NZ, x % NX, y % NY
    return (((z * 2 + x % 2) * 2 + x // 2) * NY + y) * 2 + c


def route(value, where):
    pairs = []
    for z in range(NZ):
        for x in range(NX):
            for y in range(NY):
                for c in range(2):
                    to = where(z, x, y, c)
                    if to is not None:
                        pairs.append((flat(z, x, y, c), flat(*to)))
    return lax.ppermute(value, AXES, pairs)


def other_core(value):
    return route(value, lambda z, x, y, c: (z, x, y, 1 - c))


def x_partner(value):
    return route(value, lambda z, x, y, c: (z, x ^ 1, y, c))


def along_z(value, i, core=None):
    return route(
        value,
        lambda z, x, y, c: (z + (i if c == 0 else -i), x, y, c) if core in (None, c) else None,
    )


def first_ring(value, d):
    return route(value, lambda z, x, y, c: (z, x, y ^ d, c) if c == 0 else (z, x ^ d, y, c))


def last_ring(value, d):
    return route(value, lambda z, x, y, c: (z, x ^ d, y, c) if c == 0 else (z, x, y ^ d, c))


VMEM = pl.BlockSpec(memory_space=pltpu.VMEM)
ANYWHERE = pl.BlockSpec(memory_space=pl.ANY)


def params(mib):
    return pltpu.CompilerParams(vmem_limit_bytes=mib * 2**20)


def group_row(rel, slot, group):
    z, xl = lax.axis_index("z"), lax.axis_index("xl")
    zz = lax.rem(z + SLOT_Z[slot] + NZ, NZ)
    return pl.multiple_of((zz * 2 + (xl if rel == 0 else 1 - xl)) * group, 16)


def gather_kernel(slots_ref, arm_ref, out_ref, ids_ref):
    n_slots, n_ctx, _ = out_ref.shape
    arms = arm_ref.shape[0]
    group = n_ctx // 16
    for rel in range(2):
        for slot in range(NZ):
            ids_ref[pl.ds((rel * NZ + slot) * group, group), :] = slots_ref[
                pl.ds(group_row(rel, slot, group), group), :
            ]
    rows = n_ctx // 2
    for half in range(2):
        part = pl.ds(half * rows, rows)
        for k in range(n_slots):
            hot = ids_ref[part, k : k + 1] == lax.broadcasted_iota(jnp.int32, (rows, arms), 1)
            out_ref[k, part, :] = jnp.dot(
                jnp.where(hot, F32(1.0), F32(0.0)).astype(BF),
                arm_ref[...],
                preferred_element_type=F32,
            ).astype(BF)


def gather_rows(slots, arm):
    (n_ctx, n_slots), (arms, h) = slots.shape, arm.shape
    return pl.pallas_call(
        gather_kernel,
        in_specs=[VMEM, VMEM],
        out_specs=VMEM,
        out_shape=jax.ShapeDtypeStruct((n_slots, n_ctx, h), BF),
        scratch_shapes=[pltpu.VMEM((n_ctx, n_slots), jnp.int32)],
        compiler_params=params(24),
        cost_estimate=pl.CostEstimate(
            flops=2 * n_ctx * n_slots * arms * h, bytes_accessed=2**23, transcendentals=0
        ),
        name="gather_rows",
    )(slots, arm)


def place_kernel(near_ref, far_ref, arm_ref, *refs):
    out_ref, arm_out_ref = refs[-2:]
    k = near_ref.shape[0]
    xl = lax.axis_index("xl")
    out_ref[pl.ds(pl.multiple_of(xl * k, 16), k), :] = near_ref[...]
    out_ref[pl.ds(pl.multiple_of((1 - xl) * k, 16), k), :] = far_ref[...]
    arm_out_ref[...] = arm_ref[...]


def place(near, far, arm, after):
    k, n = near.shape
    return pl.pallas_call(
        place_kernel,
        in_specs=[VMEM] * 3 + [ANYWHERE] * len(after),
        out_specs=[VMEM] * 2,
        out_shape=[jax.ShapeDtypeStruct((2 * k, n), BF), jax.ShapeDtypeStruct(arm.shape, BF)],
        compiler_params=params(16),
        cost_estimate=pl.CostEstimate(flops=0, bytes_accessed=2**22, transcendentals=0),
        name="place_weight",
    )(near, far, arm, *after)


def stack_kernel(own_ref, far_ref, g1_ref, g2_ref, g3_ref, *refs):
    out_ref = refs[-1]
    core = lax.axis_index("c")
    group = own_ref.shape[0]

    @pl.when(core == 0)
    def _():
        out_ref[:group, :] = own_ref[...]

    @pl.when(core == 1)
    def _():
        out_ref[:group, :] = far_ref[...]

    for i, ref in enumerate((g1_ref, g2_ref, g3_ref)):
        out_ref[pl.ds((i + 1) * group, group), :] = ref[...]


def stack_rows(own, far, got, after):
    group, n = own.shape
    return pl.pallas_call(
        stack_kernel,
        in_specs=[VMEM] * 5 + [ANYWHERE] * len(after),
        out_specs=VMEM,
        out_shape=jax.ShapeDtypeStruct((4 * group, n), BF),
        compiler_params=params(8),
        cost_estimate=pl.CostEstimate(flops=0, bytes_accessed=16 * group * n, transcendentals=0),
        name="stack_rows",
    )(own, far, *got, *after)


def trunk_kernel(c0_ref, c4_ref, c1_ref, c2_ref, c3_ref, wa_ref, wb_ref, p0, p1, p2, p3, ctx_ref):
    core = lax.axis_index("c")
    group = c0_ref.shape[0]
    n = wa_ref.shape[1]

    @pl.when(core == 0)
    def _():
        ctx_ref[:group, :] = c0_ref[...]

    @pl.when(core == 1)
    def _():
        ctx_ref[:group, :] = c4_ref[...]

    for i, ref in enumerate((c1_ref, c2_ref, c3_ref)):
        ctx_ref[pl.ds((i + 1) * group, group), :] = ref[...]
    for own, w_ref in ((True, wa_ref), (False, wb_ref)):
        where = core if own else 1 - core
        part = jnp.dot(ctx_ref[...], w_ref[...], preferred_element_type=F32)
        for i, ref in enumerate((p0, p1, p2, p3)):
            ref[:, pl.ds(pl.multiple_of(where * n, 128), n)] = part[i * group : (i + 1) * group]


def trunk(ctx, w_own, w_other):
    group, n = ctx[0].shape[0], w_own.shape[1]
    return pl.pallas_call(
        trunk_kernel,
        in_specs=[VMEM] * 7,
        out_specs=[VMEM] * 4,
        out_shape=[jax.ShapeDtypeStruct((group, 2 * n), F32)] * 4,
        scratch_shapes=[pltpu.VMEM((4 * group, ctx[0].shape[1]), BF)],
        compiler_params=params(16),
        cost_estimate=pl.CostEstimate(
            flops=8 * group * ctx[0].shape[1] * 2 * n, bytes_accessed=2**22, transcendentals=0
        ),
        name="trunk_sums",
    )(*ctx, w_own, w_other)


def find(pieces, p, q):
    at = 4 * q + p
    for ref in pieces:
        if at < ref.shape[0]:
            return ref, at
        at -= ref.shape[0]


def blocks_of(p, q, core):
    return (RING[q], RING[p]) if core == 0 else (RING[p], RING[q])


def act_kernel(qs, first, last, *refs):
    n = 2 * len(qs)
    pieces, refs = refs[:n], refs[n:]
    w_ref, start_ref = refs[:2]
    if last:
        shown_ref, act_ref, near_ref, far_ref, pick_ref, flat_ref = refs[2:]
    else:
        act_ref = refs[2]
    x_hi, y, core = lax.axis_index("xh"), lax.axis_index("y"), lax.axis_index("c")
    rows = pieces[0].shape[1]
    act_ref[...] = jnp.broadcast_to(start_ref[...], act_ref.shape)
    for half in range(2):
        of = core if half == 0 else 1 - core
        for i, q in enumerate(qs):
            for p in range(4):
                ref, at = find(pieces[half * n // 2 : (half + 1) * n // 2], p, i)
                x0, y0 = blocks_of(p, q, 0)
                x1, y1 = blocks_of(p, q, 1)
                dx, dy = jnp.where(of == 0, x0, x1), jnp.where(of == 0, y0, y1)
                cb = lax.bitwise_xor(x_hi, lax.div(dx, 2)) * NY + lax.bitwise_xor(y, dy)
                rg = lax.rem(dx, 2) * 2 + of
                part = pl.ds(pl.multiple_of(rg * rows, 16), rows)
                act_ref[part, :] += jnp.dot(ref[at], w_ref[cb], preferred_element_type=F32)
    if last:
        hid = jnp.maximum(act_ref[...], F32(0.0)).astype(BF)
        half_rows = near_ref.shape[0]
        near_ref[...] = hid[:half_rows]
        far_ref[...] = hid[half_rows:]
        wide = hid.astype(F32)
        lane = lax.broadcasted_iota(jnp.int32, (hid.shape[0], 128), 1)
        total = jnp.zeros((hid.shape[0], 128), F32)
        for k in range(8):
            one = jnp.sum(wide * shown_ref[k].astype(F32), axis=1, keepdims=True)
            total = jnp.where(lane == k, one, total)
        group = hid.shape[0] // 16
        for rel in range(2):
            for slot in range(NZ):
                at = (rel * NZ + slot) * group
                flat_ref[pl.ds(group_row(rel, slot, group), group), :] = total[at : at + group]
        pick_ref[...] = jnp.transpose(flat_ref[...])[:8]


def run_act(qs, pieces, weight, start, shown=None):
    blocks, depth, h = weight.shape
    rows = 4 * pieces[0].shape[1]
    first, last = start.shape[0] == 1, shown is not None
    shapes = [jax.ShapeDtypeStruct((rows, h), F32)]
    if last:
        shapes += [jax.ShapeDtypeStruct((rows // 2, h), BF)] * 2
        shapes += [jax.ShapeDtypeStruct((8, rows), F32)]
    args = list(pieces) + [weight, start] + ([shown] if last else [])
    return pl.pallas_call(
        functools.partial(act_kernel, qs, first, last),
        in_specs=[VMEM] * len(args),
        out_specs=[VMEM] * len(shapes),
        out_shape=shapes,
        scratch_shapes=[pltpu.VMEM((rows, 128), F32)] if last else [],
        compiler_params=params(24),
        cost_estimate=pl.CostEstimate(
            flops=2 * rows * blocks * depth * h // 4 if last else 0,
            bytes_accessed=2**22 if last else 0,
            transcendentals=0,
        ),
        name="pre_act",
    )(*args)


def cut_kernel(s_ref, t_ref, s_out, t_out, s_half, t_half):
    half = s_half.shape[0]
    s_out[...] = s_ref[...]
    t_out[...] = t_ref[...]
    s_half[...] = s_ref[:half]
    t_half[...] = t_ref[half:]


def cut(s_in, t_in):
    half = (s_in.shape[0] // 2,) + s_in.shape[1:]
    return pl.pallas_call(
        cut_kernel,
        in_specs=[VMEM] * 2,
        out_specs=[VMEM] * 4,
        out_shape=[jax.ShapeDtypeStruct(v, BF) for v in (s_in.shape, t_in.shape, half, half)],
        compiler_params=params(8),
        cost_estimate=pl.CostEstimate(flops=0, bytes_accessed=2**20, transcendentals=0),
        name="cut_halves",
    )(s_in, t_in)


def turn_kernel(*refs):
    pieces, out_ref = refs[:8], refs[8]
    core = lax.axis_index("c")
    rows, depth = pieces[0].shape[1:]

    def half_of(mine, core_of, dx, dy):
        p, q = (RING.index(dy), RING.index(dx)) if core_of == 0 else (RING.index(dx), RING.index(dy))
        return find(pieces[:4] if mine else pieces[4:], p, q)

    def run(own):
        for r in range(2):
            for dy in range(4):
                for low in range(2):
                    dx = 2 * r + low
                    (a, i), (b, j) = (half_of(of == own, of, dx, dy) for of in range(2))
                    both = jnp.concatenate([a[i], b[j]], 0)
                    out_ref[r * 4 + dy, :, pl.ds(low * 2 * rows, 2 * rows)] = jnp.transpose(both)

    @pl.when(core == 0)
    def _():
        run(0)

    @pl.when(core == 1)
    def _():
        run(1)


def turned(pieces):
    rows, depth = pieces[0].shape[1:]
    return pl.pallas_call(
        turn_kernel,
        in_specs=[VMEM] * 8,
        out_specs=VMEM,
        out_shape=jax.ShapeDtypeStruct((8, depth, 4 * rows), BF),
        compiler_params=params(8),
        cost_estimate=pl.CostEstimate(flops=0, bytes_accessed=24 * 2**20, transcendentals=0),
        name="turn_features",
    )(*pieces)


def grad_kernel(n_slots, feats_ref, sum_ref, fed_ref, boot_ref, shown_ref, act_ref, *refs):
    out_ref, bias_ref, flat_ref, slot_ref, pre_ref, stage, sems = refs
    x_hi, y = lax.axis_index("xh"), lax.axis_index("y")
    n_ctx = act_ref.shape[0]
    group = n_ctx // 16
    grad = boot_ref[...] * (jax.nn.sigmoid(sum_ref[...]) - fed_ref[...]) / F32(n_slots)
    grad = jnp.concatenate([grad, jnp.zeros((128 - n_slots, n_ctx), F32)], 0)
    flat_ref[...] = jnp.transpose(grad)
    for rel in range(2):
        for slot in range(NZ):
            slot_ref[pl.ds((rel * NZ + slot) * group, group), :] = flat_ref[
                pl.ds(group_row(rel, slot, group), group), :
            ]
    total = slot_ref[:, 0:1] * shown_ref[0].astype(F32)
    for k in range(1, n_slots):
        total += slot_ref[:, k : k + 1] * shown_ref[k].astype(F32)
    pre = jnp.where(act_ref[...] > 0, total, F32(0.0)).astype(BF)
    pre_ref[...] = pre
    bias_ref[...] = jnp.sum(pre.astype(F32), axis=0, keepdims=True)
    copies = []
    step = stage.shape[1] // 4
    for n in range(feats_ref.shape[0]):
        cb = lax.bitwise_xor(x_hi, n // 4) * NY + lax.bitwise_xor(y, n % 4)
        for i in range(4):
            part = pl.ds(i * step, step)
            stage[n, part, :] = jnp.dot(
                feats_ref[n, part, :], pre_ref[...], preferred_element_type=F32
            ).astype(BF)
            copy = pltpu.make_async_copy(
                stage.at[n, part, :], out_ref.at[cb, part, :], sems.at[n, i]
            )
            copy.start()
            copies.append(copy)
    for copy in copies:
        copy.wait()


def run_grad(feats, sums, fed, boot, shown, act):
    rows, h = act.shape
    blocks, depth, _ = feats.shape
    n_slots = shown.shape[0]
    return pl.pallas_call(
        functools.partial(grad_kernel, n_slots),
        in_specs=[VMEM] * 6,
        out_specs=[ANYWHERE, VMEM],
        out_shape=[
            jax.ShapeDtypeStruct((blocks, depth, h), BF),
            jax.ShapeDtypeStruct((1, h), F32),
        ],
        scratch_shapes=[
            pltpu.VMEM((rows, 128), F32),
            pltpu.VMEM((rows, 128), F32),
            pltpu.VMEM((rows, h), BF),
            pltpu.VMEM((blocks, depth, h), BF),
            pltpu.SemaphoreType.DMA((blocks, 4)),
        ],
        compiler_params=params(20),
        cost_estimate=pl.CostEstimate(flops=GRAD_COST, bytes_accessed=2**20, transcendentals=0),
        name="weight_grad",
    )(feats, sums, fed, boot, shown, act)


def share_kernel(near_ref, far_ref, arm_ref, armf_ref, sums_ref, *outs):
    outs[-1][...] = sums_ref[...]
    dims = (((1,), (1,)), ((), ()))
    arms = arm_ref.shape[0]
    group = near_ref.shape[0] // NZ
    step = 512
    for j in range(0, arms, step):
        part = lax.dot_general(
            near_ref[...], arm_ref[pl.ds(j, step), :], dims, preferred_element_type=F32
        ) + lax.dot_general(
            far_ref[...], armf_ref[pl.ds(j, step), :], dims, preferred_element_type=F32
        )
        for s in range(NZ):
            piece = part[s * group : (s + 1) * group]
            if s == 4:
                half = arms // 2
                out = outs[4] if j < half else outs[8]
                out[:, pl.ds(j % half, step)] = piece.astype(BF)
            else:
                outs[s][:, pl.ds(j, step)] = piece.astype(outs[s].dtype)


def share_scores(near, far, arm, arm_far, sums):
    group, arms = near.shape[0] // NZ, arm.shape[0]
    kinds = [F32 if s in (0, 2, 6) else BF for s in range(NZ)]
    shapes = [jax.ShapeDtypeStruct((group, arms // 2 if s == 4 else arms), kinds[s]) for s in range(NZ)]
    shapes += [shapes[4], jax.ShapeDtypeStruct(sums.shape, F32)]
    return pl.pallas_call(
        share_kernel,
        in_specs=[VMEM] * 5,
        out_specs=[VMEM] * 10,
        out_shape=shapes,
        compiler_params=params(24),
        cost_estimate=pl.CostEstimate(
            flops=4 * near.shape[0] * near.shape[1] * arms, bytes_accessed=2**22, transcendentals=0
        ),
        name="share_scores",
    )(near, far, arm, arm_far, sums)


def join_kernel(*refs):
    ins, outs = refs[:6], refs[-2:]
    half = ins[2].shape[1]
    for i, out_ref in enumerate(outs):
        own_ref, near_ref, far_ref = ins[3 * i : 3 * i + 3]
        for at in range(0, 2 * half, half):
            part = pl.ds(at, half)
            total = own_ref[:, part] + near_ref[:, part].astype(F32)
            if at == i * half:
                total += far_ref[...].astype(F32)
            out_ref[:, part] = total.astype(BF)


def join(up, down, after):
    own = up[0]
    return pl.pallas_call(
        join_kernel,
        in_specs=[VMEM] * 6 + [ANYWHERE] * len(after),
        out_specs=[VMEM] * 2,
        out_shape=[jax.ShapeDtypeStruct(own.shape, BF)] * 2,
        compiler_params=params(8),
        cost_estimate=pl.CostEstimate(flops=JOIN_COST, bytes_accessed=2**20, transcendentals=0),
        name="join_shares",
    )(*up, *down, *after)


def final_kernel(own_ref, *refs):
    total = own_ref[...]
    for ref in refs[:-1]:
        total = total + ref[...].astype(F32)
    refs[-1][...] = total.astype(BF)


def final_sum(own, parts):
    return pl.pallas_call(
        final_kernel,
        in_specs=[VMEM] * (1 + len(parts)),
        out_specs=VMEM,
        out_shape=jax.ShapeDtypeStruct(own.shape, BF),
        compiler_params=params(8),
        cost_estimate=pl.CostEstimate(flops=FINAL_COST, bytes_accessed=2**20, transcendentals=0),
        name="sum_shares",
    )(own, *parts)


def z_shift(value, d):
    return route(value, lambda z, x, y, c: (z + d, x, y, c))


def per_device(
    contexts, trunk_weight, trunk_bias, head_weight, head_bias, arm_embed, slots, feedback, boot_weight
):
    cols = trunk_weight.shape[1]
    h = arm_embed.shape[1]
    z, c = lax.axis_index("z"), lax.axis_index("c")
    low = c == 0
    pick = lambda a, b: jnp.where(low, a, b)

    k = trunk_weight.shape[0]
    cols_for = lambda zz: lax.dynamic_slice_in_dim(contexts, ((zz + NZ) % NZ) * 2 * k, 2 * k, 1)
    side = jnp.where(low, 1, -1)
    ctx = [along_z(cols_for(z + side * i), i) for i in (1, 2, 3)]
    ctx_far = along_z(cols_for(z + 4), 4, core=1)
    ctx = [cols_for(z), ctx_far] + ctx
    w_far = x_partner(trunk_weight)
    shown = gather_rows(slots, arm_embed)
    w_own, arm_copy = place(trunk_weight, w_far, arm_embed, ctx)
    arm_far = x_partner(arm_copy)
    w_other = other_core(w_own)
    p0, p1, p2, p3 = trunk(ctx, w_own, w_other)

    third = along_z(p3, -1)
    fourth = along_z(p0, -4 + 2, core=1)
    next_one = along_z(p1, -1)
    second = along_z(p2 + third + fourth, -2)
    bias = jnp.concatenate([pick(trunk_bias, 0.0), pick(0.0, trunk_bias)])
    mine = pick(p0, 0.0) + next_one + second + bias
    feat = jnp.maximum(mine + other_core(mine), F32(0.0)).astype(BF)

    got = [along_z(feat, i) for i in (1, 2, 3)]
    far = along_z(feat, 4, core=1)
    block = stack_rows(feat, far, got, [arm_far, shown])
    block = jnp.stack([block] + [first_ring(block, d) for d in RING[1:]])
    s_in, t_in = last_ring(block, 1), last_ring(block, 3)
    blocks = NX * NY // 2
    weight = head_weight[0].reshape(blocks, 2 * cols, h)
    block_other = other_core(block)
    (act,) = run_act((0,), [block, block_other], weight, head_bias)
    s_in, t_in, s_half, t_half = cut(s_in, t_in)
    u_in = jnp.concatenate([last_ring(s_half, 3), last_ring(t_half, 1)], 0)
    own = [block, s_in, t_in, u_in]
    other = [block_other] + [other_core(v) for v in own[1:]]
    both = lambda i, j: own[i:j] + other[i:j]

    (act,) = run_act((1, 2), both(1, 3), weight, act)
    act, near, far, total = run_act((3,), both(3, 4), weight, act, shown)

    z_sum = lambda v, d: v + route(v, lambda z, x, y, c: (z ^ d, x, y, c))
    total = z_sum(total + x_partner(total), 1)
    share = share_scores(near, x_partner(far), arm_embed, arm_far, total)
    up3, down3 = z_shift(share[7], 1), z_shift(share[3], -1)
    up4, down4 = z_shift(share[4], 2), z_shift(share[8], -2)
    up1, down1 = z_shift(share[5], 1), z_shift(share[1], -1)
    total = z_sum(z_sum(share[9], 2), 4)
    feats = turned(own + other)
    up2, down2 = join(
        (share[6], up3, up4), (share[2], down3, down4), [total, feats]
    )
    up2, down2 = z_shift(up2, 2), z_shift(down2, -2)
    scores = final_sum(share[0], (up1, down1, up2, down2))

    weight_grad, bias_grad = run_grad(
        feats, total, feedback.T, boot_weight.astype(F32), shown, act
    )
    return (
        scores[None],
        weight_grad.reshape(1, -1, h),
        bias_grad,
    )


def solution(mesh):
    inner = Mesh(mesh.devices.reshape(NZ, 2, 2, NY, 2), AXES)
    batch, member = ("z", "xl"), ("xh", "y", "c")
    placed = (
        P(batch, None),
        P(batch, member),
        P(member),
        P(member, None, batch),
        P(member, batch),
        P(None, batch),
        P(),
        P(),
        P(member, None),
    )
    return jax.shard_map(
        per_device,
        mesh=inner,
        in_specs=placed,
        out_specs=(P(member, batch, None), P(member, None, batch), P(member, batch)),
        check_vma=False,
    )
```

```python
import functools

import jax
import jax.numpy as jnp
from jax import lax
from jax.experimental import pallas as pl
from jax.experimental.pallas import tpu as pltpu
from jax.sharding import Mesh
from jax.sharding import PartitionSpec as P

AXES = ("z", "xl", "xh", "y", "c")
NZ, NX, NY = 8, 4, 4
BF, F32 = jnp.bfloat16, jnp.float32
GRAD_COST, JOIN_COST, FINAL_COST = 2**30, 2**34, 2**34
RING = (0, 1, 3, 2)
SLOT_Z = (0, -1, -2, -3, 4, 1, 2, 3)


def flat(z, x, y, c):
    z, x, y = z % NZ, x % NX, y % NY
    return (((z * 2 + x % 2) * 2 + x // 2) * NY + y) * 2 + c


def route(value, where):
    pairs = []
    for z in range(NZ):
        for x in range(NX):
            for y in range(NY):
                for c in range(2):
                    to = where(z, x, y, c)
                    if to is not None:
                        pairs.append((flat(z, x, y, c), flat(*to)))
    return lax.ppermute(value, AXES, pairs)


def other_core(value):
    return route(value, lambda z, x, y, c: (z, x, y, 1 - c))


def x_partner(value):
    return route(value, lambda z, x, y, c: (z, x ^ 1, y, c))


def along_z(value, i, core=None):
    return route(
        value,
        lambda z, x, y, c: (z + (i if c == 0 else -i), x, y, c) if core in (None, c) else None,
    )


def first_ring(value, d):
    return route(value, lambda z, x, y, c: (z, x, y ^ d, c) if c == 0 else (z, x ^ d, y, c))


def last_ring(value, d):
    return route(value, lambda z, x, y, c: (z, x ^ d, y, c) if c == 0 else (z, x, y ^ d, c))


VMEM = pl.BlockSpec(memory_space=pltpu.VMEM)
ANYWHERE = pl.BlockSpec(memory_space=pl.ANY)


def params(mib):
    return pltpu.CompilerParams(vmem_limit_bytes=mib * 2**20)


def group_row(rel, slot, group):
    z, xl = lax.axis_index("z"), lax.axis_index("xl")
    zz = lax.rem(z + SLOT_Z[slot] + NZ, NZ)
    return pl.multiple_of((zz * 2 + (xl if rel == 0 else 1 - xl)) * group, 16)


def gather_kernel(slots_ref, arm_ref, out_ref, ids_ref):
    n_slots, n_ctx, _ = out_ref.shape
    arms = arm_ref.shape[0]
    group = n_ctx // 16
    for rel in range(2):
        for slot in range(NZ):
            ids_ref[pl.ds((rel * NZ + slot) * group, group), :] = slots_ref[
                pl.ds(group_row(rel, slot, group), group), :
            ]
    rows = n_ctx // 2
    for half in range(2):
        part = pl.ds(half * rows, rows)
        for k in range(n_slots):
            hot = ids_ref[part, k : k + 1] == lax.broadcasted_iota(jnp.int32, (rows, arms), 1)
            out_ref[k, part, :] = jnp.dot(
                jnp.where(hot, F32(1.0), F32(0.0)).astype(BF),
                arm_ref[...],
                preferred_element_type=F32,
            ).astype(BF)


def gather_rows(slots, arm):
    (n_ctx, n_slots), (arms, h) = slots.shape, arm.shape
    return pl.pallas_call(
        gather_kernel,
        in_specs=[VMEM, VMEM],
        out_specs=VMEM,
        out_shape=jax.ShapeDtypeStruct((n_slots, n_ctx, h), BF),
        scratch_shapes=[pltpu.VMEM((n_ctx, n_slots), jnp.int32)],
        compiler_params=params(24),
        cost_estimate=pl.CostEstimate(
            flops=2 * n_ctx * n_slots * arms * h, bytes_accessed=2**23, transcendentals=0
        ),
        name="gather_rows",
    )(slots, arm)


def place_kernel(near_ref, far_ref, arm_ref, *refs):
    out_ref, arm_out_ref = refs[-2:]
    k = near_ref.shape[0]
    xl = lax.axis_index("xl")
    out_ref[pl.ds(pl.multiple_of(xl * k, 16), k), :] = near_ref[...]
    out_ref[pl.ds(pl.multiple_of((1 - xl) * k, 16), k), :] = far_ref[...]
    arm_out_ref[...] = arm_ref[...]


def place(near, far, arm, after):
    k, n = near.shape
    return pl.pallas_call(
        place_kernel,
        in_specs=[VMEM] * 3 + [ANYWHERE] * len(after),
        out_specs=[VMEM] * 2,
        out_shape=[jax.ShapeDtypeStruct((2 * k, n), BF), jax.ShapeDtypeStruct(arm.shape, BF)],
        compiler_params=params(16),
        cost_estimate=pl.CostEstimate(flops=0, bytes_accessed=2**22, transcendentals=0),
        name="place_weight",
    )(near, far, arm, *after)


def stack_kernel(own_ref, far_ref, g1_ref, g2_ref, g3_ref, *refs):
    out_ref = refs[-1]
    core = lax.axis_index("c")
    group = own_ref.shape[0]

    @pl.when(core == 0)
    def _():
        out_ref[:group, :] = own_ref[...]

    @pl.when(core == 1)
    def _():
        out_ref[:group, :] = far_ref[...]

    for i, ref in enumerate((g1_ref, g2_ref, g3_ref)):
        out_ref[pl.ds((i + 1) * group, group), :] = ref[...]


def stack_rows(own, far, got, after):
    group, n = own.shape
    return pl.pallas_call(
        stack_kernel,
        in_specs=[VMEM] * 5 + [ANYWHERE] * len(after),
        out_specs=VMEM,
        out_shape=jax.ShapeDtypeStruct((4 * group, n), BF),
        compiler_params=params(8),
        cost_estimate=pl.CostEstimate(flops=0, bytes_accessed=16 * group * n, transcendentals=0),
        name="stack_rows",
    )(own, far, *got, *after)


def trunk_kernel(c0_ref, c4_ref, c1_ref, c2_ref, c3_ref, wa_ref, wb_ref, p0, p1, p2, p3, ctx_ref):
    core = lax.axis_index("c")
    group = c0_ref.shape[0]
    n = wa_ref.shape[1]

    @pl.when(core == 0)
    def _():
        ctx_ref[:group, :] = c0_ref[...]

    @pl.when(core == 1)
    def _():
        ctx_ref[:group, :] = c4_ref[...]

    for i, ref in enumerate((c1_ref, c2_ref, c3_ref)):
        ctx_ref[pl.ds((i + 1) * group, group), :] = ref[...]
    for own, w_ref in ((True, wa_ref), (False, wb_ref)):
        where = core if own else 1 - core
        part = jnp.dot(ctx_ref[...], w_ref[...], preferred_element_type=F32)
        for i, ref in enumerate((p0, p1, p2, p3)):
            ref[:, pl.ds(pl.multiple_of(where * n, 128), n)] = part[i * group : (i + 1) * group]


def trunk(ctx, w_own, w_other):
    group, n = ctx[0].shape[0], w_own.shape[1]
    return pl.pallas_call(
        trunk_kernel,
        in_specs=[VMEM] * 7,
        out_specs=[VMEM] * 4,
        out_shape=[jax.ShapeDtypeStruct((group, 2 * n), F32)] * 4,
        scratch_shapes=[pltpu.VMEM((4 * group, ctx[0].shape[1]), BF)],
        compiler_params=params(16),
        cost_estimate=pl.CostEstimate(
            flops=8 * group * ctx[0].shape[1] * 2 * n, bytes_accessed=2**22, transcendentals=0
        ),
        name="trunk_sums",
    )(*ctx, w_own, w_other)


def find(pieces, p, q):
    at = 4 * q + p
    for ref in pieces:
        if at < ref.shape[0]:
            return ref, at
        at -= ref.shape[0]


def blocks_of(p, q, core):
    return (RING[q], RING[p]) if core == 0 else (RING[p], RING[q])


def act_kernel(qs, first, last, *refs):
    n = 2 * len(qs)
    pieces, refs = refs[:n], refs[n:]
    w_ref, start_ref = refs[:2]
    if last:
        shown_ref, act_ref, near_ref, far_ref, pick_ref, flat_ref = refs[2:]
    else:
        act_ref = refs[2]
    x_hi, y, core = lax.axis_index("xh"), lax.axis_index("y"), lax.axis_index("c")
    rows = pieces[0].shape[1]
    act_ref[...] = jnp.broadcast_to(start_ref[...], act_ref.shape)
    for half in range(2):
        of = core if half == 0 else 1 - core
        for i, q in enumerate(qs):
            for p in range(4):
                ref, at = find(pieces[half * n // 2 : (half + 1) * n // 2], p, i)
                x0, y0 = blocks_of(p, q, 0)
                x1, y1 = blocks_of(p, q, 1)
                dx, dy = jnp.where(of == 0, x0, x1), jnp.where(of == 0, y0, y1)
                cb = lax.bitwise_xor(x_hi, lax.div(dx, 2)) * NY + lax.bitwise_xor(y, dy)
                rg = lax.rem(dx, 2) * 2 + of
                part = pl.ds(pl.multiple_of(rg * rows, 16), rows)
                act_ref[part, :] += jnp.dot(ref[at], w_ref[cb], preferred_element_type=F32)
    if last:
        hid = jnp.maximum(act_ref[...], F32(0.0)).astype(BF)
        half_rows = near_ref.shape[0]
        near_ref[...] = hid[:half_rows]
        far_ref[...] = hid[half_rows:]
        wide = hid.astype(F32)
        lane = lax.broadcasted_iota(jnp.int32, (hid.shape[0], 128), 1)
        total = jnp.zeros((hid.shape[0], 128), F32)
        for k in range(8):
            one = jnp.sum(wide * shown_ref[k].astype(F32), axis=1, keepdims=True)
            total = jnp.where(lane == k, one, total)
        group = hid.shape[0] // 16
        for rel in range(2):
            for slot in range(NZ):
                at = (rel * NZ + slot) * group
                flat_ref[pl.ds(group_row(rel, slot, group), group), :] = total[at : at + group]
        pick_ref[...] = jnp.transpose(flat_ref[...])[:8]


def run_act(qs, pieces, weight, start, shown=None):
    blocks, depth, h = weight.shape
    rows = 4 * pieces[0].shape[1]
    first, last = start.shape[0] == 1, shown is not None
    shapes = [jax.ShapeDtypeStruct((rows, h), F32)]
    if last:
        shapes += [jax.ShapeDtypeStruct((rows // 2, h), BF)] * 2
        shapes += [jax.ShapeDtypeStruct((8, rows), F32)]
    args = list(pieces) + [weight, start] + ([shown] if last else [])
    return pl.pallas_call(
        functools.partial(act_kernel, qs, first, last),
        in_specs=[VMEM] * len(args),
        out_specs=[VMEM] * len(shapes),
        out_shape=shapes,
        scratch_shapes=[pltpu.VMEM((rows, 128), F32)] if last else [],
        compiler_params=params(24),
        cost_estimate=pl.CostEstimate(
            flops=2 * rows * blocks * depth * h // 4 if last else 0,
            bytes_accessed=2**22 if last else 0,
            transcendentals=0,
        ),
        name="pre_act",
    )(*args)


def cut_kernel(s_ref, t_ref, s_out, t_out, s_half, t_half):
    half = s_half.shape[0]
    s_out[...] = s_ref[...]
    t_out[...] = t_ref[...]
    s_half[...] = s_ref[:half]
    t_half[...] = t_ref[half:]


def cut(s_in, t_in):
    half = (s_in.shape[0] // 2,) + s_in.shape[1:]
    return pl.pallas_call(
        cut_kernel,
        in_specs=[VMEM] * 2,
        out_specs=[VMEM] * 4,
        out_shape=[jax.ShapeDtypeStruct(v, BF) for v in (s_in.shape, t_in.shape, half, half)],
        compiler_params=params(8),
        cost_estimate=pl.CostEstimate(flops=0, bytes_accessed=2**20, transcendentals=0),
        name="cut_halves",
    )(s_in, t_in)


def turn_kernel(*refs):
    pieces, out_ref = refs[:8], refs[-1]
    core = lax.axis_index("c")
    rows, depth = pieces[0].shape[1:]

    def half_of(mine, core_of, dx, dy):
        p, q = (RING.index(dy), RING.index(dx)) if core_of == 0 else (RING.index(dx), RING.index(dy))
        return find(pieces[:4] if mine else pieces[4:], p, q)

    def run(own):
        for r in range(2):
            for dy in range(4):
                for low in range(2):
                    dx = 2 * r + low
                    (a, i), (b, j) = (half_of(of == own, of, dx, dy) for of in range(2))
                    both = jnp.concatenate([a[i], b[j]], 0)
                    out_ref[r * 4 + dy, :, pl.ds(low * 2 * rows, 2 * rows)] = jnp.transpose(both)

    @pl.when(core == 0)
    def _():
        run(0)

    @pl.when(core == 1)
    def _():
        run(1)


def turned(pieces, after):
    rows, depth = pieces[0].shape[1:]
    return pl.pallas_call(
        turn_kernel,
        in_specs=[VMEM] * 8 + [ANYWHERE],
        out_specs=VMEM,
        out_shape=jax.ShapeDtypeStruct((8, depth, 4 * rows), BF),
        compiler_params=params(8),
        cost_estimate=pl.CostEstimate(flops=0, bytes_accessed=24 * 2**20, transcendentals=0),
        name="turn_features",
    )(*pieces, after)


def grad_kernel(n_slots, feats_ref, sum_ref, fed_ref, boot_ref, shown_ref, act_ref, *refs):
    out_ref, bias_ref, flat_ref, slot_ref, pre_ref, stage, sems = refs
    x_hi, y = lax.axis_index("xh"), lax.axis_index("y")
    n_ctx = act_ref.shape[0]
    group = n_ctx // 16
    grad = boot_ref[...] * (jax.nn.sigmoid(sum_ref[...]) - fed_ref[...]) / F32(n_slots)
    grad = jnp.concatenate([grad, jnp.zeros((128 - n_slots, n_ctx), F32)], 0)
    flat_ref[...] = jnp.transpose(grad)
    for rel in range(2):
        for slot in range(NZ):
            slot_ref[pl.ds((rel * NZ + slot) * group, group), :] = flat_ref[
                pl.ds(group_row(rel, slot, group), group), :
            ]
    total = slot_ref[:, 0:1] * shown_ref[0].astype(F32)
    for k in range(1, n_slots):
        total += slot_ref[:, k : k + 1] * shown_ref[k].astype(F32)
    pre = jnp.where(act_ref[...] > 0, total, F32(0.0)).astype(BF)
    pre_ref[...] = pre
    bias_ref[...] = jnp.sum(pre.astype(F32), axis=0, keepdims=True)
    copies = []
    step = stage.shape[1] // 4
    for n in range(feats_ref.shape[0]):
        cb = lax.bitwise_xor(x_hi, n // 4) * NY + lax.bitwise_xor(y, n % 4)
        for i in range(4):
            part = pl.ds(i * step, step)
            stage[n, part, :] = jnp.dot(
                feats_ref[n, part, :], pre_ref[...], preferred_element_type=F32
            ).astype(BF)
            copy = pltpu.make_async_copy(
                stage.at[n, part, :], out_ref.at[cb, part, :], sems.at[n, i]
            )
            copy.start()
            copies.append(copy)
    for copy in copies:
        copy.wait()


def run_grad(feats, sums, fed, boot, shown, act):
    rows, h = act.shape
    blocks, depth, _ = feats.shape
    n_slots = shown.shape[0]
    return pl.pallas_call(
        functools.partial(grad_kernel, n_slots),
        in_specs=[VMEM] * 6,
        out_specs=[ANYWHERE, VMEM],
        out_shape=[
            jax.ShapeDtypeStruct((blocks, depth, h), BF),
            jax.ShapeDtypeStruct((1, h), F32),
        ],
        scratch_shapes=[
            pltpu.VMEM((rows, 128), F32),
            pltpu.VMEM((rows, 128), F32),
            pltpu.VMEM((rows, h), BF),
            pltpu.VMEM((blocks, depth, h), BF),
            pltpu.SemaphoreType.DMA((blocks, 4)),
        ],
        compiler_params=params(20),
        cost_estimate=pl.CostEstimate(flops=GRAD_COST, bytes_accessed=2**20, transcendentals=0),
        name="weight_grad",
    )(feats, sums, fed, boot, shown, act)


def share_kernel(near_ref, far_ref, arm_ref, armf_ref, sums_ref, own, up2, down2, up, down, up4, down4, sums_out):
    sums_out[...] = sums_ref[...]
    dims = (((1,), (1,)), ((), ()))
    arms = arm_ref.shape[0]
    group = near_ref.shape[0] // NZ
    step = 512
    half = arms // 2
    for j in range(0, arms, step):
        part = lax.dot_general(
            near_ref[...], arm_ref[pl.ds(j, step), :], dims, preferred_element_type=F32
        ) + lax.dot_general(
            far_ref[...], armf_ref[pl.ds(j, step), :], dims, preferred_element_type=F32
        )
        at = pl.ds(j, step)
        for s in range(NZ):
            piece = part[s * group : (s + 1) * group]
            d = SLOT_Z[s]
            if d in (0, 2, -2):
                {0: own, 2: up2, -2: down2}[d][:, at] = piece
            elif d == 4:
                (up4 if j < half else down4)[:, pl.ds(j % half, step)] = piece.astype(BF)
            else:
                (up if d > 0 else down)[abs(d) // 2, :, at] = piece.astype(BF)


def share_scores(near, far, arm, arm_far, sums):
    group, arms = near.shape[0] // NZ, arm.shape[0]
    whole = jax.ShapeDtypeStruct((group, arms), F32)
    pair = jax.ShapeDtypeStruct((2, group, arms), BF)
    half = jax.ShapeDtypeStruct((group, arms // 2), BF)
    shapes = [whole] * 3 + [pair] * 2 + [half] * 2 + [jax.ShapeDtypeStruct(sums.shape, F32)]
    return pl.pallas_call(
        share_kernel,
        in_specs=[VMEM] * 5,
        out_specs=[VMEM] * 8,
        out_shape=shapes,
        compiler_params=params(24),
        cost_estimate=pl.CostEstimate(
            flops=4 * near.shape[0] * near.shape[1] * arms, bytes_accessed=2**22, transcendentals=0
        ),
        name="share_scores",
    )(near, far, arm, arm_far, sums)


def join_kernel(*refs):
    ins, outs = refs[:6], refs[-2:]
    half = ins[2].shape[1]
    for i, out_ref in enumerate(outs):
        own_ref, near_ref, far_ref = ins[3 * i : 3 * i + 3]
        for at in range(0, 2 * half, half):
            part = pl.ds(at, half)
            total = own_ref[:, part] + near_ref[1, :, part].astype(F32)
            if at == i * half:
                total += far_ref[...].astype(F32)
            out_ref[:, part] = total.astype(BF)


def join(up, down, after):
    own = up[0]
    return pl.pallas_call(
        join_kernel,
        in_specs=[VMEM] * 6 + [ANYWHERE] * len(after),
        out_specs=[VMEM] * 2,
        out_shape=[jax.ShapeDtypeStruct(own.shape, BF)] * 2,
        compiler_params=params(8),
        cost_estimate=pl.CostEstimate(flops=JOIN_COST, bytes_accessed=2**20, transcendentals=0),
        name="join_shares",
    )(*up, *down, *after)


def final_kernel(own_ref, up_ref, down_ref, up2_ref, down2_ref, out_ref):
    total = own_ref[...] + up_ref[0].astype(F32) + down_ref[0].astype(F32)
    out_ref[...] = (total + up2_ref[...].astype(F32) + down2_ref[...].astype(F32)).astype(BF)


def final_sum(own, *parts):
    return pl.pallas_call(
        final_kernel,
        in_specs=[VMEM] * 5,
        out_specs=VMEM,
        out_shape=jax.ShapeDtypeStruct(own.shape, BF),
        compiler_params=params(8),
        cost_estimate=pl.CostEstimate(flops=FINAL_COST, bytes_accessed=2**20, transcendentals=0),
        name="sum_shares",
    )(own, *parts)


def z_shift(value, d):
    return route(value, lambda z, x, y, c: (z + d, x, y, c))


def per_device(
    contexts, trunk_weight, trunk_bias, head_weight, head_bias, arm_embed, slots, feedback, boot_weight
):
    cols = trunk_weight.shape[1]
    h = arm_embed.shape[1]
    z, c = lax.axis_index("z"), lax.axis_index("c")
    low = c == 0
    pick = lambda a, b: jnp.where(low, a, b)

    k = trunk_weight.shape[0]
    cols_for = lambda zz: lax.dynamic_slice_in_dim(contexts, ((zz + NZ) % NZ) * 2 * k, 2 * k, 1)
    side = jnp.where(low, 1, -1)
    ctx = [along_z(cols_for(z + side * i), i) for i in (1, 2, 3)]
    ctx_far = along_z(cols_for(z + 4), 4, core=1)
    ctx = [cols_for(z), ctx_far] + ctx
    w_far = x_partner(trunk_weight)
    shown = gather_rows(slots, arm_embed)
    w_own, arm_copy = place(trunk_weight, w_far, arm_embed, ctx)
    arm_far = x_partner(arm_copy)
    w_other = other_core(w_own)
    p0, p1, p2, p3 = trunk(ctx, w_own, w_other)

    third = along_z(p3, -1)
    fourth = along_z(p0, -4 + 2, core=1)
    next_one = along_z(p1, -1)
    second = along_z(p2 + third + fourth, -2)
    bias = jnp.concatenate([pick(trunk_bias, 0.0), pick(0.0, trunk_bias)])
    mine = pick(p0, 0.0) + next_one + second + bias
    feat = jnp.maximum(mine + other_core(mine), F32(0.0)).astype(BF)

    got = [along_z(feat, i) for i in (1, 2, 3)]
    far = along_z(feat, 4, core=1)
    block = stack_rows(feat, far, got, [arm_far, shown])
    block = jnp.stack([block] + [first_ring(block, d) for d in RING[1:]])
    s_in, t_in = last_ring(block, 1), last_ring(block, 3)
    blocks = NX * NY // 2
    weight = head_weight[0].reshape(blocks, 2 * cols, h)
    block_other = other_core(block)
    (act,) = run_act((0,), [block, block_other], weight, head_bias)
    s_in, t_in, s_half, t_half = cut(s_in, t_in)
    u_in = jnp.concatenate([last_ring(s_half, 3), last_ring(t_half, 1)], 0)
    own = [block, s_in, t_in, u_in]
    other = [block_other] + [other_core(v) for v in own[1:]]
    both = lambda i, j: own[i:j] + other[i:j]

    (act,) = run_act((1, 2), both(1, 3), weight, act)
    act, near, far, total = run_act((3,), both(3, 4), weight, act, shown)

    z_sum = lambda v, d: v + route(v, lambda z, x, y, c: (z ^ d, x, y, c))
    total = z_sum(z_sum(total, 4), 1)
    score, keep_up, keep_down, up, down, up4, down4, total = share_scores(
        near, x_partner(far), arm_embed, arm_far, total
    )
    up, down = z_shift(up, 1), z_shift(down, -1)
    up4, down4 = z_shift(up4, 2), z_shift(down4, -2)
    total = total + x_partner(total)
    total = z_sum(total, 2)
    up2, down2 = join((keep_up, up, up4), (keep_down, down, down4), [total])
    feats = turned(own + other, up2)
    scores = final_sum(score, up, down, z_shift(up2, 2), z_shift(down2, -2))

    weight_grad, bias_grad = run_grad(
        feats, total, feedback.T, boot_weight.astype(F32), shown, act
    )
    return (
        scores[None],
        weight_grad.reshape(1, -1, h),
        bias_grad,
    )


def solution(mesh):
    inner = Mesh(mesh.devices.reshape(NZ, 2, 2, NY, 2), AXES)
    batch, member = ("z", "xl"), ("xh", "y", "c")
    placed = (
        P(batch, None),
        P(batch, member),
        P(member),
        P(member, None, batch),
        P(member, batch),
        P(None, batch),
        P(),
        P(),
        P(member, None),
    )
    return jax.shard_map(
        per_device,
        mesh=inner,
        in_specs=placed,
        out_specs=(P(member, batch, None), P(member, None, batch), P(member, batch)),
        check_vma=False,
    )
```

```python
import functools

import jax
import jax.numpy as jnp
from jax import lax
from jax.experimental import pallas as pl
from jax.experimental.pallas import tpu as pltpu
from jax.sharding import Mesh
from jax.sharding import PartitionSpec as P

AXES = ("z", "xl", "xh", "y", "c")
NZ, NX, NY = 8, 4, 4
BF, F32 = jnp.bfloat16, jnp.float32
GRAD_COST, JOIN_COST, FINAL_COST = 2**30, 2**34, 2**34
RING = (0, 1, 3, 2)
SLOT_Z = (0, -1, -2, -3, 4, 1, 2, 3)


def flat(z, x, y, c):
    z, x, y = z % NZ, x % NX, y % NY
    return (((z * 2 + x % 2) * 2 + x // 2) * NY + y) * 2 + c


def route(value, where):
    pairs = []
    for z in range(NZ):
        for x in range(NX):
            for y in range(NY):
                for c in range(2):
                    to = where(z, x, y, c)
                    if to is not None:
                        pairs.append((flat(z, x, y, c), flat(*to)))
    return lax.ppermute(value, AXES, pairs)


def other_core(value):
    return route(value, lambda z, x, y, c: (z, x, y, 1 - c))


def x_partner(value):
    return route(value, lambda z, x, y, c: (z, x ^ 1, y, c))


def along_z(value, i, core=None):
    return route(
        value,
        lambda z, x, y, c: (z + (i if c == 0 else -i), x, y, c) if core in (None, c) else None,
    )


def first_ring(value, d):
    return route(value, lambda z, x, y, c: (z, x, y ^ d, c) if c == 0 else (z, x ^ d, y, c))


def last_ring(value, d):
    return route(value, lambda z, x, y, c: (z, x ^ d, y, c) if c == 0 else (z, x, y ^ d, c))


VMEM = pl.BlockSpec(memory_space=pltpu.VMEM)
ANYWHERE = pl.BlockSpec(memory_space=pl.ANY)


def params(mib):
    return pltpu.CompilerParams(vmem_limit_bytes=mib * 2**20)


def group_row(rel, slot, group):
    z, xl = lax.axis_index("z"), lax.axis_index("xl")
    zz = lax.rem(z + SLOT_Z[slot] + NZ, NZ)
    return pl.multiple_of((zz * 2 + (xl if rel == 0 else 1 - xl)) * group, 16)


def gather_kernel(slots_ref, arm_ref, out_ref, ids_ref):
    n_slots, n_ctx, _ = out_ref.shape
    arms = arm_ref.shape[0]
    group = n_ctx // 16
    for rel in range(2):
        for slot in range(NZ):
            ids_ref[pl.ds((rel * NZ + slot) * group, group), :] = slots_ref[
                pl.ds(group_row(rel, slot, group), group), :
            ]
    rows = n_ctx // 2
    for half in range(2):
        part = pl.ds(half * rows, rows)
        for k in range(n_slots):
            hot = ids_ref[part, k : k + 1] == lax.broadcasted_iota(jnp.int32, (rows, arms), 1)
            out_ref[k, part, :] = jnp.dot(
                jnp.where(hot, F32(1.0), F32(0.0)).astype(BF),
                arm_ref[...],
                preferred_element_type=F32,
            ).astype(BF)


def gather_rows(slots, arm):
    (n_ctx, n_slots), (arms, h) = slots.shape, arm.shape
    return pl.pallas_call(
        gather_kernel,
        in_specs=[VMEM, VMEM],
        out_specs=VMEM,
        out_shape=jax.ShapeDtypeStruct((n_slots, n_ctx, h), BF),
        scratch_shapes=[pltpu.VMEM((n_ctx, n_slots), jnp.int32)],
        compiler_params=params(24),
        cost_estimate=pl.CostEstimate(
            flops=2 * n_ctx * n_slots * arms * h, bytes_accessed=2**23, transcendentals=0
        ),
        name="gather_rows",
    )(slots, arm)


def place_kernel(near_ref, far_ref, arm_ref, *refs):
    out_ref, arm_out_ref = refs[-2:]
    k = near_ref.shape[0]
    xl = lax.axis_index("xl")
    out_ref[pl.ds(pl.multiple_of(xl * k, 16), k), :] = near_ref[...]
    out_ref[pl.ds(pl.multiple_of((1 - xl) * k, 16), k), :] = far_ref[...]
    arm_out_ref[...] = arm_ref[...]


def place(near, far, arm, after):
    k, n = near.shape
    return pl.pallas_call(
        place_kernel,
        in_specs=[VMEM] * 3 + [ANYWHERE] * len(after),
        out_specs=[VMEM] * 2,
        out_shape=[jax.ShapeDtypeStruct((2 * k, n), BF), jax.ShapeDtypeStruct(arm.shape, BF)],
        compiler_params=params(16),
        cost_estimate=pl.CostEstimate(flops=0, bytes_accessed=2**22, transcendentals=0),
        name="place_weight",
    )(near, far, arm, *after)


def stack_kernel(own_ref, g1_ref, g2_ref, g3_ref, far_ref, after_ref, out_ref):
    del after_ref
    core = lax.axis_index("c")
    group = own_ref.shape[0]

    @pl.when(core == 0)
    def _():
        out_ref[:group, :] = own_ref[...]

    @pl.when(core == 1)
    def _():
        out_ref[:group, :] = far_ref[...]

    for i, ref in enumerate((g1_ref, g2_ref, g3_ref)):
        out_ref[pl.ds((i + 1) * group, group), :] = ref[...]


def stack_rows(own, far, got, after):
    group, n = own.shape
    return pl.pallas_call(
        stack_kernel,
        in_specs=[VMEM] * 5 + [ANYWHERE],
        out_specs=VMEM,
        out_shape=jax.ShapeDtypeStruct((4 * group, n), BF),
        compiler_params=params(8),
        cost_estimate=pl.CostEstimate(flops=0, bytes_accessed=16 * group * n, transcendentals=0),
        name="stack_rows",
    )(own, *got, far, after)


def trunk_kernel(c0_ref, c1_ref, c2_ref, c3_ref, c4_ref, wa_ref, wb_ref, p0, pair, p2, ctx_ref):
    core = lax.axis_index("c")
    group = c0_ref.shape[0]
    n = wa_ref.shape[1]

    @pl.when(core == 0)
    def _():
        ctx_ref[:group, :] = c0_ref[...]

    @pl.when(core == 1)
    def _():
        ctx_ref[:group, :] = c4_ref[...]

    for i, ref in enumerate((c1_ref, c2_ref, c3_ref)):
        ctx_ref[pl.ds((i + 1) * group, group), :] = ref[...]
    for own, w_ref in ((True, wa_ref), (False, wb_ref)):
        where = core if own else 1 - core
        part = jnp.dot(ctx_ref[...], w_ref[...], preferred_element_type=F32)
        at = pl.ds(pl.multiple_of(where * n, 128), n)
        for i in range(4):
            piece = part[i * group : (i + 1) * group]
            if i % 2:
                pair[i // 2, :, at] = piece
            else:
                (p2 if i else p0)[:, at] = piece


def trunk(ctx, w_own, w_other):
    group, n = ctx[0].shape[0], w_own.shape[1]
    return pl.pallas_call(
        trunk_kernel,
        in_specs=[VMEM] * 7,
        out_specs=[VMEM] * 3,
        out_shape=[
            jax.ShapeDtypeStruct(shape, F32)
            for shape in ((group, 2 * n), (2, group, 2 * n), (group, 2 * n))
        ],
        scratch_shapes=[pltpu.VMEM((4 * group, ctx[0].shape[1]), BF)],
        compiler_params=params(16),
        cost_estimate=pl.CostEstimate(
            flops=8 * group * ctx[0].shape[1] * 2 * n, bytes_accessed=2**22, transcendentals=0
        ),
        name="trunk_sums",
    )(*ctx, w_own, w_other)


def find(pieces, p, q):
    at = 4 * q + p
    for ref in pieces:
        if at < ref.shape[0]:
            return ref, at
        at -= ref.shape[0]


def add_kernel(own_ref, pair_ref, far_ref, out_ref):
    out_ref[...] = own_ref[...] + pair_ref[1] + far_ref[...]


def add_sums(own, pair, far):
    return pl.pallas_call(
        add_kernel,
        in_specs=[VMEM] * 3,
        out_specs=VMEM,
        out_shape=jax.ShapeDtypeStruct(own.shape, F32),
        compiler_params=params(8),
        cost_estimate=pl.CostEstimate(flops=2**20, bytes_accessed=2**20, transcendentals=0),
        name="add_sums",
    )(own, pair, far)


def blocks_of(p, q, core):
    return (RING[q], RING[p]) if core == 0 else (RING[p], RING[q])


def act_kernel(qs, first, last, *refs):
    n = 2 * len(qs)
    pieces, refs = refs[:n], refs[n:]
    w_ref, start_ref = refs[:2]
    if last:
        shown_ref, act_ref, near_ref, far_ref, pick_ref, flat_ref = refs[2:]
    else:
        act_ref = refs[2]
    x_hi, y, core = lax.axis_index("xh"), lax.axis_index("y"), lax.axis_index("c")
    rows = pieces[0].shape[1]
    act_ref[...] = jnp.broadcast_to(start_ref[...], act_ref.shape)
    for half in range(2):
        of = core if half == 0 else 1 - core
        for i, q in enumerate(qs):
            for p in range(4):
                ref, at = find(pieces[half * n // 2 : (half + 1) * n // 2], p, i)
                x0, y0 = blocks_of(p, q, 0)
                x1, y1 = blocks_of(p, q, 1)
                dx, dy = jnp.where(of == 0, x0, x1), jnp.where(of == 0, y0, y1)
                cb = lax.bitwise_xor(x_hi, lax.div(dx, 2)) * NY + lax.bitwise_xor(y, dy)
                rg = lax.rem(dx, 2) * 2 + of
                part = pl.ds(pl.multiple_of(rg * rows, 16), rows)
                act_ref[part, :] += jnp.dot(ref[at], w_ref[cb], preferred_element_type=F32)
    if last:
        hid = jnp.maximum(act_ref[...], F32(0.0)).astype(BF)
        half_rows = near_ref.shape[0]
        near_ref[...] = hid[:half_rows]
        far_ref[...] = hid[half_rows:]
        wide = hid.astype(F32)
        lane = lax.broadcasted_iota(jnp.int32, (hid.shape[0], 128), 1)
        total = jnp.zeros((hid.shape[0], 128), F32)
        for k in range(8):
            one = jnp.sum(wide * shown_ref[k].astype(F32), axis=1, keepdims=True)
            total = jnp.where(lane == k, one, total)
        group = hid.shape[0] // 16
        for rel in range(2):
            for slot in range(NZ):
                at = (rel * NZ + slot) * group
                flat_ref[pl.ds(group_row(rel, slot, group), group), :] = total[at : at + group]
        pick_ref[...] = jnp.transpose(flat_ref[...])[:8]


def run_act(qs, pieces, weight, start, shown=None):
    blocks, depth, h = weight.shape
    rows = 4 * pieces[0].shape[1]
    first, last = start.shape[0] == 1, shown is not None
    shapes = [jax.ShapeDtypeStruct((rows, h), F32)]
    if last:
        shapes += [jax.ShapeDtypeStruct((rows // 2, h), BF)] * 2
        shapes += [jax.ShapeDtypeStruct((8, rows), F32)]
    args = list(pieces) + [weight, start] + ([shown] if last else [])
    return pl.pallas_call(
        functools.partial(act_kernel, qs, first, last),
        in_specs=[VMEM] * len(args),
        out_specs=[VMEM] * len(shapes),
        out_shape=shapes,
        scratch_shapes=[pltpu.VMEM((rows, 128), F32)] if last else [],
        compiler_params=params(24),
        cost_estimate=pl.CostEstimate(
            flops=2 * rows * blocks * depth * h // 4 if last else 0,
            bytes_accessed=2**22 if last else 0,
            transcendentals=0,
        ),
        name="pre_act",
    )(*args)


def cut_kernel(s_ref, t_ref, after_ref, s_out, t_out, s_half, t_half):
    del after_ref
    half = s_half.shape[0]
    s_out[...] = s_ref[...]
    t_out[...] = t_ref[...]
    s_half[...] = s_ref[:half]
    t_half[...] = t_ref[half:]


def cut(s_in, t_in, after):
    half = (s_in.shape[0] // 2,) + s_in.shape[1:]
    return pl.pallas_call(
        cut_kernel,
        in_specs=[VMEM] * 2 + [ANYWHERE],
        out_specs=[VMEM] * 4,
        out_shape=[jax.ShapeDtypeStruct(v, BF) for v in (s_in.shape, t_in.shape, half, half)],
        compiler_params=params(8),
        cost_estimate=pl.CostEstimate(flops=0, bytes_accessed=2**20, transcendentals=0),
        name="cut_halves",
    )(s_in, t_in, after)


def turn_kernel(*refs):
    pieces, out_ref = refs[:8], refs[-1]
    core = lax.axis_index("c")
    rows, depth = pieces[0].shape[1:]

    def half_of(mine, core_of, dx, dy):
        p, q = (RING.index(dy), RING.index(dx)) if core_of == 0 else (RING.index(dx), RING.index(dy))
        return find(pieces[:4] if mine else pieces[4:], p, q)

    def run(own):
        for r in range(2):
            for dy in range(4):
                for low in range(2):
                    dx = 2 * r + low
                    (a, i), (b, j) = (half_of(of == own, of, dx, dy) for of in range(2))
                    both = jnp.concatenate([a[i], b[j]], 0)
                    out_ref[r * 4 + dy, :, pl.ds(low * 2 * rows, 2 * rows)] = jnp.transpose(both)

    @pl.when(core == 0)
    def _():
        run(0)

    @pl.when(core == 1)
    def _():
        run(1)


def turned(pieces, after):
    rows, depth = pieces[0].shape[1:]
    return pl.pallas_call(
        turn_kernel,
        in_specs=[VMEM] * 8 + [ANYWHERE],
        out_specs=VMEM,
        out_shape=jax.ShapeDtypeStruct((8, depth, 4 * rows), BF),
        compiler_params=params(8),
        cost_estimate=pl.CostEstimate(flops=0, bytes_accessed=24 * 2**20, transcendentals=0),
        name="turn_features",
    )(*pieces, after)


def grad_kernel(n_slots, feats_ref, sum_ref, fed_ref, boot_ref, shown_ref, act_ref, *refs):
    out_ref, bias_ref, flat_ref, slot_ref, pre_ref, stage, sems = refs
    x_hi, y = lax.axis_index("xh"), lax.axis_index("y")
    n_ctx = act_ref.shape[0]
    group = n_ctx // 16
    grad = boot_ref[...] * (jax.nn.sigmoid(sum_ref[...]) - fed_ref[...]) / F32(n_slots)
    grad = jnp.concatenate([grad, jnp.zeros((128 - n_slots, n_ctx), F32)], 0)
    flat_ref[...] = jnp.transpose(grad)
    for rel in range(2):
        for slot in range(NZ):
            slot_ref[pl.ds((rel * NZ + slot) * group, group), :] = flat_ref[
                pl.ds(group_row(rel, slot, group), group), :
            ]
    total = slot_ref[:, 0:1] * shown_ref[0].astype(F32)
    for k in range(1, n_slots):
        total += slot_ref[:, k : k + 1] * shown_ref[k].astype(F32)
    pre = jnp.where(act_ref[...] > 0, total, F32(0.0)).astype(BF)
    pre_ref[...] = pre
    bias_ref[...] = jnp.sum(pre.astype(F32), axis=0, keepdims=True)
    copies = []
    step = stage.shape[1] // 4
    for n in range(feats_ref.shape[0]):
        cb = lax.bitwise_xor(x_hi, n // 4) * NY + lax.bitwise_xor(y, n % 4)
        for i in range(4):
            part = pl.ds(i * step, step)
            stage[n, part, :] = jnp.dot(
                feats_ref[n, part, :], pre_ref[...], preferred_element_type=F32
            ).astype(BF)
            copy = pltpu.make_async_copy(
                stage.at[n, part, :], out_ref.at[cb, part, :], sems.at[n, i]
            )
            copy.start()
            copies.append(copy)
    for copy in copies:
        copy.wait()


def run_grad(feats, sums, fed, boot, shown, act):
    rows, h = act.shape
    blocks, depth, _ = feats.shape
    n_slots = shown.shape[0]
    return pl.pallas_call(
        functools.partial(grad_kernel, n_slots),
        in_specs=[VMEM] * 6,
        out_specs=[ANYWHERE, VMEM],
        out_shape=[
            jax.ShapeDtypeStruct((blocks, depth, h), BF),
            jax.ShapeDtypeStruct((1, h), F32),
        ],
        scratch_shapes=[
            pltpu.VMEM((rows, 128), F32),
            pltpu.VMEM((rows, 128), F32),
            pltpu.VMEM((rows, h), BF),
            pltpu.VMEM((blocks, depth, h), BF),
            pltpu.SemaphoreType.DMA((blocks, 4)),
        ],
        compiler_params=params(20),
        cost_estimate=pl.CostEstimate(flops=GRAD_COST, bytes_accessed=2**20, transcendentals=0),
        name="weight_grad",
    )(feats, sums, fed, boot, shown, act)


def share_kernel(near_ref, far_ref, arm_ref, armf_ref, sums_ref, own, up2, down2, up, down, up4, down4, sums_out):
    sums_out[...] = sums_ref[...]
    dims = (((1,), (1,)), ((), ()))
    arms = arm_ref.shape[0]
    group = near_ref.shape[0] // NZ
    step = 512
    half = arms // 2
    for j in range(0, arms, step):
        part = lax.dot_general(
            near_ref[...], arm_ref[pl.ds(j, step), :], dims, preferred_element_type=F32
        ) + lax.dot_general(
            far_ref[...], armf_ref[pl.ds(j, step), :], dims, preferred_element_type=F32
        )
        at = pl.ds(j, step)
        for s in range(NZ):
            piece = part[s * group : (s + 1) * group]
            d = SLOT_Z[s]
            if d in (0, 2, -2):
                {0: own, 2: up2, -2: down2}[d][:, at] = piece
            elif d == 4:
                (up4 if j < half else down4)[:, pl.ds(j % half, step)] = piece.astype(BF)
            else:
                (up if d > 0 else down)[abs(d) // 2, :, at] = piece.astype(BF)


def share_scores(near, far, arm, arm_far, sums):
    group, arms = near.shape[0] // NZ, arm.shape[0]
    whole = jax.ShapeDtypeStruct((group, arms), F32)
    pair = jax.ShapeDtypeStruct((2, group, arms), BF)
    half = jax.ShapeDtypeStruct((group, arms // 2), BF)
    shapes = [whole] * 3 + [pair] * 2 + [half] * 2 + [jax.ShapeDtypeStruct(sums.shape, F32)]
    return pl.pallas_call(
        share_kernel,
        in_specs=[VMEM] * 5,
        out_specs=[VMEM] * 8,
        out_shape=shapes,
        compiler_params=params(24),
        cost_estimate=pl.CostEstimate(
            flops=4 * near.shape[0] * near.shape[1] * arms, bytes_accessed=2**22, transcendentals=0
        ),
        name="share_scores",
    )(near, far, arm, arm_far, sums)


def join_kernel(*refs):
    ins, outs = refs[:6], refs[-2:]
    half = ins[2].shape[1]
    for i, out_ref in enumerate(outs):
        own_ref, near_ref, far_ref = ins[3 * i : 3 * i + 3]
        for at in range(0, 2 * half, half):
            part = pl.ds(at, half)
            total = own_ref[:, part] + near_ref[1, :, part].astype(F32)
            if at == i * half:
                total += far_ref[...].astype(F32)
            out_ref[:, part] = total.astype(BF)


def join(up, down, after):
    own = up[0]
    return pl.pallas_call(
        join_kernel,
        in_specs=[VMEM] * 6 + [ANYWHERE] * len(after),
        out_specs=[VMEM] * 2,
        out_shape=[jax.ShapeDtypeStruct(own.shape, BF)] * 2,
        compiler_params=params(8),
        cost_estimate=pl.CostEstimate(flops=JOIN_COST, bytes_accessed=2**20, transcendentals=0),
        name="join_shares",
    )(*up, *down, *after)


def final_kernel(own_ref, up_ref, down_ref, up2_ref, down2_ref, out_ref):
    total = own_ref[...] + up_ref[0].astype(F32) + down_ref[0].astype(F32)
    out_ref[...] = (total + up2_ref[...].astype(F32) + down2_ref[...].astype(F32)).astype(BF)


def final_sum(own, *parts):
    return pl.pallas_call(
        final_kernel,
        in_specs=[VMEM] * 5,
        out_specs=VMEM,
        out_shape=jax.ShapeDtypeStruct(own.shape, BF),
        compiler_params=params(8),
        cost_estimate=pl.CostEstimate(flops=FINAL_COST, bytes_accessed=2**20, transcendentals=0),
        name="sum_shares",
    )(own, *parts)


def z_shift(value, d):
    return route(value, lambda z, x, y, c: (z + d, x, y, c))


def per_device(
    contexts, trunk_weight, trunk_bias, head_weight, head_bias, arm_embed, slots, feedback, boot_weight
):
    cols = trunk_weight.shape[1]
    h = arm_embed.shape[1]
    z, c = lax.axis_index("z"), lax.axis_index("c")
    low = c == 0
    pick = lambda a, b: jnp.where(low, a, b)

    k = trunk_weight.shape[0]
    cols_for = lambda zz: lax.dynamic_slice_in_dim(contexts, ((zz + NZ) % NZ) * 2 * k, 2 * k, 1)
    side = jnp.where(low, 1, -1)
    ctx = [along_z(cols_for(z + side * i), i) for i in (1, 2, 3)]
    ctx_far = along_z(cols_for(z + 4), 4, core=1)
    ctx = [cols_for(z)] + ctx + [ctx_far]
    w_far = x_partner(trunk_weight)
    shown = gather_rows(slots, arm_embed)
    w_own, arm_copy = place(trunk_weight, w_far, arm_embed, ctx)
    arm_far = x_partner(arm_copy)
    w_other = other_core(w_own)
    p0, pair, p2 = trunk(ctx, w_own, w_other)

    pair = along_z(pair, -1)
    fourth = along_z(p0, -4 + 2, core=1)
    second = along_z(add_sums(p2, pair, fourth), -2)
    bias = jnp.concatenate([pick(trunk_bias, 0.0), pick(0.0, trunk_bias)])
    mine = pick(p0, 0.0) + pair[0] + second + bias
    feat = jnp.maximum(mine + other_core(mine), F32(0.0)).astype(BF)

    got = [along_z(feat, i) for i in (1, 2, 3)]
    far = along_z(feat, 4, core=1)
    block = stack_rows(feat, far, got, arm_far)
    block = jnp.stack([block] + [first_ring(block, d) for d in RING[1:]])
    s_in, t_in = last_ring(block, 1), last_ring(block, 3)
    blocks = NX * NY // 2
    weight = head_weight[0].reshape(blocks, 2 * cols, h)
    block_other = other_core(block)
    (act,) = run_act((0,), [block, block_other], weight, head_bias)
    s_in, t_in, s_half, t_half = cut(s_in, t_in, shown)
    u_in = jnp.concatenate([last_ring(s_half, 3), last_ring(t_half, 1)], 0)
    own = [block, s_in, t_in, u_in]
    other = [block_other] + [other_core(v) for v in own[1:]]
    both = lambda i, j: own[i:j] + other[i:j]

    (act,) = run_act((1, 2), both(1, 3), weight, act)
    act, near, far, total = run_act((3,), both(3, 4), weight, act, shown)

    z_sum = lambda v, d: v + route(v, lambda z, x, y, c: (z ^ d, x, y, c))
    total = z_sum(z_sum(total, 4), 1)
    score, keep_up, keep_down, up, down, up4, down4, total = share_scores(
        near, x_partner(far), arm_embed, arm_far, total
    )
    up, down = z_shift(up, 1), z_shift(down, -1)
    up4, down4 = z_shift(up4, 2), z_shift(down4, -2)
    total = total + x_partner(total)
    total = z_sum(total, 2)
    up2, down2 = join((keep_up, up, up4), (keep_down, down, down4), [total])
    feats = turned(own + other, up2)
    scores = final_sum(score, up, down, z_shift(up2, 2), z_shift(down2, -2))

    weight_grad, bias_grad = run_grad(
        feats, total, feedback.T, boot_weight.astype(F32), shown, act
    )
    return (
        scores[None],
        weight_grad.reshape(1, -1, h),
        bias_grad,
    )


def solution(mesh):
    inner = Mesh(mesh.devices.reshape(NZ, 2, 2, NY, 2), AXES)
    batch, member = ("z", "xl"), ("xh", "y", "c")
    placed = (
        P(batch, None),
        P(batch, member),
        P(member),
        P(member, None, batch),
        P(member, batch),
        P(None, batch),
        P(),
        P(),
        P(member, None),
    )
    return jax.shard_map(
        per_device,
        mesh=inner,
        in_specs=placed,
        out_specs=(P(member, batch, None), P(member, None, batch), P(member, batch)),
        check_vma=False,
    )
```

```python
import functools

import jax
import jax.numpy as jnp
from jax import lax
from jax.experimental import pallas as pl
from jax.experimental.pallas import tpu as pltpu
from jax.sharding import Mesh
from jax.sharding import PartitionSpec as P

AXES = ("z", "xl", "xh", "y", "c")
NZ, NX, NY = 8, 4, 4
BF, F32 = jnp.bfloat16, jnp.float32
GRAD_COST, JOIN_COST, FINAL_COST = 2**30, 2**34, 2**34
RING = (0, 1, 3, 2)
SLOT_Z = (0, -1, -2, -3, 4, 1, 2, 3)


def flat(z, x, y, c):
    z, x, y = z % NZ, x % NX, y % NY
    return (((z * 2 + x % 2) * 2 + x // 2) * NY + y) * 2 + c


def route(value, where):
    pairs = []
    for z in range(NZ):
        for x in range(NX):
            for y in range(NY):
                for c in range(2):
                    to = where(z, x, y, c)
                    if to is not None:
                        pairs.append((flat(z, x, y, c), flat(*to)))
    return lax.ppermute(value, AXES, pairs)


def other_core(value):
    return route(value, lambda z, x, y, c: (z, x, y, 1 - c))


def x_partner(value):
    return route(value, lambda z, x, y, c: (z, x ^ 1, y, c))


def along_z(value, i, core=None):
    return route(
        value,
        lambda z, x, y, c: (z + (i if c == 0 else -i), x, y, c) if core in (None, c) else None,
    )


def first_ring(value, d):
    return route(value, lambda z, x, y, c: (z, x, y ^ d, c) if c == 0 else (z, x ^ d, y, c))


def last_ring(value, d):
    return route(value, lambda z, x, y, c: (z, x ^ d, y, c) if c == 0 else (z, x, y ^ d, c))


VMEM = pl.BlockSpec(memory_space=pltpu.VMEM)
ANYWHERE = pl.BlockSpec(memory_space=pl.ANY)


def params(mib):
    return pltpu.CompilerParams(vmem_limit_bytes=mib * 2**20)


def group_row(rel, slot, group):
    z, xl = lax.axis_index("z"), lax.axis_index("xl")
    zz = lax.rem(z + SLOT_Z[slot] + NZ, NZ)
    return pl.multiple_of((zz * 2 + (xl if rel == 0 else 1 - xl)) * group, 16)


def gather_kernel(slots_ref, arm_ref, out_ref, ids_ref):
    n_slots, n_ctx, _ = out_ref.shape
    arms = arm_ref.shape[0]
    group = n_ctx // 16
    for rel in range(2):
        for slot in range(NZ):
            ids_ref[pl.ds((rel * NZ + slot) * group, group), :] = slots_ref[
                pl.ds(group_row(rel, slot, group), group), :
            ]
    rows = n_ctx // 2
    for half in range(2):
        part = pl.ds(half * rows, rows)
        for k in range(n_slots):
            hot = ids_ref[part, k : k + 1] == lax.broadcasted_iota(jnp.int32, (rows, arms), 1)
            out_ref[k, part, :] = jnp.dot(
                jnp.where(hot, F32(1.0), F32(0.0)).astype(BF),
                arm_ref[...],
                preferred_element_type=F32,
            ).astype(BF)


def gather_rows(slots, arm):
    (n_ctx, n_slots), (arms, h) = slots.shape, arm.shape
    return pl.pallas_call(
        gather_kernel,
        in_specs=[VMEM, VMEM],
        out_specs=VMEM,
        out_shape=jax.ShapeDtypeStruct((n_slots, n_ctx, h), BF),
        scratch_shapes=[pltpu.VMEM((n_ctx, n_slots), jnp.int32)],
        compiler_params=params(14),
        cost_estimate=pl.CostEstimate(
            flops=2 * n_ctx * n_slots * arms * h, bytes_accessed=2**23, transcendentals=0
        ),
        name="gather_rows",
    )(slots, arm)


def place_kernel(near_ref, far_ref, arm_ref, *refs):
    out_ref, arm_out_ref = refs[-2:]
    k = near_ref.shape[0]
    xl = lax.axis_index("xl")
    out_ref[pl.ds(pl.multiple_of(xl * k, 16), k), :] = near_ref[...]
    out_ref[pl.ds(pl.multiple_of((1 - xl) * k, 16), k), :] = far_ref[...]
    arm_out_ref[...] = arm_ref[...]


def place(near, far, arm, after):
    k, n = near.shape
    return pl.pallas_call(
        place_kernel,
        in_specs=[VMEM] * 3 + [ANYWHERE] * len(after),
        out_specs=[VMEM] * 2,
        out_shape=[jax.ShapeDtypeStruct((2 * k, n), BF), jax.ShapeDtypeStruct(arm.shape, BF)],
        compiler_params=params(4),
        cost_estimate=pl.CostEstimate(flops=0, bytes_accessed=2**22, transcendentals=0),
        name="place_weight",
    )(near, far, arm, *after)


def stack_kernel(own_ref, g1_ref, g2_ref, g3_ref, far_ref, after_ref, out_ref):
    del after_ref
    core = lax.axis_index("c")
    group = own_ref.shape[0]

    @pl.when(core == 0)
    def _():
        out_ref[:group, :] = own_ref[...]

    @pl.when(core == 1)
    def _():
        out_ref[:group, :] = far_ref[...]

    for i, ref in enumerate((g1_ref, g2_ref, g3_ref)):
        out_ref[pl.ds((i + 1) * group, group), :] = ref[...]


def stack_rows(own, far, got, after):
    group, n = own.shape
    return pl.pallas_call(
        stack_kernel,
        in_specs=[VMEM] * 5 + [ANYWHERE],
        out_specs=VMEM,
        out_shape=jax.ShapeDtypeStruct((4 * group, n), BF),
        compiler_params=params(4),
        cost_estimate=pl.CostEstimate(flops=0, bytes_accessed=16 * group * n, transcendentals=0),
        name="stack_rows",
    )(own, *got, far, after)


def trunk_kernel(c0_ref, c1_ref, c2_ref, c3_ref, c4_ref, wa_ref, wb_ref, p0, pair, p2, ctx_ref):
    core = lax.axis_index("c")
    group = c0_ref.shape[0]
    n = wa_ref.shape[1]

    @pl.when(core == 0)
    def _():
        ctx_ref[:group, :] = c0_ref[...]

    @pl.when(core == 1)
    def _():
        ctx_ref[:group, :] = c4_ref[...]

    for i, ref in enumerate((c1_ref, c2_ref, c3_ref)):
        ctx_ref[pl.ds((i + 1) * group, group), :] = ref[...]
    for own, w_ref in ((True, wa_ref), (False, wb_ref)):
        where = core if own else 1 - core
        part = jnp.dot(ctx_ref[...], w_ref[...], preferred_element_type=F32)
        at = pl.ds(pl.multiple_of(where * n, 128), n)
        for i in range(4):
            piece = part[i * group : (i + 1) * group]
            if i % 2:
                pair[i // 2, :, at] = piece
            else:
                (p2 if i else p0)[:, at] = piece


def trunk(ctx, w_own, w_other):
    group, n = ctx[0].shape[0], w_own.shape[1]
    return pl.pallas_call(
        trunk_kernel,
        in_specs=[VMEM] * 7,
        out_specs=[VMEM] * 3,
        out_shape=[
            jax.ShapeDtypeStruct(shape, F32)
            for shape in ((group, 2 * n), (2, group, 2 * n), (group, 2 * n))
        ],
        scratch_shapes=[pltpu.VMEM((4 * group, ctx[0].shape[1]), BF)],
        compiler_params=params(8),
        cost_estimate=pl.CostEstimate(
            flops=8 * group * ctx[0].shape[1] * 2 * n, bytes_accessed=2**22, transcendentals=0
        ),
        name="trunk_sums",
    )(*ctx, w_own, w_other)


def find(pieces, p, q):
    at = 4 * q + p
    for ref in pieces:
        if at < ref.shape[0]:
            return ref, at
        at -= ref.shape[0]


def add_kernel(own_ref, pair_ref, far_ref, out_ref):
    out_ref[...] = own_ref[...] + pair_ref[1] + far_ref[...]


def add_sums(own, pair, far):
    return pl.pallas_call(
        add_kernel,
        in_specs=[VMEM] * 3,
        out_specs=VMEM,
        out_shape=jax.ShapeDtypeStruct(own.shape, F32),
        compiler_params=params(4),
        cost_estimate=pl.CostEstimate(flops=2**20, bytes_accessed=2**20, transcendentals=0),
        name="add_sums",
    )(own, pair, far)


def blocks_of(p, q, core):
    return (RING[q], RING[p]) if core == 0 else (RING[p], RING[q])


def act_kernel(qs, first, last, *refs):
    n = 2 * len(qs)
    pieces, refs = refs[:n], refs[n:]
    w_ref, start_ref = refs[:2]
    if last:
        shown_ref, act_ref, near_ref, far_ref, pick_ref, flat_ref = refs[2:]
    else:
        act_ref = refs[2]
    x_hi, y, core = lax.axis_index("xh"), lax.axis_index("y"), lax.axis_index("c")
    rows = pieces[0].shape[1]
    act_ref[...] = jnp.broadcast_to(start_ref[...], act_ref.shape)
    for half in range(2):
        of = core if half == 0 else 1 - core
        for i, q in enumerate(qs):
            for p in range(4):
                ref, at = find(pieces[half * n // 2 : (half + 1) * n // 2], p, i)
                x0, y0 = blocks_of(p, q, 0)
                x1, y1 = blocks_of(p, q, 1)
                dx, dy = jnp.where(of == 0, x0, x1), jnp.where(of == 0, y0, y1)
                cb = lax.bitwise_xor(x_hi, lax.div(dx, 2)) * NY + lax.bitwise_xor(y, dy)
                rg = lax.rem(dx, 2) * 2 + of
                part = pl.ds(pl.multiple_of(rg * rows, 16), rows)
                act_ref[part, :] += jnp.dot(ref[at], w_ref[cb], preferred_element_type=F32)
    if last:
        hid = jnp.maximum(act_ref[...], F32(0.0)).astype(BF)
        half_rows = near_ref.shape[0]
        near_ref[...] = hid[:half_rows]
        far_ref[...] = hid[half_rows:]
        wide = hid.astype(F32)
        lane = lax.broadcasted_iota(jnp.int32, (hid.shape[0], 128), 1)
        total = jnp.zeros((hid.shape[0], 128), F32)
        for k in range(8):
            one = jnp.sum(wide * shown_ref[k].astype(F32), axis=1, keepdims=True)
            total = jnp.where(lane == k, one, total)
        group = hid.shape[0] // 16
        for rel in range(2):
            for slot in range(NZ):
                at = (rel * NZ + slot) * group
                flat_ref[pl.ds(group_row(rel, slot, group), group), :] = total[at : at + group]
        pick_ref[...] = jnp.transpose(flat_ref[...])[:8]


def run_act(qs, pieces, weight, start, shown=None):
    blocks, depth, h = weight.shape
    rows = 4 * pieces[0].shape[1]
    first, last = start.shape[0] == 1, shown is not None
    shapes = [jax.ShapeDtypeStruct((rows, h), F32)]
    if last:
        shapes += [jax.ShapeDtypeStruct((rows // 2, h), BF)] * 2
        shapes += [jax.ShapeDtypeStruct((8, rows), F32)]
    args = list(pieces) + [weight, start] + ([shown] if last else [])
    return pl.pallas_call(
        functools.partial(act_kernel, qs, first, last),
        in_specs=[VMEM] * len(args),
        out_specs=[VMEM] * len(shapes),
        out_shape=shapes,
        scratch_shapes=[pltpu.VMEM((rows, 128), F32)] if last else [],
        compiler_params=params(12),
        cost_estimate=pl.CostEstimate(
            flops=2 * rows * blocks * depth * h // 4 if last else 0,
            bytes_accessed=2**22 if last else 0,
            transcendentals=0,
        ),
        name="pre_act",
    )(*args)


def cut_kernel(s_ref, t_ref, after_ref, s_out, t_out, s_half, t_half):
    del after_ref
    half = s_half.shape[0]
    s_out[...] = s_ref[...]
    t_out[...] = t_ref[...]
    s_half[...] = s_ref[:half]
    t_half[...] = t_ref[half:]


def cut(s_in, t_in, after):
    half = (s_in.shape[0] // 2,) + s_in.shape[1:]
    return pl.pallas_call(
        cut_kernel,
        in_specs=[VMEM] * 2 + [ANYWHERE],
        out_specs=[VMEM] * 4,
        out_shape=[jax.ShapeDtypeStruct(v, BF) for v in (s_in.shape, t_in.shape, half, half)],
        compiler_params=params(4),
        cost_estimate=pl.CostEstimate(flops=0, bytes_accessed=2**20, transcendentals=0),
        name="cut_halves",
    )(s_in, t_in, after)


def turn_kernel(*refs):
    pieces, out_ref = refs[:8], refs[-1]
    core = lax.axis_index("c")
    rows, depth = pieces[0].shape[1:]

    def half_of(mine, core_of, dx, dy):
        p, q = (RING.index(dy), RING.index(dx)) if core_of == 0 else (RING.index(dx), RING.index(dy))
        return find(pieces[:4] if mine else pieces[4:], p, q)

    def run(own):
        for r in range(2):
            for dy in range(4):
                for low in range(2):
                    dx = 2 * r + low
                    (a, i), (b, j) = (half_of(of == own, of, dx, dy) for of in range(2))
                    both = jnp.concatenate([a[i], b[j]], 0)
                    out_ref[r * 4 + dy, :, pl.ds(low * 2 * rows, 2 * rows)] = jnp.transpose(both)

    @pl.when(core == 0)
    def _():
        run(0)

    @pl.when(core == 1)
    def _():
        run(1)


def turned(pieces, after):
    rows, depth = pieces[0].shape[1:]
    return pl.pallas_call(
        turn_kernel,
        in_specs=[VMEM] * 8 + [ANYWHERE],
        out_specs=VMEM,
        out_shape=jax.ShapeDtypeStruct((8, depth, 4 * rows), BF),
        compiler_params=params(8),
        cost_estimate=pl.CostEstimate(flops=0, bytes_accessed=24 * 2**20, transcendentals=0),
        name="turn_features",
    )(*pieces, after)


def grad_kernel(n_slots, feats_ref, sum_ref, fed_ref, boot_ref, shown_ref, act_ref, *refs):
    out_ref, bias_ref, flat_ref, slot_ref, pre_ref, stage, sems = refs
    x_hi, y = lax.axis_index("xh"), lax.axis_index("y")
    n_ctx = act_ref.shape[0]
    group = n_ctx // 16
    grad = boot_ref[...] * (jax.nn.sigmoid(sum_ref[...]) - fed_ref[...]) / F32(n_slots)
    grad = jnp.concatenate([grad, jnp.zeros((128 - n_slots, n_ctx), F32)], 0)
    flat_ref[...] = jnp.transpose(grad)
    for rel in range(2):
        for slot in range(NZ):
            slot_ref[pl.ds((rel * NZ + slot) * group, group), :] = flat_ref[
                pl.ds(group_row(rel, slot, group), group), :
            ]
    total = slot_ref[:, 0:1] * shown_ref[0].astype(F32)
    for k in range(1, n_slots):
        total += slot_ref[:, k : k + 1] * shown_ref[k].astype(F32)
    pre = jnp.where(act_ref[...] > 0, total, F32(0.0)).astype(BF)
    pre_ref[...] = pre
    bias_ref[...] = jnp.sum(pre.astype(F32), axis=0, keepdims=True)
    copies = []
    step = stage.shape[1] // 4
    for n in range(feats_ref.shape[0]):
        cb = lax.bitwise_xor(x_hi, n // 4) * NY + lax.bitwise_xor(y, n % 4)
        for i in range(4):
            part = pl.ds(i * step, step)
            stage[n, part, :] = jnp.dot(
                feats_ref[n, part, :], pre_ref[...], preferred_element_type=F32
            ).astype(BF)
            copy = pltpu.make_async_copy(
                stage.at[n, part, :], out_ref.at[cb, part, :], sems.at[n, i]
            )
            copy.start()
            copies.append(copy)
    for copy in copies:
        copy.wait()


def run_grad(feats, sums, fed, boot, shown, act):
    rows, h = act.shape
    blocks, depth, _ = feats.shape
    n_slots = shown.shape[0]
    return pl.pallas_call(
        functools.partial(grad_kernel, n_slots),
        in_specs=[VMEM] * 6,
        out_specs=[ANYWHERE, VMEM],
        out_shape=[
            jax.ShapeDtypeStruct((blocks, depth, h), BF),
            jax.ShapeDtypeStruct((1, h), F32),
        ],
        scratch_shapes=[
            pltpu.VMEM((rows, 128), F32),
            pltpu.VMEM((rows, 128), F32),
            pltpu.VMEM((rows, h), BF),
            pltpu.VMEM((blocks, depth, h), BF),
            pltpu.SemaphoreType.DMA((blocks, 4)),
        ],
        compiler_params=params(14),
        cost_estimate=pl.CostEstimate(flops=GRAD_COST, bytes_accessed=2**20, transcendentals=0),
        name="weight_grad",
    )(feats, sums, fed, boot, shown, act)


def share_kernel(near_ref, far_ref, arm_ref, armf_ref, sums_ref, own, up2, down2, up, down, up4, down4, sums_out):
    sums_out[...] = sums_ref[...]
    dims = (((1,), (1,)), ((), ()))
    arms = arm_ref.shape[0]
    group = near_ref.shape[0] // NZ
    step = 512
    half = arms // 2
    for j in range(0, arms, step):
        part = lax.dot_general(
            near_ref[...], arm_ref[pl.ds(j, step), :], dims, preferred_element_type=F32
        ) + lax.dot_general(
            far_ref[...], armf_ref[pl.ds(j, step), :], dims, preferred_element_type=F32
        )
        at = pl.ds(j, step)
        for s in range(NZ):
            piece = part[s * group : (s + 1) * group]
            d = SLOT_Z[s]
            if d in (0, 2, -2):
                {0: own, 2: up2, -2: down2}[d][:, at] = piece
            elif d == 4:
                (up4 if j < half else down4)[:, pl.ds(j % half, step)] = piece.astype(BF)
            else:
                (up if d > 0 else down)[abs(d) // 2, :, at] = piece.astype(BF)


def share_scores(near, far, arm, arm_far, sums):
    group, arms = near.shape[0] // NZ, arm.shape[0]
    whole = jax.ShapeDtypeStruct((group, arms), F32)
    pair = jax.ShapeDtypeStruct((2, group, arms), BF)
    half = jax.ShapeDtypeStruct((group, arms // 2), BF)
    shapes = [whole] * 3 + [pair] * 2 + [half] * 2 + [jax.ShapeDtypeStruct(sums.shape, F32)]
    return pl.pallas_call(
        share_kernel,
        in_specs=[VMEM] * 5,
        out_specs=[VMEM] * 8,
        out_shape=shapes,
        compiler_params=params(14),
        cost_estimate=pl.CostEstimate(
            flops=4 * near.shape[0] * near.shape[1] * arms, bytes_accessed=2**22, transcendentals=0
        ),
        name="share_scores",
    )(near, far, arm, arm_far, sums)


def join_kernel(*refs):
    ins, outs = refs[:6], refs[-2:]
    half = ins[2].shape[1]
    for i, out_ref in enumerate(outs):
        own_ref, near_ref, far_ref = ins[3 * i : 3 * i + 3]
        for at in range(0, 2 * half, half):
            part = pl.ds(at, half)
            total = own_ref[:, part] + near_ref[1, :, part].astype(F32)
            if at == i * half:
                total += far_ref[...].astype(F32)
            out_ref[:, part] = total.astype(BF)


def join(up, down, after):
    own = up[0]
    return pl.pallas_call(
        join_kernel,
        in_specs=[VMEM] * 6 + [ANYWHERE] * len(after),
        out_specs=[VMEM] * 2,
        out_shape=[jax.ShapeDtypeStruct(own.shape, BF)] * 2,
        compiler_params=params(4),
        cost_estimate=pl.CostEstimate(flops=JOIN_COST, bytes_accessed=2**20, transcendentals=0),
        name="join_shares",
    )(*up, *down, *after)


def final_kernel(own_ref, up_ref, down_ref, up2_ref, down2_ref, out_ref):
    total = own_ref[...] + up_ref[0].astype(F32) + down_ref[0].astype(F32)
    out_ref[...] = (total + up2_ref[...].astype(F32) + down2_ref[...].astype(F32)).astype(BF)


def final_sum(own, *parts):
    return pl.pallas_call(
        final_kernel,
        in_specs=[VMEM] * 5,
        out_specs=VMEM,
        out_shape=jax.ShapeDtypeStruct(own.shape, BF),
        compiler_params=params(4),
        cost_estimate=pl.CostEstimate(flops=FINAL_COST, bytes_accessed=2**20, transcendentals=0),
        name="sum_shares",
    )(own, *parts)


def z_shift(value, d):
    return route(value, lambda z, x, y, c: (z + d, x, y, c))


def per_device(
    contexts, trunk_weight, trunk_bias, head_weight, head_bias, arm_embed, slots, feedback, boot_weight
):
    cols = trunk_weight.shape[1]
    h = arm_embed.shape[1]
    z, c = lax.axis_index("z"), lax.axis_index("c")
    low = c == 0
    pick = lambda a, b: jnp.where(low, a, b)

    k = trunk_weight.shape[0]
    cols_for = lambda zz: lax.dynamic_slice_in_dim(contexts, ((zz + NZ) % NZ) * 2 * k, 2 * k, 1)
    side = jnp.where(low, 1, -1)
    ctx = [along_z(cols_for(z + side * i), i) for i in (1, 2, 3)]
    ctx_far = along_z(cols_for(z + 4), 4, core=1)
    ctx = [cols_for(z)] + ctx + [ctx_far]
    w_far = x_partner(trunk_weight)
    shown = gather_rows(slots, arm_embed)
    w_own, arm_copy = place(trunk_weight, w_far, arm_embed, ctx)
    arm_far = x_partner(arm_copy)
    w_other = other_core(w_own)
    p0, pair, p2 = trunk(ctx, w_own, w_other)

    pair = along_z(pair, -1)
    fourth = along_z(p0, -4 + 2, core=1)
    second = along_z(add_sums(p2, pair, fourth), -2)
    bias = jnp.concatenate([pick(trunk_bias, 0.0), pick(0.0, trunk_bias)])
    mine = pick(p0, 0.0) + pair[0] + second + bias
    feat = jnp.maximum(mine + other_core(mine), F32(0.0)).astype(BF)

    got = [along_z(feat, i) for i in (1, 2, 3)]
    far = along_z(got[2], 1, core=1)
    block = stack_rows(feat, far, got, arm_far)
    block = jnp.stack([block] + [first_ring(block, d) for d in RING[1:]])
    s_in, t_in = last_ring(block, 1), last_ring(block, 3)
    blocks = NX * NY // 2
    weight = head_weight[0].reshape(blocks, 2 * cols, h)
    block_other = other_core(block)
    (act,) = run_act((0,), [block, block_other], weight, head_bias)
    s_in, t_in, s_half, t_half = cut(s_in, t_in, shown)
    u_in = jnp.concatenate([last_ring(s_half, 3), last_ring(t_half, 1)], 0)
    own = [block, s_in, t_in, u_in]
    other = [block_other] + [other_core(v) for v in own[1:]]
    both = lambda i, j: own[i:j] + other[i:j]

    (act,) = run_act((1, 2), both(1, 3), weight, act)
    act, near, far, total = run_act((3,), both(3, 4), weight, act, shown)

    z_sum = lambda v, d: v + route(v, lambda z, x, y, c: (z ^ d, x, y, c))
    total = z_sum(z_sum(total, 4), 1)
    score, keep_up, keep_down, up, down, up4, down4, total = share_scores(
        near, x_partner(far), arm_embed, arm_far, total
    )
    up, down = z_shift(up, 1), z_shift(down, -1)
    up4, down4 = z_shift(up4, 2), z_shift(down4, -2)
    total = total + x_partner(total)
    total = z_sum(total, 2)
    up2, down2 = join((keep_up, up, up4), (keep_down, down, down4), [total])
    feats = turned(own + other, up2)
    scores = final_sum(score, up, down, z_shift(up2, 2), z_shift(down2, -2))

    weight_grad, bias_grad = run_grad(
        feats, total, feedback.T, boot_weight.astype(F32), shown, act
    )
    return (
        scores[None],
        weight_grad.reshape(1, -1, h),
        bias_grad,
    )


def solution(mesh):
    inner = Mesh(mesh.devices.reshape(NZ, 2, 2, NY, 2), AXES)
    batch, member = ("z", "xl"), ("xh", "y", "c")
    placed = (
        P(batch, None),
        P(batch, member),
        P(member),
        P(member, None, batch),
        P(member, batch),
        P(None, batch),
        P(),
        P(),
        P(member, None),
    )
    return jax.shard_map(
        per_device,
        mesh=inner,
        in_specs=placed,
        out_specs=(P(member, batch, None), P(member, None, batch), P(member, batch)),
        check_vma=False,
    )
```

```python
import functools

import jax
import jax.numpy as jnp
from jax import lax
from jax.experimental import pallas as pl
from jax.experimental.pallas import tpu as pltpu
from jax.sharding import Mesh
from jax.sharding import PartitionSpec as P

AXES = ("z", "xl", "xh", "y", "c")
NZ, NX, NY = 8, 4, 4
BF, F32 = jnp.bfloat16, jnp.float32
GRAD_COST, JOIN_COST, FINAL_COST = 2**30, 2**34, 2**34
RING = (0, 1, 3, 2)
SLOT_Z = (0, -1, -2, -3, 4, 1, 2, 3)


def flat(z, x, y, c):
    z, x, y = z % NZ, x % NX, y % NY
    return (((z * 2 + x % 2) * 2 + x // 2) * NY + y) * 2 + c


def route(value, where):
    pairs = []
    for z in range(NZ):
        for x in range(NX):
            for y in range(NY):
                for c in range(2):
                    to = where(z, x, y, c)
                    if to is not None:
                        pairs.append((flat(z, x, y, c), flat(*to)))
    return lax.ppermute(value, AXES, pairs)


def other_core(value):
    return route(value, lambda z, x, y, c: (z, x, y, 1 - c))


def x_partner(value):
    return route(value, lambda z, x, y, c: (z, x ^ 1, y, c))


def along_z(value, i, core=None):
    return route(
        value,
        lambda z, x, y, c: (z + (i if c == 0 else -i), x, y, c) if core in (None, c) else None,
    )


def first_ring(value, d):
    return route(value, lambda z, x, y, c: (z, x, y ^ d, c) if c == 0 else (z, x ^ d, y, c))


def last_ring(value, d):
    return route(value, lambda z, x, y, c: (z, x ^ d, y, c) if c == 0 else (z, x, y ^ d, c))


VMEM = pl.BlockSpec(memory_space=pltpu.VMEM)
ANYWHERE = pl.BlockSpec(memory_space=pl.ANY)


def params(mib):
    return pltpu.CompilerParams(vmem_limit_bytes=mib * 2**20)


def group_row(rel, slot, group):
    z, xl = lax.axis_index("z"), lax.axis_index("xl")
    zz = lax.rem(z + SLOT_Z[slot] + NZ, NZ)
    return pl.multiple_of((zz * 2 + (xl if rel == 0 else 1 - xl)) * group, 16)


def gather_kernel(slots_ref, arm_ref, out_ref, ids_ref):
    n_slots, n_ctx, _ = out_ref.shape
    arms = arm_ref.shape[0]
    group = n_ctx // 16
    for rel in range(2):
        for slot in range(NZ):
            ids_ref[pl.ds((rel * NZ + slot) * group, group), :] = slots_ref[
                pl.ds(group_row(rel, slot, group), group), :
            ]
    rows = n_ctx // 2
    for half in range(2):
        part = pl.ds(half * rows, rows)
        for k in range(n_slots):
            hot = ids_ref[part, k : k + 1] == lax.broadcasted_iota(jnp.int32, (rows, arms), 1)
            out_ref[k, part, :] = jnp.dot(
                jnp.where(hot, F32(1.0), F32(0.0)).astype(BF),
                arm_ref[...],
                preferred_element_type=F32,
            ).astype(BF)


def gather_rows(slots, arm):
    (n_ctx, n_slots), (arms, h) = slots.shape, arm.shape
    return pl.pallas_call(
        gather_kernel,
        in_specs=[VMEM, VMEM],
        out_specs=VMEM,
        out_shape=jax.ShapeDtypeStruct((n_slots, n_ctx, h), BF),
        scratch_shapes=[pltpu.VMEM((n_ctx, n_slots), jnp.int32)],
        compiler_params=params(14),
        cost_estimate=pl.CostEstimate(
            flops=2 * n_ctx * n_slots * arms * h, bytes_accessed=2**23, transcendentals=0
        ),
        name="gather_rows",
    )(slots, arm)


def place_kernel(near_ref, far_ref, arm_ref, *refs):
    out_ref, arm_out_ref = refs[-2:]
    k = near_ref.shape[0]
    xl = lax.axis_index("xl")
    out_ref[pl.ds(pl.multiple_of(xl * k, 16), k), :] = near_ref[...]
    out_ref[pl.ds(pl.multiple_of((1 - xl) * k, 16), k), :] = far_ref[...]
    arm_out_ref[...] = arm_ref[...]


def place(near, far, arm, after):
    k, n = near.shape
    return pl.pallas_call(
        place_kernel,
        in_specs=[VMEM] * 3 + [ANYWHERE] * len(after),
        out_specs=[VMEM] * 2,
        out_shape=[jax.ShapeDtypeStruct((2 * k, n), BF), jax.ShapeDtypeStruct(arm.shape, BF)],
        compiler_params=params(4),
        cost_estimate=pl.CostEstimate(flops=0, bytes_accessed=2**22, transcendentals=0),
        name="place_weight",
    )(near, far, arm, *after)


def stack_kernel(own_ref, g1_ref, g2_ref, g3_ref, far_ref, after_ref, out_ref):
    del after_ref
    core = lax.axis_index("c")
    group = own_ref.shape[0]

    @pl.when(core == 0)
    def _():
        out_ref[:group, :] = own_ref[...]

    @pl.when(core == 1)
    def _():
        out_ref[:group, :] = far_ref[...]

    for i, ref in enumerate((g1_ref, g2_ref, g3_ref)):
        out_ref[pl.ds((i + 1) * group, group), :] = ref[...]


def stack_rows(own, far, got, after):
    group, n = own.shape
    return pl.pallas_call(
        stack_kernel,
        in_specs=[VMEM] * 5 + [ANYWHERE],
        out_specs=VMEM,
        out_shape=jax.ShapeDtypeStruct((4 * group, n), BF),
        compiler_params=params(4),
        cost_estimate=pl.CostEstimate(flops=0, bytes_accessed=16 * group * n, transcendentals=0),
        name="stack_rows",
    )(own, *got, far, after)


def trunk_kernel(c0_ref, c1_ref, c2_ref, c3_ref, c4_ref, wa_ref, wb_ref, p0, pair, p2, ctx_ref):
    core = lax.axis_index("c")
    group = c0_ref.shape[0]
    n = wa_ref.shape[1]

    @pl.when(core == 0)
    def _():
        ctx_ref[:group, :] = c0_ref[...]

    @pl.when(core == 1)
    def _():
        ctx_ref[:group, :] = c4_ref[...]

    for i, ref in enumerate((c1_ref, c2_ref, c3_ref)):
        ctx_ref[pl.ds((i + 1) * group, group), :] = ref[...]
    for own, w_ref in ((True, wa_ref), (False, wb_ref)):
        where = core if own else 1 - core
        part = jnp.dot(ctx_ref[...], w_ref[...], preferred_element_type=F32)
        at = pl.ds(pl.multiple_of(where * n, 128), n)
        for i in range(4):
            piece = part[i * group : (i + 1) * group]
            if i % 2:
                pair[i // 2, :, at] = piece
            else:
                (p2 if i else p0)[:, at] = piece


def trunk(ctx, w_own, w_other):
    group, n = ctx[0].shape[0], w_own.shape[1]
    return pl.pallas_call(
        trunk_kernel,
        in_specs=[VMEM] * 7,
        out_specs=[VMEM] * 3,
        out_shape=[
            jax.ShapeDtypeStruct(shape, F32)
            for shape in ((group, 2 * n), (2, group, 2 * n), (group, 2 * n))
        ],
        scratch_shapes=[pltpu.VMEM((4 * group, ctx[0].shape[1]), BF)],
        compiler_params=params(8),
        cost_estimate=pl.CostEstimate(
            flops=8 * group * ctx[0].shape[1] * 2 * n, bytes_accessed=2**22, transcendentals=0
        ),
        name="trunk_sums",
    )(*ctx, w_own, w_other)


def find(pieces, p, q):
    at = 4 * q + p
    for ref in pieces:
        if at < ref.shape[0]:
            return ref, at
        at -= ref.shape[0]


def add_kernel(own_ref, pair_ref, far_ref, out_ref):
    out_ref[...] = own_ref[...] + pair_ref[1] + far_ref[...]


def add_sums(own, pair, far):
    return pl.pallas_call(
        add_kernel,
        in_specs=[VMEM] * 3,
        out_specs=VMEM,
        out_shape=jax.ShapeDtypeStruct(own.shape, F32),
        compiler_params=params(4),
        cost_estimate=pl.CostEstimate(flops=2**20, bytes_accessed=2**20, transcendentals=0),
        name="add_sums",
    )(own, pair, far)


def blocks_of(p, q, core):
    return (RING[q], RING[p]) if core == 0 else (RING[p], RING[q])


def act_kernel(qs, first, last, *refs):
    n = 2 * len(qs)
    pieces, refs = refs[:n], refs[n:]
    w_ref, start_ref = refs[:2]
    if last:
        shown_ref, act_ref, near_ref, far_ref, pick_ref, flat_ref = refs[2:]
    else:
        act_ref = refs[2]
    x_hi, y, core = lax.axis_index("xh"), lax.axis_index("y"), lax.axis_index("c")
    rows = pieces[0].shape[1]
    act_ref[...] = jnp.broadcast_to(start_ref[...], act_ref.shape)
    for half in range(2):
        of = core if half == 0 else 1 - core
        for i, q in enumerate(qs):
            for p in range(4):
                ref, at = find(pieces[half * n // 2 : (half + 1) * n // 2], p, i)
                x0, y0 = blocks_of(p, q, 0)
                x1, y1 = blocks_of(p, q, 1)
                dx, dy = jnp.where(of == 0, x0, x1), jnp.where(of == 0, y0, y1)
                cb = lax.bitwise_xor(x_hi, lax.div(dx, 2)) * NY + lax.bitwise_xor(y, dy)
                rg = lax.rem(dx, 2) * 2 + of
                part = pl.ds(pl.multiple_of(rg * rows, 16), rows)
                act_ref[part, :] += jnp.dot(ref[at], w_ref[cb], preferred_element_type=F32)
    if last:
        hid = jnp.maximum(act_ref[...], F32(0.0)).astype(BF)
        half_rows = near_ref.shape[0]
        near_ref[...] = hid[:half_rows]
        far_ref[...] = hid[half_rows:]
        wide = hid.astype(F32)
        lane = lax.broadcasted_iota(jnp.int32, (hid.shape[0], 128), 1)
        total = jnp.zeros((hid.shape[0], 128), F32)
        for k in range(8):
            one = jnp.sum(wide * shown_ref[k].astype(F32), axis=1, keepdims=True)
            total = jnp.where(lane == k, one, total)
        group = hid.shape[0] // 16
        for rel in range(2):
            for slot in range(NZ):
                at = (rel * NZ + slot) * group
                flat_ref[pl.ds(group_row(rel, slot, group), group), :] = total[at : at + group]
        pick_ref[...] = jnp.transpose(flat_ref[...])[:8]


def run_act(qs, pieces, weight, start, shown=None):
    blocks, depth, h = weight.shape
    rows = 4 * pieces[0].shape[1]
    first, last = start.shape[0] == 1, shown is not None
    shapes = [jax.ShapeDtypeStruct((rows, h), F32)]
    if last:
        shapes += [jax.ShapeDtypeStruct((rows // 2, h), BF)] * 2
        shapes += [jax.ShapeDtypeStruct((8, rows), F32)]
    args = list(pieces) + [weight, start] + ([shown] if last else [])
    return pl.pallas_call(
        functools.partial(act_kernel, qs, first, last),
        in_specs=[VMEM] * len(args),
        out_specs=[VMEM] * len(shapes),
        out_shape=shapes,
        scratch_shapes=[pltpu.VMEM((rows, 128), F32)] if last else [],
        compiler_params=params(12),
        cost_estimate=pl.CostEstimate(
            flops=2 * rows * blocks * depth * h // 4 if last else 0,
            bytes_accessed=2**22 if last else 0,
            transcendentals=0,
        ),
        name="pre_act",
    )(*args)


def cut_kernel(s_ref, t_ref, after_ref, s_out, t_out, s_half, t_half):
    del after_ref
    half = s_half.shape[0]
    s_out[...] = s_ref[...]
    t_out[...] = t_ref[...]
    s_half[...] = s_ref[:half]
    t_half[...] = t_ref[half:]


def cut(s_in, t_in, after):
    half = (s_in.shape[0] // 2,) + s_in.shape[1:]
    return pl.pallas_call(
        cut_kernel,
        in_specs=[VMEM] * 2 + [ANYWHERE],
        out_specs=[VMEM] * 4,
        out_shape=[jax.ShapeDtypeStruct(v, BF) for v in (s_in.shape, t_in.shape, half, half)],
        compiler_params=params(4),
        cost_estimate=pl.CostEstimate(flops=0, bytes_accessed=2**20, transcendentals=0),
        name="cut_halves",
    )(s_in, t_in, after)


def turn_kernel(*refs):
    pieces, out_ref = refs[:8], refs[-1]
    core = lax.axis_index("c")
    rows, depth = pieces[0].shape[1:]

    def half_of(mine, core_of, dx, dy):
        p, q = (RING.index(dy), RING.index(dx)) if core_of == 0 else (RING.index(dx), RING.index(dy))
        return find(pieces[:4] if mine else pieces[4:], p, q)

    def run(own):
        for r in range(2):
            for dy in range(4):
                for low in range(2):
                    dx = 2 * r + low
                    (a, i), (b, j) = (half_of(of == own, of, dx, dy) for of in range(2))
                    both = jnp.concatenate([a[i], b[j]], 0)
                    out_ref[r * 4 + dy, :, pl.ds(low * 2 * rows, 2 * rows)] = jnp.transpose(both)

    @pl.when(core == 0)
    def _():
        run(0)

    @pl.when(core == 1)
    def _():
        run(1)


def turned(pieces, after):
    rows, depth = pieces[0].shape[1:]
    return pl.pallas_call(
        turn_kernel,
        in_specs=[VMEM] * 8 + [ANYWHERE],
        out_specs=VMEM,
        out_shape=jax.ShapeDtypeStruct((8, depth, 4 * rows), BF),
        compiler_params=params(8),
        cost_estimate=pl.CostEstimate(flops=0, bytes_accessed=24 * 2**20, transcendentals=0),
        name="turn_features",
    )(*pieces, after)


def grad_kernel(n_slots, feats_ref, sum_ref, fed_ref, boot_ref, shown_ref, act_ref, *refs):
    out_ref, bias_ref, flat_ref, slot_ref, pre_ref, stage, sems = refs
    x_hi, y = lax.axis_index("xh"), lax.axis_index("y")
    n_ctx = act_ref.shape[0]
    group = n_ctx // 16
    grad = boot_ref[...] * (jax.nn.sigmoid(sum_ref[...]) - fed_ref[...]) / F32(n_slots)
    grad = jnp.concatenate([grad, jnp.zeros((128 - n_slots, n_ctx), F32)], 0)
    flat_ref[...] = jnp.transpose(grad)
    for rel in range(2):
        for slot in range(NZ):
            slot_ref[pl.ds((rel * NZ + slot) * group, group), :] = flat_ref[
                pl.ds(group_row(rel, slot, group), group), :
            ]
    total = slot_ref[:, 0:1] * shown_ref[0].astype(F32)
    for k in range(1, n_slots):
        total += slot_ref[:, k : k + 1] * shown_ref[k].astype(F32)
    pre = jnp.where(act_ref[...] > 0, total, F32(0.0)).astype(BF)
    pre_ref[...] = pre
    bias_ref[...] = jnp.sum(pre.astype(F32), axis=0, keepdims=True)
    copies = []
    step = stage.shape[1] // 4
    for n in range(feats_ref.shape[0]):
        cb = lax.bitwise_xor(x_hi, n // 4) * NY + lax.bitwise_xor(y, n % 4)
        for i in range(4):
            part = pl.ds(i * step, step)
            stage[n, part, :] = jnp.dot(
                feats_ref[n, part, :], pre_ref[...], preferred_element_type=F32
            ).astype(BF)
            copy = pltpu.make_async_copy(
                stage.at[n, part, :], out_ref.at[cb, part, :], sems.at[n, i]
            )
            copy.start()
            copies.append(copy)
    for copy in copies:
        copy.wait()


def run_grad(feats, sums, fed, boot, shown, act):
    rows, h = act.shape
    blocks, depth, _ = feats.shape
    n_slots = shown.shape[0]
    return pl.pallas_call(
        functools.partial(grad_kernel, n_slots),
        in_specs=[VMEM] * 6,
        out_specs=[ANYWHERE, VMEM],
        out_shape=[
            jax.ShapeDtypeStruct((blocks, depth, h), BF),
            jax.ShapeDtypeStruct((1, h), F32),
        ],
        scratch_shapes=[
            pltpu.VMEM((rows, 128), F32),
            pltpu.VMEM((rows, 128), F32),
            pltpu.VMEM((rows, h), BF),
            pltpu.VMEM((blocks, depth, h), BF),
            pltpu.SemaphoreType.DMA((blocks, 4)),
        ],
        compiler_params=params(14),
        cost_estimate=pl.CostEstimate(flops=GRAD_COST, bytes_accessed=2**20, transcendentals=0),
        name="weight_grad",
    )(feats, sums, fed, boot, shown, act)


def share_kernel(near_ref, far_ref, arm_ref, armf_ref, sums_ref, own, up2, down2, up, down, up4, down4, sums_out):
    sums_out[...] = sums_ref[...]
    dims = (((1,), (1,)), ((), ()))
    arms = arm_ref.shape[0]
    group = near_ref.shape[0] // NZ
    step = 512
    half = arms // 2
    for j in range(0, arms, step):
        part = lax.dot_general(
            near_ref[...], arm_ref[pl.ds(j, step), :], dims, preferred_element_type=F32
        ) + lax.dot_general(
            far_ref[...], armf_ref[pl.ds(j, step), :], dims, preferred_element_type=F32
        )
        at = pl.ds(j, step)
        for s in range(NZ):
            piece = part[s * group : (s + 1) * group]
            d = SLOT_Z[s]
            if d in (0, 2, -2):
                {0: own, 2: up2, -2: down2}[d][:, at] = piece
            elif d == 4:
                (up4 if j < half else down4)[:, pl.ds(j % half, step)] = piece.astype(BF)
            else:
                (up if d > 0 else down)[abs(d) // 2, :, at] = piece.astype(BF)


def share_scores(near, far, arm, arm_far, sums):
    group, arms = near.shape[0] // NZ, arm.shape[0]
    whole = jax.ShapeDtypeStruct((group, arms), F32)
    pair = jax.ShapeDtypeStruct((2, group, arms), BF)
    half = jax.ShapeDtypeStruct((group, arms // 2), BF)
    shapes = [whole] * 3 + [pair] * 2 + [half] * 2 + [jax.ShapeDtypeStruct(sums.shape, F32)]
    return pl.pallas_call(
        share_kernel,
        in_specs=[VMEM] * 5,
        out_specs=[VMEM] * 8,
        out_shape=shapes,
        compiler_params=params(14),
        cost_estimate=pl.CostEstimate(
            flops=4 * near.shape[0] * near.shape[1] * arms, bytes_accessed=2**22, transcendentals=0
        ),
        name="share_scores",
    )(near, far, arm, arm_far, sums)


def join_kernel(*refs):
    ins, outs = refs[:6], refs[-2:]
    half = ins[2].shape[1]
    for i, out_ref in enumerate(outs):
        own_ref, near_ref, far_ref = ins[3 * i : 3 * i + 3]
        for at in range(0, 2 * half, half):
            part = pl.ds(at, half)
            total = own_ref[:, part] + near_ref[1, :, part].astype(F32)
            if at == i * half:
                total += far_ref[...].astype(F32)
            out_ref[:, part] = total.astype(BF)


def join(up, down, after):
    own = up[0]
    return pl.pallas_call(
        join_kernel,
        in_specs=[VMEM] * 6 + [ANYWHERE] * len(after),
        out_specs=[VMEM] * 2,
        out_shape=[jax.ShapeDtypeStruct(own.shape, BF)] * 2,
        compiler_params=params(4),
        cost_estimate=pl.CostEstimate(flops=JOIN_COST, bytes_accessed=2**20, transcendentals=0),
        name="join_shares",
    )(*up, *down, *after)


def final_kernel(own_ref, up_ref, down_ref, up2_ref, down2_ref, out_ref):
    total = own_ref[...] + up_ref[0].astype(F32) + down_ref[0].astype(F32)
    out_ref[...] = (total + up2_ref[...].astype(F32) + down2_ref[...].astype(F32)).astype(BF)


def final_sum(own, *parts):
    return pl.pallas_call(
        final_kernel,
        in_specs=[VMEM] * 5,
        out_specs=VMEM,
        out_shape=jax.ShapeDtypeStruct(own.shape, BF),
        compiler_params=params(4),
        cost_estimate=pl.CostEstimate(flops=FINAL_COST, bytes_accessed=2**20, transcendentals=0),
        name="sum_shares",
    )(own, *parts)


def z_shift(value, d):
    return route(value, lambda z, x, y, c: (z + d, x, y, c))


def per_device(
    contexts, trunk_weight, trunk_bias, head_weight, head_bias, arm_embed, slots, feedback, boot_weight
):
    cols = trunk_weight.shape[1]
    h = arm_embed.shape[1]
    z, c = lax.axis_index("z"), lax.axis_index("c")
    low = c == 0
    pick = lambda a, b: jnp.where(low, a, b)

    k = trunk_weight.shape[0]
    cols_for = lambda zz: lax.dynamic_slice_in_dim(contexts, ((zz + NZ) % NZ) * 2 * k, 2 * k, 1)
    side = jnp.where(low, 1, -1)
    ctx = [along_z(cols_for(z + side * i), i) for i in (1, 2, 3)]
    ctx_far = along_z(cols_for(z + 4), 4, core=1)
    ctx = [cols_for(z)] + ctx + [ctx_far]
    w_far = x_partner(trunk_weight)
    shown = gather_rows(slots, arm_embed)
    w_own, arm_copy = place(trunk_weight, w_far, arm_embed, ctx)
    arm_far = x_partner(arm_copy)
    w_other = other_core(w_own)
    p0, pair, p2 = trunk(ctx, w_own, w_other)

    pair = along_z(pair, -1)
    fourth = along_z(p0, -4 + 2, core=1)
    second = along_z(add_sums(p2, pair, fourth), -2)
    bias = jnp.concatenate([pick(trunk_bias, 0.0), pick(0.0, trunk_bias)])
    mine = pick(p0, 0.0) + pair[0] + second + bias
    feat = jnp.maximum(mine + other_core(mine), F32(0.0)).astype(BF)

    got = [along_z(feat, i) for i in (1, 2, 3)]
    far = along_z(got[2], 1, core=1)
    block = stack_rows(feat, far, got, arm_far)
    block = jnp.stack([block] + [first_ring(block, d) for d in RING[1:]])
    s_in, t_in = last_ring(block, 1), last_ring(block, 3)
    blocks = NX * NY // 2
    weight = head_weight[0].reshape(blocks, 2 * cols, h)
    block_other = other_core(block)
    (act,) = run_act((0,), [block, block_other], weight, head_bias)
    s_in, t_in, s_half, t_half = cut(s_in, t_in, shown)
    u_in = jnp.concatenate([last_ring(s_half, 3), last_ring(t_half, 1)], 0)
    own = [block, s_in, t_in, u_in]
    other = [block_other] + [other_core(v) for v in own[1:]]
    both = lambda i, j: own[i:j] + other[i:j]

    (act,) = run_act((1, 2), both(1, 3), weight, act)
    act, near, far, total = run_act((3,), both(3, 4), weight, act, shown)

    z_sum = lambda v, d: v + route(v, lambda z, x, y, c: (z ^ d, x, y, c))
    total = z_sum(total, 4)
    score, keep_up, keep_down, up, down, up4, down4, total = share_scores(
        near, x_partner(far), arm_embed, arm_far, total
    )
    up, down = z_shift(up, 1), z_shift(down, -1)
    up4, down4 = z_shift(up4, 2), z_shift(down4, -2)
    total = total + x_partner(total)
    feats = turned(own + other, score)
    total = z_sum(z_sum(total, 1), 2)
    up2, down2 = join((keep_up, up, up4), (keep_down, down, down4), [total, feats])
    scores = final_sum(score, up, down, z_shift(up2, 2), z_shift(down2, -2))

    weight_grad, bias_grad = run_grad(
        feats, total, feedback.T, boot_weight.astype(F32), shown, act
    )
    return (
        scores[None],
        weight_grad.reshape(1, -1, h),
        bias_grad,
    )


def solution(mesh):
    inner = Mesh(mesh.devices.reshape(NZ, 2, 2, NY, 2), AXES)
    batch, member = ("z", "xl"), ("xh", "y", "c")
    placed = (
        P(batch, None),
        P(batch, member),
        P(member),
        P(member, None, batch),
        P(member, batch),
        P(None, batch),
        P(),
        P(),
        P(member, None),
    )
    return jax.shard_map(
        per_device,
        mesh=inner,
        in_specs=placed,
        out_specs=(P(member, batch, None), P(member, None, batch), P(member, batch)),
        check_vma=False,
    )
```
